32 devices in a mesh: fsdp: 2 (over core), ctx: 4 (over y, x), tp: 4 (over z).
Axes of the slice: x: 2, y: 2, z: 4, core: 2. Of those that a mesh axis runs over, the one named last changes fastest.
Arguments:
- hidden_in: bfloat16 [2, 2048, 2304], P('fsdp', 'ctx'), may hold values from -6 to 6
- lengths: int32 [2], P('fsdp'), may hold values from 512 to 2048
- query_weight: bfloat16 [2304, 2048], P(('fsdp', 'ctx'), 'tp'), may hold values from -0.125 to 0.125
- key_weight: bfloat16 [2304, 1024], P(('fsdp', 'ctx'), 'tp'), may hold values from -0.125 to 0.125
- value_weight: bfloat16 [2304, 1024], P(('fsdp', 'ctx'), 'tp'), may hold values from -0.125 to 0.125
- w_out: bfloat16 [2048, 2304], P('tp', ('fsdp', 'ctx')), may hold values from -0.125 to 0.125
- w_gate: bfloat16 [2304, 9216], P(('fsdp', 'ctx'), 'tp'), may hold values from -0.125 to 0.125
- w_up: bfloat16 [2304, 9216], P(('fsdp', 'ctx'), 'tp'), may hold values from -0.125 to 0.125
- w_down: bfloat16 [9216, 2304], P('tp', ('fsdp', 'ctx')), may hold values from -0.0625 to 0.0625
- gain_attn_in: bfloat16 [2304], P(('fsdp', 'ctx')), may hold values from -0.5 to 0.5
- gain_attn_out: bfloat16 [2304], P(('fsdp', 'ctx')), may hold values from -0.5 to 0.5
- gain_ffn_in: bfloat16 [2304], P(('fsdp', 'ctx')), may hold values from -0.5 to 0.5
- gain_ffn_out: bfloat16 [2304], P(('fsdp', 'ctx')), may hold values from -0.5 to 0.5
- cotangent: bfloat16 [2, 2048, 2304], P('fsdp', 'ctx'), may hold values from -6 to 6
Outputs:
- output: bfloat16 [2, 2048, 2304], P('fsdp', 'ctx')
- grad_hidden_in: bfloat16 [2, 2048, 2304], P('fsdp', 'ctx')
- grad_w_query: float32 [2304, 2048], P(('fsdp', 'ctx'), 'tp')
- grad_w_key: float32 [2304, 1024], P(('fsdp', 'ctx'), 'tp')
- grad_w_value: float32 [2304, 1024], P(('fsdp', 'ctx'), 'tp')
- grad_w_out: float32 [2048, 2304], P('tp', ('fsdp', 'ctx'))
- grad_w_gate: float32 [2304, 9216], P(('fsdp', 'ctx'), 'tp')
- grad_w_up: float32 [2304, 9216], P(('fsdp', 'ctx'), 'tp')
- grad_w_down: float32 [9216, 2304], P('tp', ('fsdp', 'ctx'))
- grad_gain_attn_in: float32 [2304], P(('fsdp', 'ctx'))
- grad_gain_attn_out: float32 [2304], P(('fsdp', 'ctx'))
- grad_gain_ffn_in: float32 [2304], P(('fsdp', 'ctx'))
- grad_gain_ffn_out: float32 [2304], P(('fsdp', 'ctx'))
The draws below stay inside these ranges and needn't reach their ends.
All inputs are finite; a program needn't handle non-finite values.
Results may differ from the reference program's by a relative error of at most 0.024.
Values may be sent and summed in bfloat16 or wider, within the bound.
No kernel may reach another device: no remote copies, remote signals or barrier semaphores. Data moves between devices by JAX's collectives and lax.ppermute only.
A program may use at most 192 MiB of HBM per device.

```python
import jax
import jax.numpy as jnp
from jax import lax

MODEL_WIDTH = 2304
QUERY_HEADS = 8
KEY_VALUE_HEADS = 4
HEAD_SIZE = 256
FF = 9216
SEQUENCE_SLOTS = 2048
SEQS = 2


def block_scale(rng, dims, pieces, smallest, high):
    gain = 1.0
    for axis_at, blocks in pieces:
        heights = jax.random.uniform(jax.random.fold_in(jax.random.fold_in(rng, 6), axis_at), (blocks,), jnp.float32, smallest / len(pieces), high / len(pieces))
        gain = gain * jnp.repeat(jnp.exp(heights), dims[axis_at] // blocks).reshape((-1,) + (1,) * (len(dims) - 1 - axis_at))
    return gain


def gaussian(own_key, dims, width, bound, shards=(), kind=jnp.bfloat16):
    values = width * jax.random.normal(own_key, dims, jnp.float32)
    if shards:
        values = values * block_scale(own_key, dims, shards, -0.22, 0.18)
    return jnp.clip(values, -bound, bound).astype(kind)


def setup_inputs(seed: int = 0) -> dict:
    arg_keys = jax.random.split(jax.random.key(seed), 15)
    hidden_in = gaussian(arg_keys[0], (SEQS, SEQUENCE_SLOTS, MODEL_WIDTH), 1.0, 6.0, ((0, 2), (1, 4)))
    lengths = jax.random.randint(arg_keys[1], (SEQS,), SEQUENCE_SLOTS // 4, SEQUENCE_SLOTS + 1).astype(jnp.int32)
    query_weight = gaussian(arg_keys[2], (MODEL_WIDTH, QUERY_HEADS * HEAD_SIZE), MODEL_WIDTH ** -0.5, 0.125, ((0, 8), (1, 4)))
    key_weight = gaussian(arg_keys[3], (MODEL_WIDTH, KEY_VALUE_HEADS * HEAD_SIZE), MODEL_WIDTH ** -0.5, 0.125, ((0, 8), (1, 4)))
    value_weight = gaussian(arg_keys[4], (MODEL_WIDTH, KEY_VALUE_HEADS * HEAD_SIZE), MODEL_WIDTH ** -0.5, 0.125, ((0, 8), (1, 4)))
    w_out = gaussian(arg_keys[5], (QUERY_HEADS * HEAD_SIZE, MODEL_WIDTH), (QUERY_HEADS * HEAD_SIZE) ** -0.5, 0.125, ((0, 4), (1, 8)))
    w_gate = gaussian(arg_keys[6], (MODEL_WIDTH, FF), MODEL_WIDTH ** -0.5, 0.125, ((0, 8), (1, 4)))
    w_up = gaussian(arg_keys[7], (MODEL_WIDTH, FF), MODEL_WIDTH ** -0.5, 0.125, ((0, 8), (1, 4)))
    w_down = gaussian(arg_keys[8], (FF, MODEL_WIDTH), FF ** -0.5, 0.0625, ((0, 4), (1, 8)))
    gain_attn_in = jnp.clip(jax.random.uniform(arg_keys[9], (MODEL_WIDTH,), jnp.float32, -0.5, 0.5) * block_scale(arg_keys[9], (MODEL_WIDTH,), ((0, 8),), -0.4, 0.0), -0.5, 0.5).astype(jnp.bfloat16)
    gain_attn_out = jnp.clip(jax.random.uniform(arg_keys[10], (MODEL_WIDTH,), jnp.float32, -0.5, 0.5) * block_scale(arg_keys[10], (MODEL_WIDTH,), ((0, 8),), -0.4, 0.0), -0.5, 0.5).astype(jnp.bfloat16)
    gain_ffn_in = jnp.clip(jax.random.uniform(arg_keys[11], (MODEL_WIDTH,), jnp.float32, -0.5, 0.5) * block_scale(arg_keys[11], (MODEL_WIDTH,), ((0, 8),), -0.4, 0.0), -0.5, 0.5).astype(jnp.bfloat16)
    gain_ffn_out = jnp.clip(jax.random.uniform(arg_keys[12], (MODEL_WIDTH,), jnp.float32, -0.5, 0.5) * block_scale(arg_keys[12], (MODEL_WIDTH,), ((0, 8),), -0.4, 0.0), -0.5, 0.5).astype(jnp.bfloat16)
    cotangent = gaussian(arg_keys[13], (SEQS, SEQUENCE_SLOTS, MODEL_WIDTH), 1.0, 6.0, ((0, 2), (1, 4)))
    return {"hidden_in": hidden_in, "lengths": lengths, "query_weight": query_weight, "key_weight": key_weight, "value_weight": value_weight, "w_out": w_out, "w_gate": w_gate, "w_up": w_up, "w_down": w_down, "gain_attn_in": gain_attn_in, "gain_attn_out": gain_attn_out, "gain_ffn_in": gain_ffn_in, "gain_ffn_out": gain_ffn_out, "cotangent": cotangent}


@jax.custom_vjp
def reduced_precision(v):
    return lax.optimization_barrier(v.astype(jnp.bfloat16)).astype(jnp.float32)

@jax.custom_vjp
def reduced_backward(v):
    return v

def low_keep(v):
    return (reduced_precision(v), None)

def low_pass(kept, grad):
    return (grad,)

def back_keep(v):
    return (v, None)

def back_low(kept, grad):
    return (reduced_precision(grad),)
reduced_precision.defvjp(low_keep, low_pass)
reduced_backward.defvjp(back_keep, back_low)

def matrix_product(first, second):
    return jnp.dot(first, second, precision=lax.Precision.HIGHEST, preferred_element_type=jnp.float32)

def normalize(value_rows):
    return value_rows * lax.rsqrt(lax.optimization_barrier(jnp.mean(value_rows * value_rows, -1, keepdims=True)) + 1e-06)

def layer(inputs, length, query_weight, key_weight, value_weight, w_out, w_gate, w_up, w_down, gain_attn_in, gain_attn_out, gain_ffn_in, gain_ffn_out):
    head_groups = QUERY_HEADS // KEY_VALUE_HEADS
    block_rows = min(512, SEQUENCE_SLOTS)
    attention_input = reduced_precision(normalize(inputs) * (1.0 + gain_attn_in))
    query_matrix = reduced_precision(reduced_backward(matrix_product(attention_input, query_weight))).reshape(SEQUENCE_SLOTS, KEY_VALUE_HEADS, head_groups, HEAD_SIZE)
    key_rows = reduced_precision(reduced_backward(matrix_product(attention_input, key_weight))).reshape(SEQUENCE_SLOTS, KEY_VALUE_HEADS, HEAD_SIZE)
    value_rows = reduced_precision(reduced_backward(matrix_product(attention_input, value_weight))).reshape(SEQUENCE_SLOTS, KEY_VALUE_HEADS, HEAD_SIZE)
    key_pos = jnp.arange(SEQUENCE_SLOTS, dtype=jnp.int32)

    def attend(start):
        query_block = lax.dynamic_slice_in_dim(query_matrix, start, block_rows, 0)
        raw = reduced_backward(jnp.einsum('tkgd,ukd->kgtu', query_block, key_rows, precision=lax.Precision.HIGHEST) * 0.0625)
        bent = jnp.tanh(raw / 50.0)
        query_pos = start + jnp.arange(block_rows, dtype=jnp.int32)
        allowed = (key_pos[None, :] <= query_pos[:, None]) & (key_pos[None, :] < length)
        masked = jnp.where(allowed, 50.0 * bent, -1e+30)
        largest = lax.optimization_barrier(jnp.max(masked, -1, keepdims=True))
        logsum = largest + jnp.log(lax.optimization_barrier(jnp.sum(jnp.exp(masked - largest), -1, keepdims=True)))
        probs = jnp.exp(masked - logsum)
        return jnp.einsum('kgtu,ukd->tkgd', reduced_precision(probs), value_rows, precision=lax.Precision.HIGHEST)
    starts = jnp.arange(SEQUENCE_SLOTS // block_rows, dtype=jnp.int32) * block_rows
    blocks = lax.map(jax.checkpoint(attend), starts)
    attended = reduced_precision(reduced_backward(blocks.reshape(SEQUENCE_SLOTS, QUERY_HEADS * HEAD_SIZE)))
    attn = reduced_backward(matrix_product(attended, w_out))
    after_attn = inputs + normalize(attn) * (1.0 + gain_attn_out)
    ffn_in = reduced_precision(normalize(after_attn) * (1.0 + gain_ffn_in))
    gate = reduced_backward(matrix_product(ffn_in, w_gate))
    upward = reduced_backward(matrix_product(ffn_in, w_up))
    hidden = reduced_precision(jax.nn.gelu(gate, approximate=True) * upward)
    ffn_out = reduced_backward(matrix_product(hidden, w_down))
    return after_attn + normalize(ffn_out) * (1.0 + gain_ffn_out)

def reference(hidden_in, lengths, query_weight, key_weight, value_weight, w_out, w_gate, w_up, w_down, gain_attn_in, gain_attn_out, gain_ffn_in, gain_ffn_out, cotangent):
    weights = tuple((item.astype(jnp.float32) for item in (query_weight, key_weight, value_weight, w_out, w_gate, w_up, w_down, gain_attn_in, gain_attn_out, gain_ffn_in, gain_ffn_out)))
    positions = jnp.arange(SEQUENCE_SLOTS, dtype=jnp.int32)

    def step(totals, items):
        inputs, length, cot = items

        def forward(x_in, *params):
            return layer(x_in, length, *params)
        result, pullback = jax.vjp(forward, inputs.astype(jnp.float32), *weights)
        keep = (positions < length).astype(jnp.float32)[:, None]
        grads = pullback(cot.astype(jnp.float32) * keep)
        totals = tuple((total + grad for total, grad in zip(totals, grads[1:])))
        return (totals, (result.astype(jnp.bfloat16), grads[0].astype(jnp.bfloat16)))
    zeros = tuple((jnp.zeros(item.shape, jnp.float32) for item in weights))
    totals, (outputs, input_grads) = lax.scan(step, zeros, (hidden_in, lengths, cotangent))
    return (outputs, input_grads, totals[0], totals[1], totals[2], totals[3], totals[4], totals[5], totals[6], totals[7], totals[8], totals[9], totals[10])
```

```python
import jax
import jax.numpy as jnp
from jax import lax
from jax.sharding import PartitionSpec as P

QUERY_HEADS = 8
KEY_VALUE_HEADS = 4
HEAD_SIZE = 256
SEQUENCE_SLOTS = 2048


EPS = 1e-06
CAP = 50.0
QSCALE = 0.0625
NEG = -1e30
BF = jnp.bfloat16
F32 = jnp.float32

X_PAIRS = [(0, 1), (1, 0), (2, 3), (3, 2)]
Y_PAIRS = [(0, 2), (2, 0), (1, 3), (3, 1)]
D_PAIRS = [(0, 3), (3, 0), (1, 2), (2, 1)]


def normalize(value_rows):
    factor = lax.rsqrt(jnp.mean(value_rows * value_rows, -1, keepdims=True) + EPS)
    return (value_rows * factor, factor)


def norm_back(grad_hat, normed, factor):
    return factor * (grad_hat - normed * jnp.mean(grad_hat * normed, -1, keepdims=True))


def plain_dot(first, second):
    return jnp.dot(first, second, preferred_element_type=F32)


def left_dot(first, second):
    return lax.dot_general(first, second, (((0,), (0,)), ((), ())), preferred_element_type=F32)


def right_dot(first, second):
    return lax.dot_general(first, second, (((1,), (1,)), ((), ())), preferred_element_type=F32)


def gelu_tanh(value_rows):
    return jax.nn.gelu(value_rows, approximate=True)


def over_x(value):
    return lax.ppermute(value, "ctx", X_PAIRS)


def over_y(value):
    return lax.ppermute(value, "ctx", Y_PAIRS)


def over_diagonal(value):
    return lax.ppermute(value, "ctx", D_PAIRS)


def to_other_core(value):
    return lax.ppermute(value, "fsdp", [(0, 1), (1, 0)])


def square_plane():
    return lax.axis_size("ctx") == 4


def place(pieces, at):
    rows = pieces[0].shape[0]
    whole = jnp.zeros((rows * len(pieces),) + pieces[0].shape[1:], pieces[0].dtype)
    for piece, index in zip(pieces, at):
        whole = lax.dynamic_update_slice_in_dim(whole, piece, index * rows, 0)
    return whole


def gather_ctx(shard):
    if not square_plane():
        return lax.all_gather(shard, "ctx", axis=0, tiled=True)
    me = lax.axis_index("ctx")
    half = shard.shape[0] // 2
    from_x, from_y = over_x(shard), over_y(shard)
    diag = jnp.concatenate([over_y(from_x[:half]), over_x(from_y[half:])], 0)
    return place([shard, from_x, from_y, diag], [me, me ^ 1, me ^ 2, me ^ 3])


def gather_ctx_direct(shard):
    if not square_plane():
        return lax.all_gather(shard, "ctx", axis=0, tiled=True)
    me = lax.axis_index("ctx")
    return place(
        [shard, over_x(shard), over_y(shard), over_diagonal(shard)],
        [me, me ^ 1, me ^ 2, me ^ 3],
    )


def block_of(whole, index, count):
    rows = whole.shape[0] // count
    return lax.dynamic_slice_in_dim(whole, index * rows, rows, 0)


def scatter_ctx(whole):
    if not square_plane():
        return lax.psum_scatter(whole, "ctx", scatter_dimension=0, tiled=True).astype(F32)
    me = lax.axis_index("ctx")
    own, to_x, to_y, to_d = (block_of(whole, me ^ k, 4) for k in range(4))
    half = own.shape[0] // 2
    d_x, d_y = over_x(to_d[:half]), over_y(to_d[half:])
    x_top, y_low = over_x(to_x[:half]), over_y(to_y[half:])
    y_top = over_y((to_y[:half].astype(F32) + d_x.astype(F32)).astype(BF))
    x_low = over_x((to_x[half:].astype(F32) + d_y.astype(F32)).astype(BF))
    top = own[:half].astype(F32) + x_top.astype(F32) + y_top.astype(F32)
    low = own[half:].astype(F32) + x_low.astype(F32) + y_low.astype(F32)
    return jnp.concatenate([top, low], 0)


def scatter_ctx_direct(whole):
    if not square_plane():
        return lax.psum_scatter(whole, "ctx", scatter_dimension=0, tiled=True).astype(F32)
    me = lax.axis_index("ctx")
    own, to_x, to_y, to_d = (block_of(whole, me ^ k, 4) for k in range(4))
    return (
        own.astype(F32)
        + over_x(to_x).astype(F32)
        + over_y(to_y).astype(F32)
        + over_diagonal(to_d).astype(F32)
    )


def body(
    hidden_in,
    lengths,
    query_weight,
    key_weight,
    value_weight,
    w_out,
    w_gate,
    w_up,
    w_down,
    gain_attn_in,
    gain_attn_out,
    gain_ffn_in,
    gain_ffn_out,
    cotangent,
):
    seqs_here, tok_here, width = hidden_in.shape
    row_count = seqs_here * tok_here
    head_groups = QUERY_HEADS // KEY_VALUE_HEADS
    core = lax.axis_index("fsdp")
    half_width = width // 2
    q_cols, kv_cols = query_weight.shape[1], key_weight.shape[1]
    kv_local = kv_cols // HEAD_SIZE

    def near(value):
        return lax.dynamic_slice_in_dim(value, core * half_width, half_width, 1)

    def far(value):
        return lax.dynamic_slice_in_dim(value, (1 - core) * half_width, half_width, 1)

    def gather(shard):
        mine = gather_ctx(shard)
        return mine, to_other_core(mine)

    def times(value, weight):
        return plain_dot(near(value), weight[0]) + plain_dot(far(value), weight[1])

    def join(own, other):
        return jnp.where(
            core == 0, jnp.concatenate([own, other], 1), jnp.concatenate([other, own], 1)
        )

    gains = jnp.stack([gain_attn_in, gain_attn_out, gain_ffn_in, gain_ffn_out])[None]
    gains = gather_ctx_direct(gains)
    gains = place([gains, to_other_core(gains)], [core, 1 - core])
    gains = gains.transpose(1, 0, 2).reshape(4, width).astype(F32)
    scale_one, scale_two, scale_three, scale_four = (1.0 + gains[i][None] for i in range(4))
    qkv_w = gather(jnp.concatenate([query_weight, key_weight, value_weight], 1))
    out_w = gather(w_out.T)
    gate_w = gather(w_gate)
    up_w = gather(w_up)
    down_w = gather(w_down.T)

    own_start = lax.axis_index("ctx") * tok_here
    query_pos = own_start + jnp.arange(tok_here, dtype=jnp.int32)
    key_pos = jnp.arange(SEQUENCE_SLOTS, dtype=jnp.int32)
    valid = query_pos[None, :] < lengths[:, None]
    allowed = (
        (key_pos[None, None, :] <= query_pos[None, :, None])
        & (key_pos[None, None, :] < lengths[:, None, None])
    )[:, None, None]
    flat_in = hidden_in.astype(F32).reshape(row_count, width)
    normed_one, factor_one = normalize(flat_in)
    attention_input = (normed_one * scale_one).astype(BF)
    qkv = times(attention_input, qkv_w).astype(BF)
    query_b = qkv[:, :q_cols]
    kv = qkv[:, q_cols:].reshape(seqs_here, tok_here, 2 * kv_cols).transpose(1, 0, 2)
    kv_all = gather_ctx_direct(kv).transpose(1, 0, 2)
    query_five = query_b.reshape(seqs_here, tok_here, kv_local, head_groups, HEAD_SIZE)
    key_four = kv_all[:, :, :kv_cols].reshape(seqs_here, SEQUENCE_SLOTS, kv_local, HEAD_SIZE)
    value_four = kv_all[:, :, kv_cols:].reshape(seqs_here, SEQUENCE_SLOTS, kv_local, HEAD_SIZE)
    raw = jnp.einsum("stkgd,sukd->skgtu", query_five, key_four, preferred_element_type=F32) * QSCALE
    bent = jnp.tanh(raw / CAP)
    masked = jnp.where(allowed, CAP * bent, NEG)
    largest = jnp.max(masked, -1, keepdims=True)
    logsum = largest + jnp.log(jnp.sum(jnp.exp(masked - largest), -1, keepdims=True))
    probs = jnp.exp(masked - logsum)
    probs_b = probs.astype(BF)
    attended = (
        jnp.einsum("skgtu,sukd->stkgd", probs_b, value_four, preferred_element_type=F32)
        .astype(BF)
        .reshape(row_count, -1)
    )
    attn = join(right_dot(attended, out_w[0]).astype(BF), right_dot(attended, out_w[1]).astype(BF))
    attn = lax.psum(attn, "tp").astype(F32)
    normed_two, factor_two = normalize(attn)
    after_attn = flat_in + normed_two * scale_two
    normed_three, factor_three = normalize(after_attn)
    ffn_in = (normed_three * scale_three).astype(BF)
    gate = times(ffn_in, gate_w)
    upward = times(ffn_in, up_w)
    activated, gelu_pull = jax.vjp(gelu_tanh, gate)
    hidden_b = (activated * upward).astype(BF)
    ffn_out = join(right_dot(hidden_b, down_w[0]).astype(BF), right_dot(hidden_b, down_w[1]).astype(BF))
    ffn_out = lax.psum(ffn_out, "tp").astype(F32)
    normed_four, factor_four = normalize(ffn_out)
    result = after_attn + normed_four * scale_four
    cot = cotangent.astype(F32).reshape(row_count, width) * valid.reshape(row_count, 1).astype(F32)

    def weight_grad(rows_from, cols_from):
        lhs = jnp.concatenate([near(rows_from), to_other_core(far(rows_from))], 0)
        rhs = jnp.concatenate([cols_from, to_other_core(cols_from)], 0)
        return scatter_ctx(left_dot(lhs, rhs).astype(BF))

    grad_gain_four = jnp.sum(cot * normed_four, 0)
    dffn_b = norm_back(cot * scale_four, normed_four, factor_four).astype(BF)
    grad_down = weight_grad(dffn_b, hidden_b).T
    dhidden = plain_dot(near(dffn_b), down_w[0]) + plain_dot(far(dffn_b), down_w[1])
    dgate_b = gelu_pull(dhidden * upward)[0].astype(BF)
    dup_b = (dhidden * activated).astype(BF)
    grad_gate = weight_grad(ffn_in, dgate_b)
    grad_up = weight_grad(ffn_in, dup_b)
    dffn_in = join(
        *(
            (right_dot(dgate_b, gate_w[i]) + right_dot(dup_b, up_w[i])).astype(BF)
            for i in range(2)
        )
    )
    dffn_in = lax.psum(dffn_in, "tp").astype(F32)
    grad_gain_three = jnp.sum(dffn_in * normed_three, 0)
    dafter = cot + norm_back(dffn_in * scale_three, normed_three, factor_three)
    grad_gain_two = jnp.sum(dafter * normed_two, 0)
    dattn_b = norm_back(dafter * scale_two, normed_two, factor_two).astype(BF)
    grad_out = weight_grad(dattn_b, attended).T
    dattended = (
        plain_dot(near(dattn_b), out_w[0]) + plain_dot(far(dattn_b), out_w[1])
    ).astype(BF).reshape(query_five.shape)
    dprobs = jnp.einsum("stkgd,sukd->skgtu", dattended, value_four, preferred_element_type=F32)
    weighted = jnp.sum(probs * dprobs, -1, keepdims=True)
    draw_b = (probs * (dprobs - weighted) * (1.0 - bent * bent)).astype(BF)
    dquery_b = (
        (jnp.einsum("skgtu,sukd->stkgd", draw_b, key_four, preferred_element_type=F32) * QSCALE)
        .astype(BF)
        .reshape(row_count, -1)
    )
    dvalue_part = jnp.einsum("skgtu,stkgd->sukd", probs_b, dattended, preferred_element_type=F32)
    dkey_part = (
        jnp.einsum("skgtu,stkgd->sukd", draw_b, query_five, preferred_element_type=F32) * QSCALE
    )
    dkv_part = jnp.concatenate(
        [
            dkey_part.astype(BF).reshape(seqs_here, SEQUENCE_SLOTS, kv_cols),
            dvalue_part.astype(BF).reshape(seqs_here, SEQUENCE_SLOTS, kv_cols),
        ],
        2,
    ).transpose(1, 0, 2)
    dkv_b = scatter_ctx_direct(dkv_part).astype(BF).transpose(1, 0, 2).reshape(row_count, -1)
    dqkv_b = jnp.concatenate([dquery_b, dkv_b], 1)
    dattn_in = join(*(right_dot(dqkv_b, qkv_w[i]).astype(BF) for i in range(2)))
    dattn_in = lax.psum(dattn_in, "tp").astype(F32)
    grad_qkv = weight_grad(attention_input, dqkv_b)
    grad_gain_one = jnp.sum(dattn_in * normed_one, 0)
    grad_input = dafter + norm_back(dattn_in * scale_one, normed_one, factor_one)
    grad_gains = jnp.stack([grad_gain_one, grad_gain_two, grad_gain_three, grad_gain_four])
    grad_gains = grad_gains.reshape(4, 2, half_width).transpose(1, 0, 2)
    grad_gains = block_of(grad_gains, core, 2) + to_other_core(block_of(grad_gains, 1 - core, 2))
    grad_gains = grad_gains.reshape(4, lax.axis_size("ctx"), -1).transpose(1, 0, 2)
    grad_gains = scatter_ctx_direct(grad_gains).reshape(4, -1)
    return (
        result.astype(BF).reshape(hidden_in.shape),
        grad_input.astype(BF).reshape(hidden_in.shape),
        grad_qkv[:, :q_cols],
        grad_qkv[:, q_cols : q_cols + kv_cols],
        grad_qkv[:, q_cols + kv_cols :],
        grad_out,
        grad_gate,
        grad_up,
        grad_down,
        grad_gains[0],
        grad_gains[1],
        grad_gains[2],
        grad_gains[3],
    )


def solution(mesh):
    return jax.shard_map(
        body,
        mesh=mesh,
        in_specs=(
            P("fsdp", "ctx", None),
            P("fsdp"),
            P(("fsdp", "ctx"), "tp"),
            P(("fsdp", "ctx"), "tp"),
            P(("fsdp", "ctx"), "tp"),
            P("tp", ("fsdp", "ctx")),
            P(("fsdp", "ctx"), "tp"),
            P(("fsdp", "ctx"), "tp"),
            P("tp", ("fsdp", "ctx")),
            P(("fsdp", "ctx")),
            P(("fsdp", "ctx")),
            P(("fsdp", "ctx")),
            P(("fsdp", "ctx")),
            P("fsdp", "ctx", None),
        ),
        out_specs=(
            P("fsdp", "ctx", None),
            P("fsdp", "ctx", None),
            P(("fsdp", "ctx"), "tp"),
            P(("fsdp", "ctx"), "tp"),
            P(("fsdp", "ctx"), "tp"),
            P("tp", ("fsdp", "ctx")),
            P(("fsdp", "ctx"), "tp"),
            P(("fsdp", "ctx"), "tp"),
            P("tp", ("fsdp", "ctx")),
            P(("fsdp", "ctx")),
            P(("fsdp", "ctx")),
            P(("fsdp", "ctx")),
            P(("fsdp", "ctx")),
        ),
        check_vma=False,
    )
```

```python
import jax
import jax.numpy as jnp
from jax import lax
from jax.sharding import PartitionSpec as P

QUERY_HEADS = 8
KEY_VALUE_HEADS = 4
HEAD_SIZE = 256
SEQUENCE_SLOTS = 2048


EPS = 1e-06
CAP = 50.0
QSCALE = 0.0625
NEG = -1e30


def normalize(value_rows):
    factor = lax.rsqrt(jnp.mean(value_rows * value_rows, -1, keepdims=True) + EPS)
    return (value_rows * factor, factor)


def norm_back(grad_hat, normed, factor):
    return factor * (grad_hat - normed * jnp.mean(grad_hat * normed, -1, keepdims=True))


def plain_dot(first, second):
    return jnp.dot(first, second, preferred_element_type=jnp.float32)


def left_dot(first, second):
    return lax.dot_general(
        first, second, (((0,), (0,)), ((), ())), preferred_element_type=jnp.float32
    )


def right_dot(first, second):
    return lax.dot_general(
        first, second, (((1,), (1,)), ((), ())), preferred_element_type=jnp.float32
    )


def gelu_tanh(value_rows):
    return jax.nn.gelu(value_rows, approximate=True)


BF = jnp.bfloat16
F32 = jnp.float32

LINKS = {
    "x": ("ctx", [(0, 1), (1, 0), (2, 3), (3, 2)]),
    "y": ("ctx", [(0, 2), (2, 0), (1, 3), (3, 1)]),
    "diagonal": ("ctx", [(0, 3), (3, 0), (1, 2), (2, 1)]),
    "core": ("fsdp", [(0, 1), (1, 0)]),
}
ORDER = [(0, 0), (0, 1), (1, 1), (2, 0), (1, 0), (3, 0), (3, 1), (2, 1)]


def tied(*values):
    return lax.optimization_barrier(values)


def send(link, value):
    return lax.ppermute(value, *LINKS[link])


def around(value, by=1):
    size = lax.axis_size("tp")
    return lax.ppermute(value, "tp", [(i, (i + by) % size) for i in range(size)])


def halves(block):
    half = block.shape[0] // 2
    return block[:half], block[half:]


class Scatter:
    def __init__(self, partial):
        block = partial.shape[0] // 4
        self.half = block // 2
        self.kept = partial[: 2 * block]
        self.first = (send("x", partial[2 * block : 3 * block]), send("y", partial[3 * block :]))

    def second(self):
        half, (from_x, from_y) = self.half, self.first
        x_low, y_top = self.kept[2 * half : 3 * half], self.kept[3 * half :]
        self.last = (
            send("y", (y_top.astype(F32) + from_x[half:].astype(F32)).astype(BF)),
            send("x", (x_low.astype(F32) + from_y[:half].astype(F32)).astype(BF)),
        )

    def result(self):
        half, (from_x, from_y), (y_top, x_low) = self.half, self.first, self.last
        kept = self.kept
        top = kept[:half].astype(F32) + from_x[:half].astype(F32) + y_top.astype(F32)
        low = kept[half : 2 * half].astype(F32) + from_y[half:].astype(F32) + x_low.astype(F32)
        return jnp.concatenate([top, low], 0)


class Ring:
    def __init__(self, value):
        self.value, self.step = value, 0
        self.size, self.me = lax.axis_size("tp"), lax.axis_index("tp")
        self.rows = value.shape[0] // self.size
        self.whole = jnp.zeros_like(value)
        self.going = around(self.block(self.me - 1))

    def block(self, index):
        start = (index + self.size) % self.size * self.rows
        return lax.dynamic_slice_in_dim(self.value, start, self.rows, 0)

    def put(self):
        index = (self.me - (self.step - self.size + 1) + self.size) % self.size
        self.whole = lax.dynamic_update_slice_in_dim(self.whole, self.going, index * self.rows, 0)

    def go(self):
        if self.step < self.size - 1:
            own = self.block(self.me - 2 - self.step)
            self.going = (self.going.astype(F32) + own.astype(F32)).astype(BF)
        self.step += 1
        if self.step >= self.size - 1:
            self.put()
        if self.step < 2 * self.size - 2:
            self.going = around(self.going)

    def finish(self):
        while self.step < 2 * self.size - 2:
            self.go()
        return self.whole


def column_order(width):
    core, me = lax.axis_index("fsdp"), lax.axis_index("ctx")
    half_width, half = width // 2, width // 16
    run = jnp.arange(half, dtype=jnp.int32)
    place = jnp.concatenate([(me ^ k) * (2 * half) + low * half + run for k, low in ORDER])
    place = jnp.concatenate([core * half_width + place, (1 - core) * half_width + place])
    return (jnp.arange(width, dtype=jnp.int32)[:, None] == place[None, :]).astype(BF)


def plane_body(
    hidden_in,
    lengths,
    query_weight,
    key_weight,
    value_weight,
    w_out,
    w_gate,
    w_up,
    w_down,
    gain_attn_in,
    gain_attn_out,
    gain_ffn_in,
    gain_ffn_out,
    cotangent,
):
    seqs_here, tok_here, width = hidden_in.shape
    row_count = seqs_here * tok_here
    head_groups = QUERY_HEADS // KEY_VALUE_HEADS
    half_width = width // 2
    q_cols, kv_cols = query_weight.shape[1], key_weight.shape[1]
    kv_local = kv_cols // HEAD_SIZE
    planes, me = lax.axis_size("ctx"), lax.axis_index("ctx")

    def both_cores(mine):
        return jnp.concatenate([mine, send("core", mine)], 0)

    def gather(shard, axis):
        return lax.all_gather(shard, ("fsdp", "ctx"), axis=axis, tiled=True)

    attention_shards = jnp.concatenate([query_weight, key_weight, value_weight, w_out.T], 1)
    attention_w = gather(attention_shards, 0)
    gains = jnp.stack([gain_attn_in, gain_attn_out, gain_ffn_in, gain_ffn_out])[None]
    gains = jnp.broadcast_to(gains, (2 * planes,) + gains.shape[1:])
    gains = lax.all_to_all(gains, ("fsdp", "ctx"), 0, 0, tiled=True)
    gains = gains.transpose(1, 0, 2).reshape(4, width).astype(F32)
    scale_one, scale_two, scale_three, scale_four = (1.0 + gains[i][None] for i in range(4))
    flat_in = hidden_in.astype(F32).reshape(row_count, width)
    normed_one, factor_one = normalize(flat_in)
    attention_input = (normed_one * scale_one).astype(BF)
    to_blocks = column_order(width)

    attention_w, attention_input, gate_t = tied(attention_w, attention_input, w_gate)
    gate_w = gather(gate_t, 0)
    qkv_cols = q_cols + 2 * kv_cols
    qkv_w, out_w = attention_w[:, :qkv_cols], attention_w[:, qkv_cols:]
    run = jnp.arange(tok_here, dtype=jnp.int32)
    query_pos = me * tok_here + run
    key_pos = jnp.arange(planes * tok_here, dtype=jnp.int32)
    valid = query_pos[None, :] < lengths[:, None]
    allowed = (
        (key_pos[None, None, :] <= query_pos[None, :, None])
        & (key_pos[None, None, :] < lengths[:, None, None])
    )[:, None, None]
    qkv = plain_dot(attention_input, qkv_w).astype(BF)
    query_b = qkv[:, :q_cols]
    kv = qkv[:, q_cols:].reshape(1, seqs_here, tok_here, 2 * kv_cols)
    kv = lax.all_to_all(jnp.broadcast_to(kv, (planes,) + kv.shape[1:]), "ctx", 0, 0, tiled=True)

    kv_all = kv.transpose(1, 0, 2, 3).reshape(seqs_here, SEQUENCE_SLOTS, 2 * kv_cols)
    query_five = query_b.reshape(seqs_here, tok_here, kv_local, head_groups, HEAD_SIZE)
    key_four = kv_all[:, :, :kv_cols].reshape(seqs_here, SEQUENCE_SLOTS, kv_local, HEAD_SIZE)
    value_four = kv_all[:, :, kv_cols:].reshape(seqs_here, SEQUENCE_SLOTS, kv_local, HEAD_SIZE)
    raw = jnp.einsum("stkgd,sukd->skgtu", query_five, key_four, preferred_element_type=F32) * QSCALE
    bent = jnp.tanh(raw / CAP)
    masked = jnp.where(allowed, CAP * bent, NEG)
    largest = jnp.max(masked, -1, keepdims=True)
    logsum = largest + jnp.log(jnp.sum(jnp.exp(masked - largest), -1, keepdims=True))
    probs = jnp.exp(masked - logsum)
    probs_b = probs.astype(BF)
    attended = (
        jnp.einsum("skgtu,sukd->stkgd", probs_b, value_four, preferred_element_type=F32)
        .astype(BF)
        .reshape(row_count, -1)
    )
    attn = right_dot(attended, out_w).astype(BF)
    ring = Ring(attn)

    ring.going, gate_w, up_t = tied(ring.going, gate_w, w_up)
    up_w = gather(up_t, 0)
    ring.go()
    ring.go()
    ring.go()
    ring.go()
    ring.going, up_w, down_t = tied(ring.going, up_w, w_down)
    down_w = gather(down_t, 1)
    attn = ring.finish().astype(F32)
    normed_two, factor_two = normalize(attn)
    after_attn = flat_in + normed_two * scale_two
    normed_three, factor_three = normalize(after_attn)
    ffn_in = (normed_three * scale_three).astype(BF)
    gate = plain_dot(ffn_in, gate_w)
    upward = plain_dot(ffn_in, up_w)
    activated, gelu_pull = jax.vjp(gelu_tanh, gate)
    hidden_b = (activated * upward).astype(BF)
    hidden_b, down_w = tied(hidden_b, down_w)
    ffn_out = lax.psum(plain_dot(hidden_b, down_w).astype(BF), "tp")
    cot = cotangent.astype(F32).reshape(row_count, width) * valid.reshape(row_count, 1).astype(F32)

    def near_far(rows_from):
        blocks = plain_dot(rows_from, to_blocks).astype(BF)
        return jnp.concatenate([blocks[:, :half_width], send("core", blocks[:, half_width:])], 0)

    def weight_grad(rows_both, cols_both):
        return left_dot(rows_both, cols_both).astype(BF)

    hidden_both, attended_both = both_cores(hidden_b), both_cores(attended)
    ffn_in_both, attention_input_both = near_far(ffn_in), near_far(attention_input)
    ffn_out, hidden_both, attended_both, ffn_in_both, attention_input_both = tied(
        ffn_out, hidden_both, attended_both, ffn_in_both, attention_input_both
    )
    ffn_out = ffn_out.astype(F32)
    normed_four, factor_four = normalize(ffn_out)
    result = after_attn + normed_four * scale_four
    grad_gain_four = jnp.sum(cot * normed_four, 0)
    dffn_b = norm_back(cot * scale_four, normed_four, factor_four).astype(BF)
    dhidden = right_dot(dffn_b, down_w)
    dgate_b = gelu_pull(dhidden * upward)[0].astype(BF)
    dup_b = (dhidden * activated).astype(BF)
    dffn_in = (right_dot(dgate_b, gate_w) + right_dot(dup_b, up_w)).astype(BF)
    dffn_in, dgate_b, dup_b, dffn_b = tied(dffn_in, dgate_b, dup_b, dffn_b)

    ring = Ring(dffn_in)
    down_part = weight_grad(near_far(dffn_b), hidden_both)
    ring.going, down_part, dgate_b = tied(ring.going, down_part, dgate_b)
    ring.go()
    down_s = Scatter(down_part)
    gate_part = weight_grad(ffn_in_both, both_cores(dgate_b))
    ring.going, gate_part = tied(ring.going, gate_part)
    ring.go()
    dup_both = both_cores(dup_b)
    ring.going, down_s.first, dup_both = tied(ring.going, down_s.first, dup_both)
    ring.go()
    down_s.second()
    gate_s = Scatter(gate_part)
    output = result.astype(BF)
    ring.going, output = tied(ring.going, output)
    ring.go()
    ring.going, down_s.last = tied(ring.going, down_s.last)
    ring.go()
    grad_down = down_s.result().T
    ring.going, gate_s.first, grad_down = tied(ring.going, gate_s.first, grad_down)
    gate_s.second()
    dffn_in = ring.finish()
    dffn_in = dffn_in.astype(F32)
    grad_gain_three = jnp.sum(dffn_in * normed_three, 0)
    dafter = cot + norm_back(dffn_in * scale_three, normed_three, factor_three)
    grad_gain_two = jnp.sum(dafter * normed_two, 0)
    dattn_b = norm_back(dafter * scale_two, normed_two, factor_two).astype(BF)
    dattended = plain_dot(dattn_b, out_w).astype(BF).reshape(query_five.shape)
    dprobs = jnp.einsum("stkgd,sukd->skgtu", dattended, value_four, preferred_element_type=F32)
    weighted = jnp.sum(probs * dprobs, -1, keepdims=True)
    draw_b = (probs * (dprobs - weighted) * (1.0 - bent * bent)).astype(BF)
    dvalue_part = jnp.einsum("skgtu,stkgd->sukd", probs_b, dattended, preferred_element_type=F32)
    dkey_part = (
        jnp.einsum("skgtu,stkgd->sukd", draw_b, query_five, preferred_element_type=F32) * QSCALE
    )
    dkv = jnp.concatenate(
        [
            part.astype(BF).reshape(seqs_here, planes, tok_here, kv_cols)
            for part in (dkey_part, dvalue_part)
        ],
        3,
    ).transpose(1, 0, 2, 3)
    dkv, dattn_b, dup_both, gate_s.last = tied(dkv, dattn_b, dup_both, gate_s.last)
    dkv = lax.all_to_all(dkv, "ctx", 0, 0, tiled=True)
    up_part = weight_grad(ffn_in_both, dup_both)
    out_part = weight_grad(near_far(dattn_b), attended_both)
    dquery_b = (
        (jnp.einsum("skgtu,sukd->stkgd", draw_b, key_four, preferred_element_type=F32) * QSCALE)
        .astype(BF)
        .reshape(row_count, -1)
    )
    grad_gate = gate_s.result()
    dkv, dquery_b, up_part, out_part, grad_gate = tied(dkv, dquery_b, up_part, out_part, grad_gate)
    up_s = Scatter(up_part)
    dkv_b = jnp.sum(dkv.astype(F32), 0).astype(BF).reshape(row_count, -1)
    dqkv_b = jnp.concatenate([dquery_b, dkv_b], 1)
    dattn_in = right_dot(dqkv_b, qkv_w)
    dattn_in, dqkv_b, dafter = tied(dattn_in.astype(BF), dqkv_b, dafter)

    ring = Ring(dattn_in)
    grad_gain_one = jnp.sum(dattn_in.astype(F32) * normed_one, 0)[None]
    qkv_part = weight_grad(attention_input_both, both_cores(dqkv_b))
    ring.going, up_s.first, qkv_part, grad_gain_one = tied(
        ring.going, up_s.first, qkv_part, grad_gain_one
    )
    ring.go()
    up_s.second()
    qkv_s = Scatter(qkv_part)
    grad_gain_one = grad_gain_one + sum(
        around(grad_gain_one, by) for by in range(1, lax.axis_size("tp"))
    )
    ring.going, grad_gain_one = tied(ring.going, grad_gain_one)
    ring.go()
    ring.going, up_s.last, qkv_s.first = tied(ring.going, up_s.last, qkv_s.first)
    ring.go()
    qkv_s.second()
    out_s = Scatter(out_part)
    grad_up = up_s.result()
    ring.going, qkv_s.last, out_s.first, grad_up = tied(
        ring.going, qkv_s.last, out_s.first, grad_up
    )
    ring.go()
    out_s.second()
    grad_qkv = qkv_s.result()
    grad_gains = jnp.concatenate(
        [grad_gain_one, grad_gain_two[None], grad_gain_three[None], grad_gain_four[None]], 0
    )
    grad_gains = jnp.sum(
        lax.all_to_all(
            grad_gains.reshape(4, 2 * planes, -1).transpose(1, 0, 2),
            ("fsdp", "ctx"),
            0,
            0,
            tiled=True,
        ),
        0,
    )
    ring.going, out_s.last, grad_qkv = tied(ring.going, out_s.last, grad_qkv)
    ring.go()
    grad_out = out_s.result().T
    ring.going, grad_out, grad_gains = tied(ring.going, grad_out, grad_gains)
    dattn_in = ring.finish()
    dattn_in = dattn_in.astype(F32)
    grad_input = dafter + norm_back(dattn_in * scale_one, normed_one, factor_one)
    grad_input = grad_input.astype(BF)
    return (
        output.reshape(hidden_in.shape),
        grad_input.reshape(hidden_in.shape),
        grad_qkv[:, :q_cols],
        grad_qkv[:, q_cols : q_cols + kv_cols],
        grad_qkv[:, q_cols + kv_cols :],
        grad_out,
        grad_gate,
        grad_up,
        grad_down,
        grad_gains[0],
        grad_gains[1],
        grad_gains[2],
        grad_gains[3],
    )


def general_body(
    hidden_in,
    lengths,
    query_weight,
    key_weight,
    value_weight,
    w_out,
    w_gate,
    w_up,
    w_down,
    gain_attn_in,
    gain_attn_out,
    gain_ffn_in,
    gain_ffn_out,
    cotangent,
):
    seqs_here, tok_here, width = hidden_in.shape
    row_count = seqs_here * tok_here
    head_groups = QUERY_HEADS // KEY_VALUE_HEADS
    gathered = (
        lax.all_gather(query_weight, ("fsdp", "ctx"), axis=0, tiled=True),
        lax.all_gather(key_weight, ("fsdp", "ctx"), axis=0, tiled=True),
        lax.all_gather(value_weight, ("fsdp", "ctx"), axis=0, tiled=True),
        lax.all_gather(w_out, ("fsdp", "ctx"), axis=1, tiled=True),
        lax.all_gather(w_gate, ("fsdp", "ctx"), axis=0, tiled=True),
        lax.all_gather(w_up, ("fsdp", "ctx"), axis=0, tiled=True),
        lax.all_gather(w_down, ("fsdp", "ctx"), axis=1, tiled=True),
        lax.all_gather(gain_attn_in, ("fsdp", "ctx"), axis=0, tiled=True),
        lax.all_gather(gain_attn_out, ("fsdp", "ctx"), axis=0, tiled=True),
        lax.all_gather(gain_ffn_in, ("fsdp", "ctx"), axis=0, tiled=True),
        lax.all_gather(gain_ffn_out, ("fsdp", "ctx"), axis=0, tiled=True),
    )
    query_full, key_full, value_full, out_full, gate_full, up_full, down_full = gathered[:7]
    scale_one = 1.0 + gathered[7].astype(jnp.float32)
    scale_two = 1.0 + gathered[8].astype(jnp.float32)
    scale_three = 1.0 + gathered[9].astype(jnp.float32)
    scale_four = 1.0 + gathered[10].astype(jnp.float32)
    kv_local = key_full.shape[1] // HEAD_SIZE
    own_start = lax.axis_index("ctx") * tok_here
    query_pos = own_start + jnp.arange(tok_here, dtype=jnp.int32)
    key_pos = jnp.arange(SEQUENCE_SLOTS, dtype=jnp.int32)
    valid = query_pos[None, :] < lengths[:, None]
    allowed = (
        (key_pos[None, None, :] <= query_pos[None, :, None])
        & (key_pos[None, None, :] < lengths[:, None, None])
    )[:, None, None]
    flat_in = hidden_in.astype(jnp.float32).reshape(row_count, width)
    normed_one, factor_one = normalize(flat_in)
    attention_input = (normed_one * scale_one).astype(jnp.bfloat16)
    query_b = plain_dot(attention_input, query_full).astype(jnp.bfloat16)
    key_b = (
        plain_dot(attention_input, key_full)
        .astype(jnp.bfloat16)
        .reshape(seqs_here, tok_here, kv_local * HEAD_SIZE)
    )
    value_b = (
        plain_dot(attention_input, value_full)
        .astype(jnp.bfloat16)
        .reshape(seqs_here, tok_here, kv_local * HEAD_SIZE)
    )
    key_all, value_all = (
        lax.all_gather(key_b, "ctx", axis=1, tiled=True),
        lax.all_gather(value_b, "ctx", axis=1, tiled=True),
    )
    query_five = query_b.reshape(seqs_here, tok_here, kv_local, head_groups, HEAD_SIZE)
    key_four = key_all.reshape(seqs_here, SEQUENCE_SLOTS, kv_local, HEAD_SIZE)
    value_four = value_all.reshape(seqs_here, SEQUENCE_SLOTS, kv_local, HEAD_SIZE)
    raw = (
        jnp.einsum("stkgd,sukd->skgtu", query_five, key_four, preferred_element_type=jnp.float32)
        * QSCALE
    )
    bent = jnp.tanh(raw / CAP)
    masked = jnp.where(allowed, CAP * bent, NEG)
    largest = jnp.max(masked, -1, keepdims=True)
    logsum = largest + jnp.log(jnp.sum(jnp.exp(masked - largest), -1, keepdims=True))
    probs = jnp.exp(masked - logsum)
    probs_b = probs.astype(jnp.bfloat16)
    attended = (
        jnp.einsum("skgtu,sukd->stkgd", probs_b, value_four, preferred_element_type=jnp.float32)
        .astype(jnp.bfloat16)
        .reshape(row_count, -1)
    )
    attn = lax.psum(plain_dot(attended, out_full).astype(jnp.bfloat16), "tp").astype(jnp.float32)
    normed_two, factor_two = normalize(attn)
    after_attn = flat_in + normed_two * scale_two
    normed_three, factor_three = normalize(after_attn)
    ffn_in = (normed_three * scale_three).astype(jnp.bfloat16)
    gate = plain_dot(ffn_in, gate_full)
    upward = plain_dot(ffn_in, up_full)
    activated, gelu_pull = jax.vjp(gelu_tanh, gate)
    hidden_b = (activated * upward).astype(jnp.bfloat16)
    ffn_out = lax.psum(plain_dot(hidden_b, down_full).astype(jnp.bfloat16), "tp").astype(
        jnp.float32
    )
    normed_four, factor_four = normalize(ffn_out)
    result = after_attn + normed_four * scale_four
    cot = cotangent.astype(jnp.float32).reshape(row_count, width) * valid.reshape(
        row_count, 1
    ).astype(jnp.float32)
    query_back, key_back, value_back, out_back, gate_back, up_back, down_back = (
        lax.all_gather(query_weight, ("fsdp", "ctx"), axis=0, tiled=True),
        lax.all_gather(key_weight, ("fsdp", "ctx"), axis=0, tiled=True),
        lax.all_gather(value_weight, ("fsdp", "ctx"), axis=0, tiled=True),
        lax.all_gather(w_out, ("fsdp", "ctx"), axis=1, tiled=True),
        lax.all_gather(w_gate, ("fsdp", "ctx"), axis=0, tiled=True),
        lax.all_gather(w_up, ("fsdp", "ctx"), axis=0, tiled=True),
        lax.all_gather(w_down, ("fsdp", "ctx"), axis=1, tiled=True),
    )
    grad_gain_four = jnp.sum(cot * normed_four, 0)
    dffn_b = norm_back(cot * scale_four, normed_four, factor_four).astype(jnp.bfloat16)
    grad_down = left_dot(hidden_b, dffn_b)
    dhidden = right_dot(dffn_b, down_back)
    dgate_b = gelu_pull(dhidden * upward)[0].astype(jnp.bfloat16)
    dup_b = (dhidden * activated).astype(jnp.bfloat16)
    grad_gate = left_dot(ffn_in, dgate_b)
    grad_up = left_dot(ffn_in, dup_b)
    dffn_in = lax.psum(
        (right_dot(dgate_b, gate_back) + right_dot(dup_b, up_back)).astype(jnp.bfloat16), "tp"
    ).astype(jnp.float32)
    grad_gain_three = jnp.sum(dffn_in * normed_three, 0)
    dafter = cot + norm_back(dffn_in * scale_three, normed_three, factor_three)
    grad_gain_two = jnp.sum(dafter * normed_two, 0)
    dattn_b = norm_back(dafter * scale_two, normed_two, factor_two).astype(jnp.bfloat16)
    grad_out = left_dot(attended, dattn_b)
    dattended = right_dot(dattn_b, out_back).astype(jnp.bfloat16).reshape(query_five.shape)
    dprobs = jnp.einsum(
        "stkgd,sukd->skgtu", dattended, value_four, preferred_element_type=jnp.float32
    )
    weighted = jnp.sum(probs * dprobs, -1, keepdims=True)
    draw_b = (probs * (dprobs - weighted) * (1.0 - bent * bent)).astype(jnp.bfloat16)
    dquery_b = (
        (
            jnp.einsum("skgtu,sukd->stkgd", draw_b, key_four, preferred_element_type=jnp.float32)
            * QSCALE
        )
        .astype(jnp.bfloat16)
        .reshape(row_count, -1)
    )
    dvalue_part = jnp.einsum(
        "skgtu,stkgd->sukd", probs_b, dattended, preferred_element_type=jnp.float32
    )
    dkey_part = (
        jnp.einsum("skgtu,stkgd->sukd", draw_b, query_five, preferred_element_type=jnp.float32)
        * QSCALE
    )
    dkey, dvalue = (
        lax.psum_scatter(
            dkey_part.astype(jnp.bfloat16), "ctx", scatter_dimension=1, tiled=True
        ).astype(jnp.float32),
        lax.psum_scatter(
            dvalue_part.astype(jnp.bfloat16), "ctx", scatter_dimension=1, tiled=True
        ).astype(jnp.float32),
    )
    dkey_b = dkey.astype(jnp.bfloat16).reshape(row_count, -1)
    dvalue_b = dvalue.astype(jnp.bfloat16).reshape(row_count, -1)
    grad_query = left_dot(attention_input, dquery_b)
    grad_key = left_dot(attention_input, dkey_b)
    grad_value = left_dot(attention_input, dvalue_b)
    dattn_in = lax.psum(
        (
            right_dot(dquery_b, query_back)
            + right_dot(dkey_b, key_back)
            + right_dot(dvalue_b, value_back)
        ).astype(jnp.bfloat16),
        "tp",
    ).astype(jnp.float32)
    grad_gain_one = jnp.sum(dattn_in * normed_one, 0)
    grad_input = dafter + norm_back(dattn_in * scale_one, normed_one, factor_one)
    summed = (
        lax.psum_scatter(
            grad_query.astype(jnp.bfloat16), ("fsdp", "ctx"), scatter_dimension=0, tiled=True
        ).astype(jnp.float32),
        lax.psum_scatter(
            grad_key.astype(jnp.bfloat16), ("fsdp", "ctx"), scatter_dimension=0, tiled=True
        ).astype(jnp.float32),
        lax.psum_scatter(
            grad_value.astype(jnp.bfloat16), ("fsdp", "ctx"), scatter_dimension=0, tiled=True
        ).astype(jnp.float32),
        lax.psum_scatter(
            grad_out.astype(jnp.bfloat16), ("fsdp", "ctx"), scatter_dimension=1, tiled=True
        ).astype(jnp.float32),
        lax.psum_scatter(
            grad_gate.astype(jnp.bfloat16), ("fsdp", "ctx"), scatter_dimension=0, tiled=True
        ).astype(jnp.float32),
        lax.psum_scatter(
            grad_up.astype(jnp.bfloat16), ("fsdp", "ctx"), scatter_dimension=0, tiled=True
        ).astype(jnp.float32),
        lax.psum_scatter(
            grad_down.astype(jnp.bfloat16), ("fsdp", "ctx"), scatter_dimension=1, tiled=True
        ).astype(jnp.float32),
        lax.psum_scatter(
            grad_gain_one.astype(jnp.bfloat16), ("fsdp", "ctx"), scatter_dimension=0, tiled=True
        ).astype(jnp.float32),
        lax.psum_scatter(
            grad_gain_two.astype(jnp.bfloat16), ("fsdp", "ctx"), scatter_dimension=0, tiled=True
        ).astype(jnp.float32),
        lax.psum_scatter(
            grad_gain_three.astype(jnp.bfloat16), ("fsdp", "ctx"), scatter_dimension=0, tiled=True
        ).astype(jnp.float32),
        lax.psum_scatter(
            grad_gain_four.astype(jnp.bfloat16), ("fsdp", "ctx"), scatter_dimension=0, tiled=True
        ).astype(jnp.float32),
    )
    return (
        result.astype(jnp.bfloat16).reshape(hidden_in.shape),
        grad_input.astype(jnp.bfloat16).reshape(hidden_in.shape),
        summed[0],
        summed[1],
        summed[2],
        summed[3],
        summed[4],
        summed[5],
        summed[6],
        summed[7],
        summed[8],
        summed[9],
        summed[10],
    )


def solution(mesh):
    square = mesh.shape["ctx"] == 4 and mesh.shape["fsdp"] == 2
    return jax.shard_map(
        plane_body if square else general_body,
        mesh=mesh,
        in_specs=(
            P("fsdp", "ctx", None),
            P("fsdp"),
            P(("fsdp", "ctx"), "tp"),
            P(("fsdp", "ctx"), "tp"),
            P(("fsdp", "ctx"), "tp"),
            P("tp", ("fsdp", "ctx")),
            P(("fsdp", "ctx"), "tp"),
            P(("fsdp", "ctx"), "tp"),
            P("tp", ("fsdp", "ctx")),
            P(("fsdp", "ctx")),
            P(("fsdp", "ctx")),
            P(("fsdp", "ctx")),
            P(("fsdp", "ctx")),
            P("fsdp", "ctx", None),
        ),
        out_specs=(
            P("fsdp", "ctx", None),
            P("fsdp", "ctx", None),
            P(("fsdp", "ctx"), "tp"),
            P(("fsdp", "ctx"), "tp"),
            P(("fsdp", "ctx"), "tp"),
            P("tp", ("fsdp", "ctx")),
            P(("fsdp", "ctx"), "tp"),
            P(("fsdp", "ctx"), "tp"),
            P("tp", ("fsdp", "ctx")),
            P(("fsdp", "ctx")),
            P(("fsdp", "ctx")),
            P(("fsdp", "ctx")),
            P(("fsdp", "ctx")),
        ),
        check_vma=False,
    )
```

```python
import jax
import jax.numpy as jnp
from jax import lax
from jax.experimental import pallas as pl
from jax.experimental.pallas import tpu as pltpu
from jax.sharding import PartitionSpec as P

QUERY_HEADS = 8
KEY_VALUE_HEADS = 4
HEAD_SIZE = 256
SEQUENCE_SLOTS = 2048


EPS = 1e-06
CAP = 50.0
QSCALE = 0.0625
NEG = -1e30


def normalize(value_rows):
    factor = lax.rsqrt(jnp.mean(value_rows * value_rows, -1, keepdims=True) + EPS)
    return (value_rows * factor, factor)


def norm_back(grad_hat, normed, factor):
    return factor * (grad_hat - normed * jnp.mean(grad_hat * normed, -1, keepdims=True))


def plain_dot(first, second):
    return jnp.dot(first, second, preferred_element_type=jnp.float32)


def left_dot(first, second):
    return lax.dot_general(
        first, second, (((0,), (0,)), ((), ())), preferred_element_type=jnp.float32
    )


def right_dot(first, second):
    return lax.dot_general(
        first, second, (((1,), (1,)), ((), ())), preferred_element_type=jnp.float32
    )


def gelu_tanh(value_rows):
    return jax.nn.gelu(value_rows, approximate=True)


BF = jnp.bfloat16
F32 = jnp.float32

LINKS = {
    "x": ("ctx", [(0, 1), (1, 0), (2, 3), (3, 2)]),
    "y": ("ctx", [(0, 2), (2, 0), (1, 3), (3, 1)]),
    "diagonal": ("ctx", [(0, 3), (3, 0), (1, 2), (2, 1)]),
    "core": ("fsdp", [(0, 1), (1, 0)]),
}
ORDER = [(0, 0), (0, 1), (1, 1), (2, 0), (1, 0), (3, 0), (3, 1), (2, 1)]


def tied(*values):
    return lax.optimization_barrier(values)


def send(link, value):
    return lax.ppermute(value, *LINKS[link])


def around(value, by=1):
    size = lax.axis_size("tp")
    return lax.ppermute(value, "tp", [(i, (i + by) % size) for i in range(size)])


def halves(block):
    half = block.shape[0] // 2
    return block[:half], block[half:]


class Scatter:
    def __init__(self, blocks):
        self.kept, to_x, to_y = blocks
        self.half = to_x.shape[0] // 2
        self.first = (send("x", to_x), send("y", to_y))

    def second(self):
        half, (from_x, from_y) = self.half, self.first
        x_low, y_top = self.kept[2 * half : 3 * half], self.kept[3 * half :]
        self.last = (
            send("y", (y_top.astype(F32) + from_x[half:].astype(F32)).astype(BF)),
            send("x", (x_low.astype(F32) + from_y[:half].astype(F32)).astype(BF)),
        )

    def result(self):
        half, (from_x, from_y), (y_top, x_low) = self.half, self.first, self.last
        kept = self.kept
        top = kept[:half].astype(F32) + from_x[:half].astype(F32) + y_top.astype(F32)
        low = kept[half : 2 * half].astype(F32) + from_y[half:].astype(F32) + x_low.astype(F32)
        return jnp.concatenate([top, low], 0)


class Ring:
    def __init__(self, value):
        self.value, self.step = value, 0
        self.size, self.me = lax.axis_size("tp"), lax.axis_index("tp")
        self.rows = value.shape[0] // self.size
        self.whole = jnp.zeros_like(value)
        self.going = around(self.block(self.me - 1))

    def block(self, index):
        start = (index + self.size) % self.size * self.rows
        return lax.dynamic_slice_in_dim(self.value, start, self.rows, 0)

    def put(self):
        index = (self.me - (self.step - self.size + 1) + self.size) % self.size
        self.whole = lax.dynamic_update_slice_in_dim(self.whole, self.going, index * self.rows, 0)

    def go(self):
        if self.step < self.size - 1:
            own = self.block(self.me - 2 - self.step)
            self.going = (self.going.astype(F32) + own.astype(F32)).astype(BF)
        self.step += 1
        if self.step >= self.size - 1:
            self.put()
        if self.step < 2 * self.size - 2:
            self.going = around(self.going)

    def finish(self):
        while self.step < 2 * self.size - 2:
            self.go()
        return self.whole


VMEM_BYTES = 56 * 2**20


def kernel_params():
    return pltpu.CompilerParams(vmem_limit_bytes=VMEM_BYTES)


def cut_of(size):
    return next((cut for cut in (768, 512) if size % cut == 0), size)


def rowwise(fn, rows, vectors, dtypes, sums=0, block=128):
    count, width = rows[0].shape
    n_in, n_out = len(rows) + len(vectors), len(dtypes)

    def kernel(*refs):
        results = fn(*(ref[...] for ref in refs[:n_in]))
        for ref, value in zip(refs[n_in : n_in + n_out], results):
            ref[...] = value.astype(ref.dtype)
        for ref, value in zip(refs[n_in + n_out :], results[n_out:]):
            part = jnp.sum(value.reshape(block // 8, 8, width), 0)

            @pl.when(pl.program_id(0) == 0)
            def _():
                ref[...] = part

            @pl.when(pl.program_id(0) > 0)
            def _():
                ref[...] += part

    by_row = pl.BlockSpec((block, width), lambda i: (i, 0))
    return pl.pallas_call(
        kernel,
        grid=(count // block,),
        in_specs=[by_row] * len(rows) + [pl.BlockSpec((1, width), lambda i: (0, 0))] * len(vectors),
        out_specs=[by_row] * n_out + [pl.BlockSpec((8, width), lambda i: (0, 0))] * sums,
        out_shape=[jax.ShapeDtypeStruct((count, width), dtype) for dtype in dtypes]
        + [jax.ShapeDtypeStruct((8, width), F32)] * sums,
        compiler_params=kernel_params(),
        cost_estimate=pl.CostEstimate(
            flops=20 * count * width, bytes_accessed=4 * count * width * n_in, transcendentals=0
        ),
    )(*rows, *vectors)


ROOT = 0.7978845608028654


def gelu_parts(z):
    bend = jnp.tanh(ROOT * (z + 0.044715 * (z * z * z)))
    value = 0.5 * z * (1.0 + bend)
    slope = 0.5 * (1.0 + bend) + 0.5 * z * (1.0 - bend * bend) * (
        ROOT * (1.0 + (3.0 * 0.044715) * (z * z))
    )
    return value, slope


def ffn_hidden(x, weights):
    count, width = x.shape
    units = weights.shape[1] // 3
    cut = cut_of(units)

    def kernel(x_ref, gate_w, up_w, gate_ref, up_ref, hidden_ref):
        gate = plain_dot(x_ref[...], gate_w[...])
        up = plain_dot(x_ref[...], up_w[...])
        gate_ref[...] = gate
        up_ref[...] = up
        hidden_ref[...] = (gelu_parts(gate)[0] * up).astype(BF)

    out = pl.BlockSpec((count, cut), lambda j: (0, j))
    return pl.pallas_call(
        kernel,
        grid=(units // cut,),
        in_specs=[
            pl.BlockSpec((count, width), lambda j: (0, 0)),
            pl.BlockSpec((width, cut), lambda j: (0, j)),
            pl.BlockSpec((width, cut), lambda j: (0, j + units // cut)),
        ],
        out_specs=[out] * 3,
        out_shape=[
            jax.ShapeDtypeStruct((count, units), F32),
            jax.ShapeDtypeStruct((count, units), F32),
            jax.ShapeDtypeStruct((count, units), BF),
        ],
        compiler_params=kernel_params(),
        cost_estimate=pl.CostEstimate(
            flops=4 * count * width * units,
            bytes_accessed=4 * width * units + 10 * count * units,
            transcendentals=count * units,
        ),
    )(x, weights, weights)


def ffn_down(hidden, weights):
    count, units = hidden.shape
    width = weights.shape[0]
    cut = cut_of(width)

    def kernel(x_ref, w_ref, out_ref):
        out_ref[...] = right_dot(x_ref[...], w_ref[...]).astype(BF)

    return pl.pallas_call(
        kernel,
        grid=(width // cut,),
        in_specs=[
            pl.BlockSpec((count, units), lambda j: (0, 0)),
            pl.BlockSpec((cut, units), lambda j: (j, 2)),
        ],
        out_specs=pl.BlockSpec((count, cut), lambda j: (0, j)),
        out_shape=jax.ShapeDtypeStruct((count, width), BF),
        compiler_params=kernel_params(),
        cost_estimate=pl.CostEstimate(
            flops=2 * count * width * units, bytes_accessed=2 * width * units, transcendentals=0
        ),
    )(hidden, weights)


def ffn_hidden_back(dffn, weights, gate, up):
    count, width = dffn.shape
    units = gate.shape[1]
    cut = cut_of(units)

    def kernel(d_ref, w_ref, gate_ref, up_ref, dgate_ref, dup_ref):
        dhidden = plain_dot(d_ref[...], w_ref[...])
        value, slope = gelu_parts(gate_ref[...])
        dgate_ref[...] = (dhidden * up_ref[...] * slope).astype(BF)
        dup_ref[...] = (dhidden * value).astype(BF)

    out = pl.BlockSpec((count, cut), lambda j: (0, j))
    return pl.pallas_call(
        kernel,
        grid=(units // cut,),
        in_specs=[
            pl.BlockSpec((count, width), lambda j: (0, 0)),
            pl.BlockSpec((width, cut), lambda j: (0, j + 2 * (units // cut))),
            out,
            out,
        ],
        out_specs=[out] * 2,
        out_shape=[jax.ShapeDtypeStruct((count, units), BF)] * 2,
        compiler_params=kernel_params(),
        cost_estimate=pl.CostEstimate(
            flops=2 * count * width * units,
            bytes_accessed=2 * width * units + 12 * count * units,
            transcendentals=count * units,
        ),
    )(dffn, weights, gate, up)


def ffn_input_back(dgate, dup, weights):
    count, units = dgate.shape
    width = weights.shape[0]
    cut = cut_of(width)

    def kernel(dgate_ref, dup_ref, gate_w, up_w, out_ref):
        out_ref[...] = (
            right_dot(dgate_ref[...], gate_w[...]) + right_dot(dup_ref[...], up_w[...])
        ).astype(BF)

    whole = pl.BlockSpec((count, units), lambda j: (0, 0))
    return pl.pallas_call(
        kernel,
        grid=(width // cut,),
        in_specs=[
            whole,
            whole,
            pl.BlockSpec((cut, units), lambda j: (j, 0)),
            pl.BlockSpec((cut, units), lambda j: (j, 1)),
        ],
        out_specs=pl.BlockSpec((count, cut), lambda j: (0, j)),
        out_shape=jax.ShapeDtypeStruct((count, width), BF),
        compiler_params=kernel_params(),
        cost_estimate=pl.CostEstimate(
            flops=4 * count * width * units, bytes_accessed=4 * width * units, transcendentals=0
        ),
    )(dgate, dup, weights, weights)


def weight_grad(rows, rows_far, cols, cols_far):
    count, half_width = rows_far.shape
    width = cols.shape[1]
    cut = cut_of(width)
    half = half_width // 8
    place = jnp.stack([lax.axis_index("fsdp"), lax.axis_index("ctx")]).astype(jnp.int32)

    def kernel(
        place_ref, near_ref, far_ref, cols_ref, cols_far_ref, *rest
    ):
        outs, (near_t, far_t, total) = rest[:3], rest[3:]

        @pl.when(pl.program_id(0) == 0)
        def _():
            near_t[...] = near_ref[...].T
            far_t[...] = far_ref[...].T

        total[...] = plain_dot(near_t[...], cols_ref[...]) + plain_dot(
            far_t[...], cols_far_ref[...]
        )
        for index, (k, low) in enumerate(ORDER):
            start = (lax.bitwise_xor(place_ref[1], k) * 2 + low) * half
            block = total[pl.ds(pl.multiple_of(start, 16), half), :].astype(BF)
            out, at = (outs[0], index) if index < 4 else (outs[1 + (index - 4) // 2], index % 2)
            out[at * half : (at + 1) * half, :] = block

    by_cut = pl.BlockSpec((count, cut), lambda j, place: (0, j))
    sizes = (4 * half, 2 * half, 2 * half)
    return pl.pallas_call(
        kernel,
        grid_spec=pltpu.PrefetchScalarGridSpec(
            num_scalar_prefetch=1,
            grid=(width // cut,),
            in_specs=[
                pl.BlockSpec((count, half_width), lambda j, place: (0, place[0])),
                pl.BlockSpec((count, half_width), lambda j, place: (0, 0)),
                by_cut,
                by_cut,
            ],
            out_specs=[pl.BlockSpec((size, cut), lambda j, place: (0, j)) for size in sizes],
            scratch_shapes=[
                pltpu.VMEM((half_width, count), BF),
                pltpu.VMEM((half_width, count), BF),
                pltpu.VMEM((half_width, cut), F32),
            ],
        ),
        out_shape=[jax.ShapeDtypeStruct((size, width), BF) for size in sizes],
        compiler_params=kernel_params(),
        cost_estimate=pl.CostEstimate(
            flops=4 * count * half_width * width,
            bytes_accessed=2 * half_width * width + 4 * count * (width + half_width),
            transcendentals=0,
        ),
    )(place, rows, rows_far, cols, cols_far)


def residual_rows(attn, hidden, scale_two, scale_three):
    attn, hidden = attn.astype(F32), hidden.astype(F32)
    after = hidden + normalize(attn)[0] * scale_two
    return after, normalize(after)[0] * scale_three


def output_rows(ffn_out, after, cot, scale_four):
    normed, factor = normalize(ffn_out.astype(F32))
    cot = cot.astype(F32)
    return (
        after + normed * scale_four,
        norm_back(cot * scale_four, normed, factor),
        cot * normed,
    )


def residual_back_rows(dffn_in, after, attn, cot, scale_three, scale_two):
    dffn_in = dffn_in.astype(F32)
    normed, factor = normalize(after)
    dafter = cot.astype(F32) + norm_back(dffn_in * scale_three, normed, factor)
    normed_two, factor_two = normalize(attn.astype(F32))
    dattn = norm_back(dafter * scale_two, normed_two, factor_two)
    return dafter, dattn, dffn_in * normed, dafter * normed_two


def plane_body(
    hidden_in,
    lengths,
    query_weight,
    key_weight,
    value_weight,
    w_out,
    w_gate,
    w_up,
    w_down,
    gain_attn_in,
    gain_attn_out,
    gain_ffn_in,
    gain_ffn_out,
    cotangent,
):
    seqs_here, tok_here, width = hidden_in.shape
    row_count = seqs_here * tok_here
    head_groups = QUERY_HEADS // KEY_VALUE_HEADS
    half_width = width // 2
    q_cols, kv_cols = query_weight.shape[1], key_weight.shape[1]
    size = lax.axis_size("tp")
    kv_local = kv_cols // HEAD_SIZE
    planes, me = lax.axis_size("ctx"), lax.axis_index("ctx")

    core = lax.axis_index("fsdp")

    def gather(shard):
        return lax.all_gather(shard, ("fsdp", "ctx"), axis=0, tiled=True)

    def far_half(rows):
        return send("core", lax.dynamic_slice_in_dim(rows, (1 - core) * half_width, half_width, 1))

    attention_shards = jnp.concatenate([query_weight, key_weight, value_weight, w_out.T], 1)
    attention_w = gather(attention_shards)
    ffn_shards = jnp.concatenate([w_gate, w_up, w_down.T], 1)
    gains = jnp.stack([gain_attn_in, gain_attn_out, gain_ffn_in, gain_ffn_out])[None]
    gains = jnp.broadcast_to(gains, (2 * planes,) + gains.shape[1:])
    gains = lax.all_to_all(gains, ("fsdp", "ctx"), 0, 0, tiled=True)
    gains = gains.transpose(1, 0, 2).reshape(4, width).astype(F32)
    scale_one, scale_two, scale_three, scale_four = (1.0 + gains[i][None] for i in range(4))
    flat_in = hidden_in.astype(F32).reshape(row_count, width)
    normed_one, factor_one = normalize(flat_in)
    attention_input = (normed_one * scale_one).astype(BF)

    attention_w, attention_input, ffn_shards = tied(attention_w, attention_input, ffn_shards)
    ffn_w = gather(ffn_shards)
    qkv_cols = q_cols + 2 * kv_cols
    qkv_w, out_w = attention_w[:, :qkv_cols], attention_w[:, qkv_cols:]
    run = jnp.arange(tok_here, dtype=jnp.int32)
    query_pos = me * tok_here + run
    key_pos = jnp.concatenate([(me ^ k) * tok_here + run for k in range(planes)])
    valid = query_pos[None, :] < lengths[:, None]
    allowed = (
        (key_pos[None, None, :] <= query_pos[None, :, None])
        & (key_pos[None, None, :] < lengths[:, None, None])
    )[:, None, None]
    qkv = plain_dot(attention_input, qkv_w).astype(BF)
    query_b = qkv[:, :q_cols]
    kv = qkv[:, q_cols:].reshape(seqs_here, tok_here, 2 * kv_cols)
    kv_all = jnp.concatenate([kv, send("x", kv), send("y", kv), send("diagonal", kv)], 1)
    query_five = query_b.reshape(seqs_here, tok_here, kv_local, head_groups, HEAD_SIZE)
    key_four = kv_all[:, :, :kv_cols].reshape(seqs_here, SEQUENCE_SLOTS, kv_local, HEAD_SIZE)
    value_four = kv_all[:, :, kv_cols:].reshape(seqs_here, SEQUENCE_SLOTS, kv_local, HEAD_SIZE)
    raw = jnp.einsum("stkgd,sukd->skgtu", query_five, key_four, preferred_element_type=F32) * QSCALE
    bent = jnp.tanh(raw / CAP)
    masked = jnp.where(allowed, CAP * bent, NEG)
    largest = jnp.max(masked, -1, keepdims=True)
    logsum = largest + jnp.log(jnp.sum(jnp.exp(masked - largest), -1, keepdims=True))
    probs = jnp.exp(masked - logsum)
    probs_b = probs.astype(BF)
    attended = (
        jnp.einsum("skgtu,sukd->stkgd", probs_b, value_four, preferred_element_type=F32)
        .astype(BF)
        .reshape(row_count, -1)
    )
    attn = right_dot(attended, out_w).astype(BF)
    ring = Ring(attn)
    for _ in range(2 * size - 3):
        ring.go()
    attn = ring.finish()
    hidden_rows = hidden_in.reshape(row_count, width)
    after_attn, ffn_in = rowwise(
        residual_rows, [attn, hidden_rows], [scale_two, scale_three], [F32, BF]
    )
    gate, upward, hidden_b = ffn_hidden(ffn_in, ffn_w)
    ffn_out = ffn_down(hidden_b, ffn_w)
    ffn_out, hidden_b, attended, ffn_in, attention_input, cotangent = tied(
        ffn_out, hidden_b, attended, ffn_in, attention_input, cotangent
    )
    ffn_out = lax.psum(ffn_out, "tp")

    hidden_far, attended_far = send("core", hidden_b), send("core", attended)
    ffn_in_far, attention_input_far = far_half(ffn_in), far_half(attention_input)
    cot = jnp.where(
        valid.reshape(row_count, 1), cotangent.reshape(row_count, width), jnp.zeros((), BF)
    )
    ffn_out, hidden_far, attended_far, ffn_in_far, attention_input_far, cot = tied(
        ffn_out, hidden_far, attended_far, ffn_in_far, attention_input_far, cot
    )
    output, dffn_b, gain_four_rows = rowwise(
        output_rows, [ffn_out, after_attn, cot], [scale_four], [BF, BF], 1
    )
    dgate_b, dup_b = ffn_hidden_back(dffn_b, ffn_w, gate, upward)
    dffn_in = ffn_input_back(dgate_b, dup_b, ffn_w)
    dffn_far = far_half(dffn_b)

    dffn_in, dffn_far, dgate_b, dup_b = tied(dffn_in, dffn_far, dgate_b, dup_b)
    ring = Ring(dffn_in)
    dgate_far = send("core", dgate_b)
    down_part = weight_grad(dffn_b, dffn_far, hidden_b, hidden_far)
    ring.going, down_part, dgate_far = tied(ring.going, down_part, dgate_far)
    ring.go()
    down_s = Scatter(down_part)
    dup_far = send("core", dup_b)
    gate_part = weight_grad(ffn_in, ffn_in_far, dgate_b, dgate_far)
    ring.going, gate_part, dup_far = tied(ring.going, gate_part, dup_far)
    ring.go()
    up_part = weight_grad(ffn_in, ffn_in_far, dup_b, dup_far)
    ring.going, up_part = tied(ring.going, up_part)
    ring.go()
    ring.going, down_s.first, gate_part = tied(ring.going, down_s.first, gate_part)
    ring.go()
    down_s.second()
    gate_s = Scatter(gate_part)
    ring.go()
    dffn_in, gate_s.first, down_s.last, up_part = tied(
        ring.finish(), gate_s.first, down_s.last, up_part
    )
    gate_s.second()
    dafter, dattn_b, gain_three_rows, gain_two_rows = rowwise(
        residual_back_rows,
        [dffn_in, after_attn, attn, cot],
        [scale_three, scale_two],
        [F32, BF],
        2,
    )
    dattended = plain_dot(dattn_b, out_w).astype(BF).reshape(query_five.shape)
    dprobs = jnp.einsum("stkgd,sukd->skgtu", dattended, value_four, preferred_element_type=F32)
    weighted = jnp.sum(probs * dprobs, -1, keepdims=True)
    draw_b = (probs * (dprobs - weighted) * (1.0 - bent * bent)).astype(BF)
    dvalue_part = jnp.einsum("skgtu,stkgd->sukd", probs_b, dattended, preferred_element_type=F32)
    dkey_part = (
        jnp.einsum("skgtu,stkgd->sukd", draw_b, query_five, preferred_element_type=F32) * QSCALE
    )
    dkv = [
        jnp.concatenate(
            [
                part[:, k * tok_here : (k + 1) * tok_here].astype(BF).reshape(row_count, kv_cols)
                for part in (dkey_part, dvalue_part)
            ],
            1,
        )
        for k in range(planes)
    ]
    dattn_far = far_half(dattn_b)
    dkv, dattn_far, gate_s.last = tied(dkv, dattn_far, gate_s.last)
    dkv = [dkv[0], send("x", dkv[1]), send("y", dkv[2]), send("diagonal", dkv[3])]
    out_part = weight_grad(dattn_b, dattn_far, attended, attended_far)
    dquery_b = (
        (jnp.einsum("skgtu,sukd->stkgd", draw_b, key_four, preferred_element_type=F32) * QSCALE)
        .astype(BF)
        .reshape(row_count, -1)
    )
    grad_down = down_s.result().T
    grad_gate = gate_s.result()
    dkv, dquery_b, out_part, grad_down, grad_gate, up_part = tied(
        dkv, dquery_b, out_part, grad_down, grad_gate, up_part
    )
    up_s = Scatter(up_part)
    dkv_b = sum(part.astype(F32) for part in dkv).astype(BF)
    dqkv_b = jnp.concatenate([dquery_b, dkv_b], 1)
    dattn_in = right_dot(dqkv_b, qkv_w)
    dattn_in, dqkv_b, dafter = tied(dattn_in.astype(BF), dqkv_b, dafter)

    ring = Ring(dattn_in)
    dqkv_far = send("core", dqkv_b)
    grad_gain_one = jnp.sum(dattn_in.astype(F32) * normed_one, 0)
    qkv_part = weight_grad(attention_input, attention_input_far, dqkv_b, dqkv_far)
    grad_gains = jnp.stack(
        [grad_gain_one]
        + [jnp.sum(rows, 0) / size for rows in (gain_two_rows, gain_three_rows, gain_four_rows)]
    )
    grad_gains = grad_gains.reshape(4, 2 * planes, 1, -1).transpose(1, 2, 0, 3)
    grad_gains = jnp.broadcast_to(grad_gains, (2 * planes, size) + grad_gains.shape[2:])
    grad_gains = grad_gains.reshape((-1,) + grad_gains.shape[2:])
    ring.going, qkv_part = tied(ring.going, qkv_part)
    ring.go()
    ring.going, grad_gains = tied(ring.going, grad_gains)
    ring.go()
    grad_gains = lax.all_to_all(grad_gains, ("fsdp", "ctx", "tp"), 0, 0, tiled=True)
    ring.going, up_s.first = tied(ring.going, up_s.first)
    up_s.second()
    qkv_s = Scatter(qkv_part)
    ring.go()
    ring.going, out_part = tied(ring.going, out_part)
    ring.go()
    ring.going, up_s.last, qkv_s.first = tied(ring.going, up_s.last, qkv_s.first)
    qkv_s.second()
    out_s = Scatter(out_part)
    ring.go()
    grad_up = up_s.result()
    ring.going, qkv_s.last, out_s.first, grad_up = tied(
        ring.going, qkv_s.last, out_s.first, grad_up
    )
    out_s.second()
    grad_qkv = qkv_s.result()
    dattn_in, out_s.last, grad_gains, grad_qkv = tied(
        ring.finish(), out_s.last, grad_gains, grad_qkv
    )
    grad_gains = jnp.sum(grad_gains, 0)
    grad_out = out_s.result().T
    dattn_in = dattn_in.astype(F32)
    grad_input = dafter + norm_back(dattn_in * scale_one, normed_one, factor_one)
    grad_input = grad_input.astype(BF)
    return (
        output.reshape(hidden_in.shape),
        grad_input.reshape(hidden_in.shape),
        grad_qkv[:, :q_cols],
        grad_qkv[:, q_cols : q_cols + kv_cols],
        grad_qkv[:, q_cols + kv_cols :],
        grad_out,
        grad_gate,
        grad_up,
        grad_down,
        grad_gains[0],
        grad_gains[1],
        grad_gains[2],
        grad_gains[3],
    )


def general_body(
    hidden_in,
    lengths,
    query_weight,
    key_weight,
    value_weight,
    w_out,
    w_gate,
    w_up,
    w_down,
    gain_attn_in,
    gain_attn_out,
    gain_ffn_in,
    gain_ffn_out,
    cotangent,
):
    seqs_here, tok_here, width = hidden_in.shape
    row_count = seqs_here * tok_here
    head_groups = QUERY_HEADS // KEY_VALUE_HEADS
    gathered = (
        lax.all_gather(query_weight, ("fsdp", "ctx"), axis=0, tiled=True),
        lax.all_gather(key_weight, ("fsdp", "ctx"), axis=0, tiled=True),
        lax.all_gather(value_weight, ("fsdp", "ctx"), axis=0, tiled=True),
        lax.all_gather(w_out, ("fsdp", "ctx"), axis=1, tiled=True),
        lax.all_gather(w_gate, ("fsdp", "ctx"), axis=0, tiled=True),
        lax.all_gather(w_up, ("fsdp", "ctx"), axis=0, tiled=True),
        lax.all_gather(w_down, ("fsdp", "ctx"), axis=1, tiled=True),
        lax.all_gather(gain_attn_in, ("fsdp", "ctx"), axis=0, tiled=True),
        lax.all_gather(gain_attn_out, ("fsdp", "ctx"), axis=0, tiled=True),
        lax.all_gather(gain_ffn_in, ("fsdp", "ctx"), axis=0, tiled=True),
        lax.all_gather(gain_ffn_out, ("fsdp", "ctx"), axis=0, tiled=True),
    )
    query_full, key_full, value_full, out_full, gate_full, up_full, down_full = gathered[:7]
    scale_one = 1.0 + gathered[7].astype(jnp.float32)
    scale_two = 1.0 + gathered[8].astype(jnp.float32)
    scale_three = 1.0 + gathered[9].astype(jnp.float32)
    scale_four = 1.0 + gathered[10].astype(jnp.float32)
    kv_local = key_full.shape[1] // HEAD_SIZE
    own_start = lax.axis_index("ctx") * tok_here
    query_pos = own_start + jnp.arange(tok_here, dtype=jnp.int32)
    key_pos = jnp.arange(SEQUENCE_SLOTS, dtype=jnp.int32)
    valid = query_pos[None, :] < lengths[:, None]
    allowed = (
        (key_pos[None, None, :] <= query_pos[None, :, None])
        & (key_pos[None, None, :] < lengths[:, None, None])
    )[:, None, None]
    flat_in = hidden_in.astype(jnp.float32).reshape(row_count, width)
    normed_one, factor_one = normalize(flat_in)
    attention_input = (normed_one * scale_one).astype(jnp.bfloat16)
    query_b = plain_dot(attention_input, query_full).astype(jnp.bfloat16)
    key_b = (
        plain_dot(attention_input, key_full)
        .astype(jnp.bfloat16)
        .reshape(seqs_here, tok_here, kv_local * HEAD_SIZE)
    )
    value_b = (
        plain_dot(attention_input, value_full)
        .astype(jnp.bfloat16)
        .reshape(seqs_here, tok_here, kv_local * HEAD_SIZE)
    )
    key_all, value_all = (
        lax.all_gather(key_b, "ctx", axis=1, tiled=True),
        lax.all_gather(value_b, "ctx", axis=1, tiled=True),
    )
    query_five = query_b.reshape(seqs_here, tok_here, kv_local, head_groups, HEAD_SIZE)
    key_four = key_all.reshape(seqs_here, SEQUENCE_SLOTS, kv_local, HEAD_SIZE)
    value_four = value_all.reshape(seqs_here, SEQUENCE_SLOTS, kv_local, HEAD_SIZE)
    raw = (
        jnp.einsum("stkgd,sukd->skgtu", query_five, key_four, preferred_element_type=jnp.float32)
        * QSCALE
    )
    bent = jnp.tanh(raw / CAP)
    masked = jnp.where(allowed, CAP * bent, NEG)
    largest = jnp.max(masked, -1, keepdims=True)
    logsum = largest + jnp.log(jnp.sum(jnp.exp(masked - largest), -1, keepdims=True))
    probs = jnp.exp(masked - logsum)
    probs_b = probs.astype(jnp.bfloat16)
    attended = (
        jnp.einsum("skgtu,sukd->stkgd", probs_b, value_four, preferred_element_type=jnp.float32)
        .astype(jnp.bfloat16)
        .reshape(row_count, -1)
    )
    attn = lax.psum(plain_dot(attended, out_full).astype(jnp.bfloat16), "tp").astype(jnp.float32)
    normed_two, factor_two = normalize(attn)
    after_attn = flat_in + normed_two * scale_two
    normed_three, factor_three = normalize(after_attn)
    ffn_in = (normed_three * scale_three).astype(jnp.bfloat16)
    gate = plain_dot(ffn_in, gate_full)
    upward = plain_dot(ffn_in, up_full)
    activated, gelu_pull = jax.vjp(gelu_tanh, gate)
    hidden_b = (activated * upward).astype(jnp.bfloat16)
    ffn_out = lax.psum(plain_dot(hidden_b, down_full).astype(jnp.bfloat16), "tp").astype(
        jnp.float32
    )
    normed_four, factor_four = normalize(ffn_out)
    result = after_attn + normed_four * scale_four
    cot = cotangent.astype(jnp.float32).reshape(row_count, width) * valid.reshape(
        row_count, 1
    ).astype(jnp.float32)
    query_back, key_back, value_back, out_back, gate_back, up_back, down_back = (
        lax.all_gather(query_weight, ("fsdp", "ctx"), axis=0, tiled=True),
        lax.all_gather(key_weight, ("fsdp", "ctx"), axis=0, tiled=True),
        lax.all_gather(value_weight, ("fsdp", "ctx"), axis=0, tiled=True),
        lax.all_gather(w_out, ("fsdp", "ctx"), axis=1, tiled=True),
        lax.all_gather(w_gate, ("fsdp", "ctx"), axis=0, tiled=True),
        lax.all_gather(w_up, ("fsdp", "ctx"), axis=0, tiled=True),
        lax.all_gather(w_down, ("fsdp", "ctx"), axis=1, tiled=True),
    )
    grad_gain_four = jnp.sum(cot * normed_four, 0)
    dffn_b = norm_back(cot * scale_four, normed_four, factor_four).astype(jnp.bfloat16)
    grad_down = left_dot(hidden_b, dffn_b)
    dhidden = right_dot(dffn_b, down_back)
    dgate_b = gelu_pull(dhidden * upward)[0].astype(jnp.bfloat16)
    dup_b = (dhidden * activated).astype(jnp.bfloat16)
    grad_gate = left_dot(ffn_in, dgate_b)
    grad_up = left_dot(ffn_in, dup_b)
    dffn_in = lax.psum(
        (right_dot(dgate_b, gate_back) + right_dot(dup_b, up_back)).astype(jnp.bfloat16), "tp"
    ).astype(jnp.float32)
    grad_gain_three = jnp.sum(dffn_in * normed_three, 0)
    dafter = cot + norm_back(dffn_in * scale_three, normed_three, factor_three)
    grad_gain_two = jnp.sum(dafter * normed_two, 0)
    dattn_b = norm_back(dafter * scale_two, normed_two, factor_two).astype(jnp.bfloat16)
    grad_out = left_dot(attended, dattn_b)
    dattended = right_dot(dattn_b, out_back).astype(jnp.bfloat16).reshape(query_five.shape)
    dprobs = jnp.einsum(
        "stkgd,sukd->skgtu", dattended, value_four, preferred_element_type=jnp.float32
    )
    weighted = jnp.sum(probs * dprobs, -1, keepdims=True)
    draw_b = (probs * (dprobs - weighted) * (1.0 - bent * bent)).astype(jnp.bfloat16)
    dquery_b = (
        (
            jnp.einsum("skgtu,sukd->stkgd", draw_b, key_four, preferred_element_type=jnp.float32)
            * QSCALE
        )
        .astype(jnp.bfloat16)
        .reshape(row_count, -1)
    )
    dvalue_part = jnp.einsum(
        "skgtu,stkgd->sukd", probs_b, dattended, preferred_element_type=jnp.float32
    )
    dkey_part = (
        jnp.einsum("skgtu,stkgd->sukd", draw_b, query_five, preferred_element_type=jnp.float32)
        * QSCALE
    )
    dkey, dvalue = (
        lax.psum_scatter(
            dkey_part.astype(jnp.bfloat16), "ctx", scatter_dimension=1, tiled=True
        ).astype(jnp.float32),
        lax.psum_scatter(
            dvalue_part.astype(jnp.bfloat16), "ctx", scatter_dimension=1, tiled=True
        ).astype(jnp.float32),
    )
    dkey_b = dkey.astype(jnp.bfloat16).reshape(row_count, -1)
    dvalue_b = dvalue.astype(jnp.bfloat16).reshape(row_count, -1)
    grad_query = left_dot(attention_input, dquery_b)
    grad_key = left_dot(attention_input, dkey_b)
    grad_value = left_dot(attention_input, dvalue_b)
    dattn_in = lax.psum(
        (
            right_dot(dquery_b, query_back)
            + right_dot(dkey_b, key_back)
            + right_dot(dvalue_b, value_back)
        ).astype(jnp.bfloat16),
        "tp",
    ).astype(jnp.float32)
    grad_gain_one = jnp.sum(dattn_in * normed_one, 0)
    grad_input = dafter + norm_back(dattn_in * scale_one, normed_one, factor_one)
    summed = (
        lax.psum_scatter(
            grad_query.astype(jnp.bfloat16), ("fsdp", "ctx"), scatter_dimension=0, tiled=True
        ).astype(jnp.float32),
        lax.psum_scatter(
            grad_key.astype(jnp.bfloat16), ("fsdp", "ctx"), scatter_dimension=0, tiled=True
        ).astype(jnp.float32),
        lax.psum_scatter(
            grad_value.astype(jnp.bfloat16), ("fsdp", "ctx"), scatter_dimension=0, tiled=True
        ).astype(jnp.float32),
        lax.psum_scatter(
            grad_out.astype(jnp.bfloat16), ("fsdp", "ctx"), scatter_dimension=1, tiled=True
        ).astype(jnp.float32),
        lax.psum_scatter(
            grad_gate.astype(jnp.bfloat16), ("fsdp", "ctx"), scatter_dimension=0, tiled=True
        ).astype(jnp.float32),
        lax.psum_scatter(
            grad_up.astype(jnp.bfloat16), ("fsdp", "ctx"), scatter_dimension=0, tiled=True
        ).astype(jnp.float32),
        lax.psum_scatter(
            grad_down.astype(jnp.bfloat16), ("fsdp", "ctx"), scatter_dimension=1, tiled=True
        ).astype(jnp.float32),
        lax.psum_scatter(
            grad_gain_one.astype(jnp.bfloat16), ("fsdp", "ctx"), scatter_dimension=0, tiled=True
        ).astype(jnp.float32),
        lax.psum_scatter(
            grad_gain_two.astype(jnp.bfloat16), ("fsdp", "ctx"), scatter_dimension=0, tiled=True
        ).astype(jnp.float32),
        lax.psum_scatter(
            grad_gain_three.astype(jnp.bfloat16), ("fsdp", "ctx"), scatter_dimension=0, tiled=True
        ).astype(jnp.float32),
        lax.psum_scatter(
            grad_gain_four.astype(jnp.bfloat16), ("fsdp", "ctx"), scatter_dimension=0, tiled=True
        ).astype(jnp.float32),
    )
    return (
        result.astype(jnp.bfloat16).reshape(hidden_in.shape),
        grad_input.astype(jnp.bfloat16).reshape(hidden_in.shape),
        summed[0],
        summed[1],
        summed[2],
        summed[3],
        summed[4],
        summed[5],
        summed[6],
        summed[7],
        summed[8],
        summed[9],
        summed[10],
    )


def solution(mesh):
    square = mesh.shape["ctx"] == 4 and mesh.shape["fsdp"] == 2
    return jax.shard_map(
        plane_body if square else general_body,
        mesh=mesh,
        in_specs=(
            P("fsdp", "ctx", None),
            P("fsdp"),
            P(("fsdp", "ctx"), "tp"),
            P(("fsdp", "ctx"), "tp"),
            P(("fsdp", "ctx"), "tp"),
            P("tp", ("fsdp", "ctx")),
            P(("fsdp", "ctx"), "tp"),
            P(("fsdp", "ctx"), "tp"),
            P("tp", ("fsdp", "ctx")),
            P(("fsdp", "ctx")),
            P(("fsdp", "ctx")),
            P(("fsdp", "ctx")),
            P(("fsdp", "ctx")),
            P("fsdp", "ctx", None),
        ),
        out_specs=(
            P("fsdp", "ctx", None),
            P("fsdp", "ctx", None),
            P(("fsdp", "ctx"), "tp"),
            P(("fsdp", "ctx"), "tp"),
            P(("fsdp", "ctx"), "tp"),
            P("tp", ("fsdp", "ctx")),
            P(("fsdp", "ctx"), "tp"),
            P(("fsdp", "ctx"), "tp"),
            P("tp", ("fsdp", "ctx")),
            P(("fsdp", "ctx")),
            P(("fsdp", "ctx")),
            P(("fsdp", "ctx")),
            P(("fsdp", "ctx")),
        ),
        check_vma=False,
    )
```

```python
import jax
import jax.numpy as jnp
from jax import lax
from jax.experimental import pallas as pl
from jax.experimental.pallas import tpu as pltpu
from jax.sharding import PartitionSpec as P

QUERY_HEADS = 8
KEY_VALUE_HEADS = 4
HEAD_SIZE = 256
SEQUENCE_SLOTS = 2048


EPS = 1e-06
CAP = 50.0
QSCALE = 0.0625
NEG = -1e30


def normalize(value_rows):
    factor = lax.rsqrt(jnp.mean(value_rows * value_rows, -1, keepdims=True) + EPS)
    return (value_rows * factor, factor)


def norm_back(grad_hat, normed, factor):
    return factor * (grad_hat - normed * jnp.mean(grad_hat * normed, -1, keepdims=True))


def plain_dot(first, second):
    return jnp.dot(first, second, preferred_element_type=jnp.float32)


def left_dot(first, second):
    return lax.dot_general(
        first, second, (((0,), (0,)), ((), ())), preferred_element_type=jnp.float32
    )


def right_dot(first, second):
    return lax.dot_general(
        first, second, (((1,), (1,)), ((), ())), preferred_element_type=jnp.float32
    )


def gelu_tanh(value_rows):
    return jax.nn.gelu(value_rows, approximate=True)


BF = jnp.bfloat16
F32 = jnp.float32

LINKS = {
    "x": ("ctx", [(0, 1), (1, 0), (2, 3), (3, 2)]),
    "y": ("ctx", [(0, 2), (2, 0), (1, 3), (3, 1)]),
    "diagonal": ("ctx", [(0, 3), (3, 0), (1, 2), (2, 1)]),
    "core": ("fsdp", [(0, 1), (1, 0)]),
}
ORDER = [(0, 0), (0, 1), (1, 1), (2, 0), (1, 0), (3, 0), (3, 1), (2, 1)]


def tied(*values):
    return lax.optimization_barrier(values)


def send(link, value):
    return lax.ppermute(value, *LINKS[link])


def around(value, by=1):
    size = lax.axis_size("tp")
    return lax.ppermute(value, "tp", [(i, (i + by) % size) for i in range(size)])


def halves(block):
    half = block.shape[0] // 2
    return block[:half], block[half:]


class Scatter:
    def __init__(self, blocks):
        self.blocks = blocks
        self.half = blocks[1].shape[0]

    def diagonal(self):
        self.first = (send("x", self.blocks[2]), send("y", self.blocks[3]))

    def direct(self):
        self.middle = (send("x", self.blocks[1]), send("y", self.blocks[4]))

    def sums(self):
        half, kept, (d_top, d_low) = self.half, self.blocks[0], self.first
        x_low, y_top = kept[2 * half : 3 * half], kept[3 * half :]
        self.last = (
            send("x", (x_low.astype(F32) + d_low.astype(F32)).astype(BF)),
            send("y", (y_top.astype(F32) + d_top.astype(F32)).astype(BF)),
        )

    def result(self):
        half, kept = self.half, self.blocks[0]
        (x_top, y_low), (x_low, y_top) = self.middle, self.last
        top = kept[:half].astype(F32) + x_top.astype(F32) + y_top.astype(F32)
        low = kept[half : 2 * half].astype(F32) + y_low.astype(F32) + x_low.astype(F32)
        return jnp.concatenate([top, low], 0)


class Ring:
    def __init__(self, value, parts=1):
        self.value, self.step, self.parts = value, 0, parts
        self.size, self.me = lax.axis_size("tp"), lax.axis_index("tp")
        self.rows = value.shape[0] // (parts * self.size)
        self.whole = jnp.zeros_like(value)
        self.sent = [self.block(part, self.me - 1) for part in range(parts)]
        self.going = [around(sent) for sent in self.sent]

    def start(self, part, index):
        return (part * self.size + (index + self.size) % self.size) * self.rows

    def block(self, part, index):
        return lax.dynamic_slice_in_dim(self.value, self.start(part, index), self.rows, 0)

    def go(self):
        self.step += 1
        for part in range(self.parts):
            going = self.going[part]
            if self.parts > 1:
                going, _ = tied(going, self.sent[1 - part])
            if self.step < self.size:
                own = self.block(part, self.me - 1 - self.step)
                going = (going.astype(F32) + own.astype(F32)).astype(BF)
            if self.step >= self.size - 1:
                at = self.start(part, self.me - self.step + self.size - 1)
                self.whole = lax.dynamic_update_slice_in_dim(self.whole, going, at, 0)
            if self.step < 2 * self.size - 2:
                self.sent[part] = going
                self.going[part] = around(going)

    def finish(self):
        while self.step < 2 * self.size - 2:
            self.go()
        return self.whole


VMEM_BYTES = 56 * 2**20


def kernel_params():
    return pltpu.CompilerParams(vmem_limit_bytes=VMEM_BYTES)


def cut_of(size):
    return next((cut for cut in (768, 512) if size % cut == 0), size)


def rowwise(fn, rows, vectors, dtypes, sums=0, block=128):
    count, width = rows[0].shape
    n_in, n_out = len(rows) + len(vectors), len(dtypes)

    def kernel(*refs):
        results = fn(*(ref[...] for ref in refs[:n_in]))
        for ref, value in zip(refs[n_in : n_in + n_out], results):
            ref[...] = value.astype(ref.dtype)
        for ref, value in zip(refs[n_in + n_out :], results[n_out:]):
            part = jnp.sum(value.reshape(block // 8, 8, width), 0)

            @pl.when(pl.program_id(0) == 0)
            def _():
                ref[...] = part

            @pl.when(pl.program_id(0) > 0)
            def _():
                ref[...] += part

    by_row = pl.BlockSpec((block, width), lambda i: (i, 0))
    return pl.pallas_call(
        kernel,
        grid=(count // block,),
        in_specs=[by_row] * len(rows) + [pl.BlockSpec((1, width), lambda i: (0, 0))] * len(vectors),
        out_specs=[by_row] * n_out + [pl.BlockSpec((8, width), lambda i: (0, 0))] * sums,
        out_shape=[jax.ShapeDtypeStruct((count, width), dtype) for dtype in dtypes]
        + [jax.ShapeDtypeStruct((8, width), F32)] * sums,
        compiler_params=kernel_params(),
        cost_estimate=pl.CostEstimate(
            flops=20 * count * width, bytes_accessed=4 * count * width * n_in, transcendentals=0
        ),
    )(*rows, *vectors)


ROOT = 0.7978845608028654


def gelu_parts(z):
    bend = jnp.tanh(ROOT * (z + 0.044715 * (z * z * z)))
    value = 0.5 * z * (1.0 + bend)
    slope = 0.5 * (1.0 + bend) + 0.5 * z * (1.0 - bend * bend) * (
        ROOT * (1.0 + (3.0 * 0.044715) * (z * z))
    )
    return value, slope


def ffn_hidden(x, weights):
    count, width = x.shape
    units = weights.shape[1] // 3
    cut = cut_of(units)

    def kernel(x_ref, gate_w, up_w, gate_ref, up_ref, hidden_ref):
        gate = plain_dot(x_ref[...], gate_w[...])
        up = plain_dot(x_ref[...], up_w[...])
        gate_ref[...] = gate
        up_ref[...] = up
        hidden_ref[...] = (gelu_parts(gate)[0] * up).astype(BF)

    out = pl.BlockSpec((count, cut), lambda j: (0, j))
    return pl.pallas_call(
        kernel,
        grid=(units // cut,),
        in_specs=[
            pl.BlockSpec((count, width), lambda j: (0, 0)),
            pl.BlockSpec((width, cut), lambda j: (0, j)),
            pl.BlockSpec((width, cut), lambda j: (0, j + units // cut)),
        ],
        out_specs=[out] * 3,
        out_shape=[
            jax.ShapeDtypeStruct((count, units), F32),
            jax.ShapeDtypeStruct((count, units), F32),
            jax.ShapeDtypeStruct((count, units), BF),
        ],
        compiler_params=kernel_params(),
        cost_estimate=pl.CostEstimate(
            flops=4 * count * width * units,
            bytes_accessed=4 * width * units + 10 * count * units,
            transcendentals=count * units,
        ),
    )(x, weights, weights)


def ffn_down(hidden, weights):
    count, units = hidden.shape
    width = weights.shape[0]
    cut = cut_of(width)

    def kernel(x_ref, w_ref, out_ref):
        out_ref[...] = right_dot(x_ref[...], w_ref[...]).astype(BF)

    return pl.pallas_call(
        kernel,
        grid=(width // cut,),
        in_specs=[
            pl.BlockSpec((count, units), lambda j: (0, 0)),
            pl.BlockSpec((cut, units), lambda j: (j, 2)),
        ],
        out_specs=pl.BlockSpec((count, cut), lambda j: (0, j)),
        out_shape=jax.ShapeDtypeStruct((count, width), BF),
        compiler_params=kernel_params(),
        cost_estimate=pl.CostEstimate(
            flops=2 * count * width * units, bytes_accessed=2 * width * units, transcendentals=0
        ),
    )(hidden, weights)


def ffn_hidden_back(dffn, weights, gate, up):
    count, width = dffn.shape
    units = gate.shape[1]
    cut = cut_of(units)

    def kernel(d_ref, w_ref, gate_ref, up_ref, dgate_ref, dup_ref):
        dhidden = plain_dot(d_ref[...], w_ref[...])
        value, slope = gelu_parts(gate_ref[...])
        dgate_ref[...] = (dhidden * up_ref[...] * slope).astype(BF)
        dup_ref[...] = (dhidden * value).astype(BF)

    out = pl.BlockSpec((count, cut), lambda j: (0, j))
    return pl.pallas_call(
        kernel,
        grid=(units // cut,),
        in_specs=[
            pl.BlockSpec((count, width), lambda j: (0, 0)),
            pl.BlockSpec((width, cut), lambda j: (0, j + 2 * (units // cut))),
            out,
            out,
        ],
        out_specs=[out] * 2,
        out_shape=[jax.ShapeDtypeStruct((count, units), BF)] * 2,
        compiler_params=kernel_params(),
        cost_estimate=pl.CostEstimate(
            flops=2 * count * width * units,
            bytes_accessed=2 * width * units + 12 * count * units,
            transcendentals=count * units,
        ),
    )(dffn, weights, gate, up)


def ffn_input_back(dgate, dup, weights):
    count, units = dgate.shape
    width = weights.shape[0]
    cut = cut_of(width)

    def kernel(dgate_ref, dup_ref, gate_w, up_w, out_ref):
        out_ref[...] = (
            right_dot(dgate_ref[...], gate_w[...]) + right_dot(dup_ref[...], up_w[...])
        ).astype(BF)

    whole = pl.BlockSpec((count, units), lambda j: (0, 0))
    return pl.pallas_call(
        kernel,
        grid=(width // cut,),
        in_specs=[
            whole,
            whole,
            pl.BlockSpec((cut, units), lambda j: (j, 0)),
            pl.BlockSpec((cut, units), lambda j: (j, 1)),
        ],
        out_specs=pl.BlockSpec((count, cut), lambda j: (0, j)),
        out_shape=jax.ShapeDtypeStruct((count, width), BF),
        compiler_params=kernel_params(),
        cost_estimate=pl.CostEstimate(
            flops=4 * count * width * units, bytes_accessed=4 * width * units, transcendentals=0
        ),
    )(dgate, dup, weights, weights)


def weight_grad(rows, rows_far, cols, cols_far):
    count, half_width = rows_far.shape
    width = cols.shape[1]
    cut = cut_of(width)
    half = half_width // 8
    place = jnp.stack([lax.axis_index("fsdp"), lax.axis_index("ctx")]).astype(jnp.int32)

    def kernel(
        place_ref, near_ref, far_ref, cols_ref, cols_far_ref, *rest
    ):
        outs, (near_t, far_t, total) = rest[:5], rest[5:]

        @pl.when(pl.program_id(0) == 0)
        def _():
            near_t[...] = near_ref[...].T
            far_t[...] = far_ref[...].T

        total[...] = plain_dot(near_t[...], cols_ref[...]) + plain_dot(
            far_t[...], cols_far_ref[...]
        )
        for index, (k, low) in enumerate(ORDER):
            start = (lax.bitwise_xor(place_ref[1], k) * 2 + low) * half
            block = total[pl.ds(pl.multiple_of(start, 16), half), :].astype(BF)
            out, at = (outs[0], index) if index < 4 else (outs[index - 3], 0)
            out[at * half : (at + 1) * half, :] = block

    by_cut = pl.BlockSpec((count, cut), lambda j, place: (0, j))
    sizes = (4 * half,) + (half,) * 4
    return pl.pallas_call(
        kernel,
        grid_spec=pltpu.PrefetchScalarGridSpec(
            num_scalar_prefetch=1,
            grid=(width // cut,),
            in_specs=[
                pl.BlockSpec((count, half_width), lambda j, place: (0, place[0])),
                pl.BlockSpec((count, half_width), lambda j, place: (0, 0)),
                by_cut,
                by_cut,
            ],
            out_specs=[pl.BlockSpec((size, cut), lambda j, place: (0, j)) for size in sizes],
            scratch_shapes=[
                pltpu.VMEM((half_width, count), BF),
                pltpu.VMEM((half_width, count), BF),
                pltpu.VMEM((half_width, cut), F32),
            ],
        ),
        out_shape=[jax.ShapeDtypeStruct((size, width), BF) for size in sizes],
        compiler_params=kernel_params(),
        cost_estimate=pl.CostEstimate(
            flops=4 * count * half_width * width,
            bytes_accessed=2 * half_width * width + 4 * count * (width + half_width),
            transcendentals=0,
        ),
    )(place, rows, rows_far, cols, cols_far)


def residual_rows(attn, hidden, scale_two, scale_three):
    attn, hidden = attn.astype(F32), hidden.astype(F32)
    after = hidden + normalize(attn)[0] * scale_two
    return after, normalize(after)[0] * scale_three


def output_rows(ffn_out, after, cot, scale_four):
    normed, factor = normalize(ffn_out.astype(F32))
    cot = cot.astype(F32)
    return (
        after + normed * scale_four,
        norm_back(cot * scale_four, normed, factor),
        cot * normed,
    )


def residual_back_rows(dffn_in, after, attn, cot, scale_three, scale_two):
    dffn_in = dffn_in.astype(F32)
    normed, factor = normalize(after)
    dafter = cot.astype(F32) + norm_back(dffn_in * scale_three, normed, factor)
    normed_two, factor_two = normalize(attn.astype(F32))
    dattn = norm_back(dafter * scale_two, normed_two, factor_two)
    return dafter, dattn, dffn_in * normed, dafter * normed_two


def plane_body(
    hidden_in,
    lengths,
    query_weight,
    key_weight,
    value_weight,
    w_out,
    w_gate,
    w_up,
    w_down,
    gain_attn_in,
    gain_attn_out,
    gain_ffn_in,
    gain_ffn_out,
    cotangent,
):
    seqs_here, tok_here, width = hidden_in.shape
    row_count = seqs_here * tok_here
    head_groups = QUERY_HEADS // KEY_VALUE_HEADS
    half_width = width // 2
    q_cols, kv_cols = query_weight.shape[1], key_weight.shape[1]
    size = lax.axis_size("tp")
    kv_local = kv_cols // HEAD_SIZE
    planes, me = lax.axis_size("ctx"), lax.axis_index("ctx")

    core = lax.axis_index("fsdp")

    def gather(shard):
        return lax.all_gather(shard, ("fsdp", "ctx"), axis=0, tiled=True)

    def far_half(rows):
        return send("core", lax.dynamic_slice_in_dim(rows, (1 - core) * half_width, half_width, 1))

    attention_shards = jnp.concatenate([query_weight, key_weight, value_weight, w_out.T], 1)
    attention_w = gather(attention_shards)
    ffn_shards = jnp.concatenate([w_gate, w_up, w_down.T], 1)
    gains = jnp.stack([gain_attn_in, gain_attn_out, gain_ffn_in, gain_ffn_out])[None]
    gains = jnp.broadcast_to(gains, (2 * planes,) + gains.shape[1:])
    gains = lax.all_to_all(gains, ("fsdp", "ctx"), 0, 0, tiled=True)
    gains = gains.transpose(1, 0, 2).reshape(4, width).astype(F32)
    scale_one, scale_two, scale_three, scale_four = (1.0 + gains[i][None] for i in range(4))
    flat_in = hidden_in.astype(F32).reshape(row_count, width)
    normed_one, factor_one = normalize(flat_in)
    attention_input = (normed_one * scale_one).astype(BF)

    attention_w, attention_input, ffn_shards = tied(attention_w, attention_input, ffn_shards)
    ffn_w = gather(ffn_shards)
    qkv_cols = q_cols + 2 * kv_cols
    qkv_w, out_w = attention_w[:, :qkv_cols], attention_w[:, qkv_cols:]
    run = jnp.arange(tok_here, dtype=jnp.int32)
    query_pos = me * tok_here + run
    key_pos = jnp.concatenate([(me ^ k) * tok_here + run for k in range(planes)])
    valid = query_pos[None, :] < lengths[:, None]
    allowed = (
        (key_pos[None, None, :] <= query_pos[None, :, None])
        & (key_pos[None, None, :] < lengths[:, None, None])
    )[:, None, None]
    qkv = plain_dot(attention_input, qkv_w).astype(BF)
    query_b = qkv[:, :q_cols]
    kv = qkv[:, q_cols:].reshape(seqs_here, tok_here, 2 * kv_cols)
    kv_all = jnp.concatenate([kv, send("x", kv), send("y", kv), send("diagonal", kv)], 1)
    query_five = query_b.reshape(seqs_here, tok_here, kv_local, head_groups, HEAD_SIZE)
    key_four = kv_all[:, :, :kv_cols].reshape(seqs_here, SEQUENCE_SLOTS, kv_local, HEAD_SIZE)
    value_four = kv_all[:, :, kv_cols:].reshape(seqs_here, SEQUENCE_SLOTS, kv_local, HEAD_SIZE)
    raw = jnp.einsum("stkgd,sukd->skgtu", query_five, key_four, preferred_element_type=F32) * QSCALE
    bent = jnp.tanh(raw / CAP)
    masked = jnp.where(allowed, CAP * bent, NEG)
    largest = jnp.max(masked, -1, keepdims=True)
    logsum = largest + jnp.log(jnp.sum(jnp.exp(masked - largest), -1, keepdims=True))
    probs = jnp.exp(masked - logsum)
    probs_b = probs.astype(BF)
    attended = (
        jnp.einsum("skgtu,sukd->stkgd", probs_b, value_four, preferred_element_type=F32)
        .astype(BF)
        .reshape(row_count, -1)
    )
    attn = right_dot(attended, out_w).astype(BF)
    ring = Ring(attn, 2)
    for _ in range(2 * size - 3):
        ring.go()
    attn = ring.finish()
    hidden_rows = hidden_in.reshape(row_count, width)
    after_attn, ffn_in = rowwise(
        residual_rows, [attn, hidden_rows], [scale_two, scale_three], [F32, BF]
    )
    gate, upward, hidden_b = ffn_hidden(ffn_in, ffn_w)
    ffn_out = ffn_down(hidden_b, ffn_w)
    ffn_out, hidden_b, attended, ffn_in, attention_input, cotangent = tied(
        ffn_out, hidden_b, attended, ffn_in, attention_input, cotangent
    )
    ring = Ring(ffn_out, 2)

    hidden_far, attended_far = send("core", hidden_b), send("core", attended)
    ffn_in_far, attention_input_far = far_half(ffn_in), far_half(attention_input)
    cot = jnp.where(
        valid.reshape(row_count, 1), cotangent.reshape(row_count, width), jnp.zeros((), BF)
    )
    ring.go()
    ring.going, hidden_far, attended_far, ffn_in_far, attention_input_far, cot = tied(
        ring.going, hidden_far, attended_far, ffn_in_far, attention_input_far, cot
    )
    ffn_out = ring.finish()
    output, dffn_b, gain_four_rows = rowwise(
        output_rows, [ffn_out, after_attn, cot], [scale_four], [BF, BF], 1
    )
    dgate_b, dup_b = ffn_hidden_back(dffn_b, ffn_w, gate, upward)
    dffn_in = ffn_input_back(dgate_b, dup_b, ffn_w)
    dffn_far = far_half(dffn_b)

    dffn_in, dffn_far, dgate_b, dup_b = tied(dffn_in, dffn_far, dgate_b, dup_b)
    ring = Ring(dffn_in)
    dgate_far = send("core", dgate_b)
    down_s = Scatter(weight_grad(dffn_b, dffn_far, hidden_b, hidden_far))
    ring.going, down_s.blocks, dgate_far = tied(ring.going, down_s.blocks, dgate_far)
    ring.go()
    down_s.diagonal()
    dup_far = send("core", dup_b)
    gate_s = Scatter(weight_grad(ffn_in, ffn_in_far, dgate_b, dgate_far))
    ring.going, gate_s.blocks, dup_far, down_s.first = tied(
        ring.going, gate_s.blocks, dup_far, down_s.first
    )
    ring.go()
    down_s.direct()
    up_s = Scatter(weight_grad(ffn_in, ffn_in_far, dup_b, dup_far))
    ring.going, up_s.blocks, down_s.middle = tied(ring.going, up_s.blocks, down_s.middle)
    ring.go()
    down_s.sums()
    ring.going, down_s.last, gate_s.blocks = tied(ring.going, down_s.last, gate_s.blocks)
    ring.go()
    gate_s.diagonal()
    grad_down = down_s.result().T
    ring.going, gate_s.first, grad_down = tied(ring.going, gate_s.first, grad_down)
    ring.go()
    gate_s.direct()
    dffn_in, up_s.blocks, gate_s.first = tied(ring.finish(), up_s.blocks, gate_s.first)
    gate_s.sums()
    dafter, dattn_b, gain_three_rows, gain_two_rows = rowwise(
        residual_back_rows,
        [dffn_in, after_attn, attn, cot],
        [scale_three, scale_two],
        [F32, BF],
        2,
    )
    dattended = plain_dot(dattn_b, out_w).astype(BF).reshape(query_five.shape)
    dattended, gate_s.middle = tied(dattended, gate_s.middle)
    dprobs = jnp.einsum("stkgd,sukd->skgtu", dattended, value_four, preferred_element_type=F32)
    weighted = jnp.sum(probs * dprobs, -1, keepdims=True)
    draw_b = (probs * (dprobs - weighted) * (1.0 - bent * bent)).astype(BF)
    draw_b, gate_s.last, up_s.blocks = tied(draw_b, gate_s.last, up_s.blocks)
    up_s.diagonal()
    dvalue_part = jnp.einsum("skgtu,stkgd->sukd", probs_b, dattended, preferred_element_type=F32)
    dkey_part = (
        jnp.einsum("skgtu,stkgd->sukd", draw_b, query_five, preferred_element_type=F32) * QSCALE
    )
    dkv = [
        jnp.concatenate(
            [
                part[:, k * tok_here : (k + 1) * tok_here].astype(BF).reshape(row_count, kv_cols)
                for part in (dkey_part, dvalue_part)
            ],
            1,
        )
        for k in range(planes)
    ]
    dattn_far = far_half(dattn_b)
    dkv, dattn_far, up_s.first = tied(dkv, dattn_far, up_s.first)
    dkv = [dkv[0], send("x", dkv[1]), send("y", dkv[2]), send("diagonal", dkv[3])]
    out_s = Scatter(weight_grad(dattn_b, dattn_far, attended, attended_far))
    dquery_b = (
        (jnp.einsum("skgtu,sukd->stkgd", draw_b, key_four, preferred_element_type=F32) * QSCALE)
        .astype(BF)
        .reshape(row_count, -1)
    )
    grad_gate = gate_s.result()
    dkv, dquery_b, out_s.blocks, grad_gate, up_s.blocks = tied(
        dkv, dquery_b, out_s.blocks, grad_gate, up_s.blocks
    )
    dkv_b = sum(part.astype(F32) for part in dkv).astype(BF)
    dqkv_b = jnp.concatenate([dquery_b, dkv_b], 1)
    dattn_in = right_dot(dqkv_b, qkv_w)
    dattn_in, dqkv_b, dafter, up_s.blocks = tied(
        dattn_in.astype(BF), dqkv_b, dafter, up_s.blocks
    )

    ring = Ring(dattn_in)
    dqkv_far = send("core", dqkv_b)
    up_s.direct()
    qkv_s = Scatter(weight_grad(attention_input, attention_input_far, dqkv_b, dqkv_far))
    ring.going, qkv_s.blocks, up_s.middle = tied(ring.going, qkv_s.blocks, up_s.middle)
    ring.go()
    up_s.sums()
    grad_gain_one = jnp.sum(dattn_in.astype(F32) * normed_one, 0)
    grad_gains = jnp.stack(
        [grad_gain_one]
        + [jnp.sum(rows, 0) / size for rows in (gain_two_rows, gain_three_rows, gain_four_rows)]
    )
    grad_gains = grad_gains.reshape(4, 2 * planes, 1, -1).transpose(1, 2, 0, 3)
    grad_gains = jnp.broadcast_to(grad_gains, (2 * planes, size) + grad_gains.shape[2:])
    grad_gains = grad_gains.reshape((-1,) + grad_gains.shape[2:])
    ring.going, grad_gains, up_s.last = tied(ring.going, grad_gains, up_s.last)
    ring.go()
    grad_gains = lax.all_to_all(grad_gains, ("fsdp", "ctx", "tp"), 0, 0, tiled=True)
    qkv_s.diagonal()
    qkv_s.direct()
    grad_up = up_s.result()
    ring.going, qkv_s.first, qkv_s.middle, grad_up = tied(
        ring.going, qkv_s.first, qkv_s.middle, grad_up
    )
    ring.go()
    qkv_s.sums()
    out_s.diagonal()
    ring.going, qkv_s.last, out_s.first = tied(ring.going, qkv_s.last, out_s.first)
    ring.go()
    out_s.direct()
    out_s.sums()
    grad_qkv = qkv_s.result()
    ring.going, out_s.middle, out_s.last, grad_qkv = tied(
        ring.going, out_s.middle, out_s.last, grad_qkv
    )
    ring.go()
    grad_out = out_s.result().T
    ring.going, grad_out = tied(ring.going, grad_out)
    dattn_in, grad_gains = tied(ring.finish(), grad_gains)
    grad_gains = jnp.sum(grad_gains, 0)
    dattn_in = dattn_in.astype(F32)
    grad_input = dafter + norm_back(dattn_in * scale_one, normed_one, factor_one)
    grad_input = grad_input.astype(BF)
    return (
        output.reshape(hidden_in.shape),
        grad_input.reshape(hidden_in.shape),
        grad_qkv[:, :q_cols],
        grad_qkv[:, q_cols : q_cols + kv_cols],
        grad_qkv[:, q_cols + kv_cols :],
        grad_out,
        grad_gate,
        grad_up,
        grad_down,
        grad_gains[0],
        grad_gains[1],
        grad_gains[2],
        grad_gains[3],
    )


def general_body(
    hidden_in,
    lengths,
    query_weight,
    key_weight,
    value_weight,
    w_out,
    w_gate,
    w_up,
    w_down,
    gain_attn_in,
    gain_attn_out,
    gain_ffn_in,
    gain_ffn_out,
    cotangent,
):
    seqs_here, tok_here, width = hidden_in.shape
    row_count = seqs_here * tok_here
    head_groups = QUERY_HEADS // KEY_VALUE_HEADS
    gathered = (
        lax.all_gather(query_weight, ("fsdp", "ctx"), axis=0, tiled=True),
        lax.all_gather(key_weight, ("fsdp", "ctx"), axis=0, tiled=True),
        lax.all_gather(value_weight, ("fsdp", "ctx"), axis=0, tiled=True),
        lax.all_gather(w_out, ("fsdp", "ctx"), axis=1, tiled=True),
        lax.all_gather(w_gate, ("fsdp", "ctx"), axis=0, tiled=True),
        lax.all_gather(w_up, ("fsdp", "ctx"), axis=0, tiled=True),
        lax.all_gather(w_down, ("fsdp", "ctx"), axis=1, tiled=True),
        lax.all_gather(gain_attn_in, ("fsdp", "ctx"), axis=0, tiled=True),
        lax.all_gather(gain_attn_out, ("fsdp", "ctx"), axis=0, tiled=True),
        lax.all_gather(gain_ffn_in, ("fsdp", "ctx"), axis=0, tiled=True),
        lax.all_gather(gain_ffn_out, ("fsdp", "ctx"), axis=0, tiled=True),
    )
    query_full, key_full, value_full, out_full, gate_full, up_full, down_full = gathered[:7]
    scale_one = 1.0 + gathered[7].astype(jnp.float32)
    scale_two = 1.0 + gathered[8].astype(jnp.float32)
    scale_three = 1.0 + gathered[9].astype(jnp.float32)
    scale_four = 1.0 + gathered[10].astype(jnp.float32)
    kv_local = key_full.shape[1] // HEAD_SIZE
    own_start = lax.axis_index("ctx") * tok_here
    query_pos = own_start + jnp.arange(tok_here, dtype=jnp.int32)
    key_pos = jnp.arange(SEQUENCE_SLOTS, dtype=jnp.int32)
    valid = query_pos[None, :] < lengths[:, None]
    allowed = (
        (key_pos[None, None, :] <= query_pos[None, :, None])
        & (key_pos[None, None, :] < lengths[:, None, None])
    )[:, None, None]
    flat_in = hidden_in.astype(jnp.float32).reshape(row_count, width)
    normed_one, factor_one = normalize(flat_in)
    attention_input = (normed_one * scale_one).astype(jnp.bfloat16)
    query_b = plain_dot(attention_input, query_full).astype(jnp.bfloat16)
    key_b = (
        plain_dot(attention_input, key_full)
        .astype(jnp.bfloat16)
        .reshape(seqs_here, tok_here, kv_local * HEAD_SIZE)
    )
    value_b = (
        plain_dot(attention_input, value_full)
        .astype(jnp.bfloat16)
        .reshape(seqs_here, tok_here, kv_local * HEAD_SIZE)
    )
    key_all, value_all = (
        lax.all_gather(key_b, "ctx", axis=1, tiled=True),
        lax.all_gather(value_b, "ctx", axis=1, tiled=True),
    )
    query_five = query_b.reshape(seqs_here, tok_here, kv_local, head_groups, HEAD_SIZE)
    key_four = key_all.reshape(seqs_here, SEQUENCE_SLOTS, kv_local, HEAD_SIZE)
    value_four = value_all.reshape(seqs_here, SEQUENCE_SLOTS, kv_local, HEAD_SIZE)
    raw = (
        jnp.einsum("stkgd,sukd->skgtu", query_five, key_four, preferred_element_type=jnp.float32)
        * QSCALE
    )
    bent = jnp.tanh(raw / CAP)
    masked = jnp.where(allowed, CAP * bent, NEG)
    largest = jnp.max(masked, -1, keepdims=True)
    logsum = largest + jnp.log(jnp.sum(jnp.exp(masked - largest), -1, keepdims=True))
    probs = jnp.exp(masked - logsum)
    probs_b = probs.astype(jnp.bfloat16)
    attended = (
        jnp.einsum("skgtu,sukd->stkgd", probs_b, value_four, preferred_element_type=jnp.float32)
        .astype(jnp.bfloat16)
        .reshape(row_count, -1)
    )
    attn = lax.psum(plain_dot(attended, out_full).astype(jnp.bfloat16), "tp").astype(jnp.float32)
    normed_two, factor_two = normalize(attn)
    after_attn = flat_in + normed_two * scale_two
    normed_three, factor_three = normalize(after_attn)
    ffn_in = (normed_three * scale_three).astype(jnp.bfloat16)
    gate = plain_dot(ffn_in, gate_full)
    upward = plain_dot(ffn_in, up_full)
    activated, gelu_pull = jax.vjp(gelu_tanh, gate)
    hidden_b = (activated * upward).astype(jnp.bfloat16)
    ffn_out = lax.psum(plain_dot(hidden_b, down_full).astype(jnp.bfloat16), "tp").astype(
        jnp.float32
    )
    normed_four, factor_four = normalize(ffn_out)
    result = after_attn + normed_four * scale_four
    cot = cotangent.astype(jnp.float32).reshape(row_count, width) * valid.reshape(
        row_count, 1
    ).astype(jnp.float32)
    query_back, key_back, value_back, out_back, gate_back, up_back, down_back = (
        lax.all_gather(query_weight, ("fsdp", "ctx"), axis=0, tiled=True),
        lax.all_gather(key_weight, ("fsdp", "ctx"), axis=0, tiled=True),
        lax.all_gather(value_weight, ("fsdp", "ctx"), axis=0, tiled=True),
        lax.all_gather(w_out, ("fsdp", "ctx"), axis=1, tiled=True),
        lax.all_gather(w_gate, ("fsdp", "ctx"), axis=0, tiled=True),
        lax.all_gather(w_up, ("fsdp", "ctx"), axis=0, tiled=True),
        lax.all_gather(w_down, ("fsdp", "ctx"), axis=1, tiled=True),
    )
    grad_gain_four = jnp.sum(cot * normed_four, 0)
    dffn_b = norm_back(cot * scale_four, normed_four, factor_four).astype(jnp.bfloat16)
    grad_down = left_dot(hidden_b, dffn_b)
    dhidden = right_dot(dffn_b, down_back)
    dgate_b = gelu_pull(dhidden * upward)[0].astype(jnp.bfloat16)
    dup_b = (dhidden * activated).astype(jnp.bfloat16)
    grad_gate = left_dot(ffn_in, dgate_b)
    grad_up = left_dot(ffn_in, dup_b)
    dffn_in = lax.psum(
        (right_dot(dgate_b, gate_back) + right_dot(dup_b, up_back)).astype(jnp.bfloat16), "tp"
    ).astype(jnp.float32)
    grad_gain_three = jnp.sum(dffn_in * normed_three, 0)
    dafter = cot + norm_back(dffn_in * scale_three, normed_three, factor_three)
    grad_gain_two = jnp.sum(dafter * normed_two, 0)
    dattn_b = norm_back(dafter * scale_two, normed_two, factor_two).astype(jnp.bfloat16)
    grad_out = left_dot(attended, dattn_b)
    dattended = right_dot(dattn_b, out_back).astype(jnp.bfloat16).reshape(query_five.shape)
    dprobs = jnp.einsum(
        "stkgd,sukd->skgtu", dattended, value_four, preferred_element_type=jnp.float32
    )
    weighted = jnp.sum(probs * dprobs, -1, keepdims=True)
    draw_b = (probs * (dprobs - weighted) * (1.0 - bent * bent)).astype(jnp.bfloat16)
    dquery_b = (
        (
            jnp.einsum("skgtu,sukd->stkgd", draw_b, key_four, preferred_element_type=jnp.float32)
            * QSCALE
        )
        .astype(jnp.bfloat16)
        .reshape(row_count, -1)
    )
    dvalue_part = jnp.einsum(
        "skgtu,stkgd->sukd", probs_b, dattended, preferred_element_type=jnp.float32
    )
    dkey_part = (
        jnp.einsum("skgtu,stkgd->sukd", draw_b, query_five, preferred_element_type=jnp.float32)
        * QSCALE
    )
    dkey, dvalue = (
        lax.psum_scatter(
            dkey_part.astype(jnp.bfloat16), "ctx", scatter_dimension=1, tiled=True
        ).astype(jnp.float32),
        lax.psum_scatter(
            dvalue_part.astype(jnp.bfloat16), "ctx", scatter_dimension=1, tiled=True
        ).astype(jnp.float32),
    )
    dkey_b = dkey.astype(jnp.bfloat16).reshape(row_count, -1)
    dvalue_b = dvalue.astype(jnp.bfloat16).reshape(row_count, -1)
    grad_query = left_dot(attention_input, dquery_b)
    grad_key = left_dot(attention_input, dkey_b)
    grad_value = left_dot(attention_input, dvalue_b)
    dattn_in = lax.psum(
        (
            right_dot(dquery_b, query_back)
            + right_dot(dkey_b, key_back)
            + right_dot(dvalue_b, value_back)
        ).astype(jnp.bfloat16),
        "tp",
    ).astype(jnp.float32)
    grad_gain_one = jnp.sum(dattn_in * normed_one, 0)
    grad_input = dafter + norm_back(dattn_in * scale_one, normed_one, factor_one)
    summed = (
        lax.psum_scatter(
            grad_query.astype(jnp.bfloat16), ("fsdp", "ctx"), scatter_dimension=0, tiled=True
        ).astype(jnp.float32),
        lax.psum_scatter(
            grad_key.astype(jnp.bfloat16), ("fsdp", "ctx"), scatter_dimension=0, tiled=True
        ).astype(jnp.float32),
        lax.psum_scatter(
            grad_value.astype(jnp.bfloat16), ("fsdp", "ctx"), scatter_dimension=0, tiled=True
        ).astype(jnp.float32),
        lax.psum_scatter(
            grad_out.astype(jnp.bfloat16), ("fsdp", "ctx"), scatter_dimension=1, tiled=True
        ).astype(jnp.float32),
        lax.psum_scatter(
            grad_gate.astype(jnp.bfloat16), ("fsdp", "ctx"), scatter_dimension=0, tiled=True
        ).astype(jnp.float32),
        lax.psum_scatter(
            grad_up.astype(jnp.bfloat16), ("fsdp", "ctx"), scatter_dimension=0, tiled=True
        ).astype(jnp.float32),
        lax.psum_scatter(
            grad_down.astype(jnp.bfloat16), ("fsdp", "ctx"), scatter_dimension=1, tiled=True
        ).astype(jnp.float32),
        lax.psum_scatter(
            grad_gain_one.astype(jnp.bfloat16), ("fsdp", "ctx"), scatter_dimension=0, tiled=True
        ).astype(jnp.float32),
        lax.psum_scatter(
            grad_gain_two.astype(jnp.bfloat16), ("fsdp", "ctx"), scatter_dimension=0, tiled=True
        ).astype(jnp.float32),
        lax.psum_scatter(
            grad_gain_three.astype(jnp.bfloat16), ("fsdp", "ctx"), scatter_dimension=0, tiled=True
        ).astype(jnp.float32),
        lax.psum_scatter(
            grad_gain_four.astype(jnp.bfloat16), ("fsdp", "ctx"), scatter_dimension=0, tiled=True
        ).astype(jnp.float32),
    )
    return (
        result.astype(jnp.bfloat16).reshape(hidden_in.shape),
        grad_input.astype(jnp.bfloat16).reshape(hidden_in.shape),
        summed[0],
        summed[1],
        summed[2],
        summed[3],
        summed[4],
        summed[5],
        summed[6],
        summed[7],
        summed[8],
        summed[9],
        summed[10],
    )


def solution(mesh):
    square = mesh.shape["ctx"] == 4 and mesh.shape["fsdp"] == 2
    return jax.shard_map(
        plane_body if square else general_body,
        mesh=mesh,
        in_specs=(
            P("fsdp", "ctx", None),
            P("fsdp"),
            P(("fsdp", "ctx"), "tp"),
            P(("fsdp", "ctx"), "tp"),
            P(("fsdp", "ctx"), "tp"),
            P("tp", ("fsdp", "ctx")),
            P(("fsdp", "ctx"), "tp"),
            P(("fsdp", "ctx"), "tp"),
            P("tp", ("fsdp", "ctx")),
            P(("fsdp", "ctx")),
            P(("fsdp", "ctx")),
            P(("fsdp", "ctx")),
            P(("fsdp", "ctx")),
            P("fsdp", "ctx", None),
        ),
        out_specs=(
            P("fsdp", "ctx", None),
            P("fsdp", "ctx", None),
            P(("fsdp", "ctx"), "tp"),
            P(("fsdp", "ctx"), "tp"),
            P(("fsdp", "ctx"), "tp"),
            P("tp", ("fsdp", "ctx")),
            P(("fsdp", "ctx"), "tp"),
            P(("fsdp", "ctx"), "tp"),
            P("tp", ("fsdp", "ctx")),
            P(("fsdp", "ctx")),
            P(("fsdp", "ctx")),
            P(("fsdp", "ctx")),
            P(("fsdp", "ctx")),
        ),
        check_vma=False,
    )
```

```python
import jax
import jax.numpy as jnp
from jax import lax
from jax.experimental import pallas as pl
from jax.experimental.pallas import tpu as pltpu
from jax.sharding import PartitionSpec as P

QUERY_HEADS = 8
KEY_VALUE_HEADS = 4
HEAD_SIZE = 256
SEQUENCE_SLOTS = 2048


EPS = 1e-06
CAP = 50.0
QSCALE = 0.0625
NEG = -1e30


def normalize(value_rows):
    factor = lax.rsqrt(jnp.mean(value_rows * value_rows, -1, keepdims=True) + EPS)
    return (value_rows * factor, factor)


def norm_back(grad_hat, normed, factor):
    return factor * (grad_hat - normed * jnp.mean(grad_hat * normed, -1, keepdims=True))


def plain_dot(first, second):
    return jnp.dot(first, second, preferred_element_type=jnp.float32)


def left_dot(first, second):
    return lax.dot_general(
        first, second, (((0,), (0,)), ((), ())), preferred_element_type=jnp.float32
    )


def right_dot(first, second):
    return lax.dot_general(
        first, second, (((1,), (1,)), ((), ())), preferred_element_type=jnp.float32
    )


def gelu_tanh(value_rows):
    return jax.nn.gelu(value_rows, approximate=True)


BF = jnp.bfloat16
F32 = jnp.float32

LINKS = {
    "x": ("ctx", [(0, 1), (1, 0), (2, 3), (3, 2)]),
    "y": ("ctx", [(0, 2), (2, 0), (1, 3), (3, 1)]),
    "diagonal": ("ctx", [(0, 3), (3, 0), (1, 2), (2, 1)]),
    "core": ("fsdp", [(0, 1), (1, 0)]),
}
ORDER = [(0, 0), (0, 1), (1, 1), (2, 0), (1, 0), (3, 0), (3, 1), (2, 1)]


def tied(*values):
    return lax.optimization_barrier(values)


def send(link, value):
    return lax.ppermute(value, *LINKS[link])


def around(value, by=1):
    size = lax.axis_size("tp")
    return lax.ppermute(value, "tp", [(i, (i + by) % size) for i in range(size)])


def halves(block):
    half = block.shape[0] // 2
    return block[:half], block[half:]


class Scatter:
    def __init__(self, blocks):
        self.blocks = blocks
        self.half = blocks[1].shape[0]

    def diagonal(self):
        self.first = (send("x", self.blocks[2]), send("y", self.blocks[3]))

    def both(self):
        half = self.half = self.blocks[1].shape[0] // 2
        from_x, from_y = send("x", self.blocks[1]), send("y", self.blocks[2])
        self.first, self.middle = (from_x[half:], from_y[:half]), (from_x[:half], from_y[half:])

    def direct(self):
        self.middle = (send("x", self.blocks[1]), send("y", self.blocks[4]))

    def sums(self):
        half, kept, (d_top, d_low) = self.half, self.blocks[0], self.first
        x_low, y_top = kept[2 * half : 3 * half], kept[3 * half :]
        self.last = (
            send("x", (x_low.astype(F32) + d_low.astype(F32)).astype(BF)),
            send("y", (y_top.astype(F32) + d_top.astype(F32)).astype(BF)),
        )

    def result(self):
        half, kept = self.half, self.blocks[0]
        (x_top, y_low), (x_low, y_top) = self.middle, self.last
        top = kept[:half].astype(F32) + x_top.astype(F32) + y_top.astype(F32)
        low = kept[half : 2 * half].astype(F32) + y_low.astype(F32) + x_low.astype(F32)
        return jnp.concatenate([top, low], 0)


class Ring:
    def __init__(self, value, parts=1):
        self.value, self.step, self.parts = value, 0, parts
        self.size, self.me = lax.axis_size("tp"), lax.axis_index("tp")
        self.rows = value.shape[0] // (parts * self.size)
        self.whole = jnp.zeros_like(value)
        self.sent = [self.block(part, self.me - 1) for part in range(parts)]
        self.going = [around(sent) for sent in self.sent]

    def start(self, part, index):
        return (part * self.size + (index + self.size) % self.size) * self.rows

    def block(self, part, index):
        return lax.dynamic_slice_in_dim(self.value, self.start(part, index), self.rows, 0)

    def go(self):
        self.step += 1
        for part in range(self.parts):
            going = self.going[part]
            if self.parts > 1:
                going, _ = tied(going, self.sent[1 - part])
            if self.step < self.size:
                own = self.block(part, self.me - 1 - self.step)
                going = (going.astype(F32) + own.astype(F32)).astype(BF)
            if self.step >= self.size - 1:
                at = self.start(part, self.me - self.step + self.size - 1)
                self.whole = lax.dynamic_update_slice_in_dim(self.whole, going, at, 0)
            if self.step < 2 * self.size - 2:
                self.sent[part] = going
                self.going[part] = around(going)

    def finish(self):
        while self.step < 2 * self.size - 2:
            self.go()
        return self.whole


VMEM_BYTES = 56 * 2**20


def kernel_params():
    return pltpu.CompilerParams(vmem_limit_bytes=VMEM_BYTES)


def cut_of(size):
    return next((cut for cut in (768, 512) if size % cut == 0), size)


def rowwise(fn, rows, vectors, dtypes, sums=0, block=128):
    count, width = rows[0].shape
    n_in, n_out = len(rows) + len(vectors), len(dtypes)

    def kernel(*refs):
        results = fn(*(ref[...] for ref in refs[:n_in]))
        for ref, value in zip(refs[n_in : n_in + n_out], results):
            ref[...] = value.astype(ref.dtype)
        for ref, value in zip(refs[n_in + n_out :], results[n_out:]):
            part = jnp.sum(value.reshape(block // 8, 8, width), 0)

            @pl.when(pl.program_id(0) == 0)
            def _():
                ref[...] = part

            @pl.when(pl.program_id(0) > 0)
            def _():
                ref[...] += part

    by_row = pl.BlockSpec((block, width), lambda i: (i, 0))
    return pl.pallas_call(
        kernel,
        grid=(count // block,),
        in_specs=[by_row] * len(rows) + [pl.BlockSpec((1, width), lambda i: (0, 0))] * len(vectors),
        out_specs=[by_row] * n_out + [pl.BlockSpec((8, width), lambda i: (0, 0))] * sums,
        out_shape=[jax.ShapeDtypeStruct((count, width), dtype) for dtype in dtypes]
        + [jax.ShapeDtypeStruct((8, width), F32)] * sums,
        compiler_params=kernel_params(),
        cost_estimate=pl.CostEstimate(
            flops=20 * count * width, bytes_accessed=4 * count * width * n_in, transcendentals=0
        ),
    )(*rows, *vectors)


ROOT = 0.7978845608028654


def gelu_parts(z):
    bend = jnp.tanh(ROOT * (z + 0.044715 * (z * z * z)))
    value = 0.5 * z * (1.0 + bend)
    slope = 0.5 * (1.0 + bend) + 0.5 * z * (1.0 - bend * bend) * (
        ROOT * (1.0 + (3.0 * 0.044715) * (z * z))
    )
    return value, slope


def ffn_hidden(x, weights):
    count, width = x.shape
    units = weights.shape[1] // 3
    cut = cut_of(units)

    def kernel(x_ref, gate_w, up_w, gate_ref, up_ref, hidden_ref):
        gate = plain_dot(x_ref[...], gate_w[...])
        up = plain_dot(x_ref[...], up_w[...])
        gate_ref[...] = gate
        up_ref[...] = up
        hidden_ref[...] = (gelu_parts(gate)[0] * up).astype(BF)

    out = pl.BlockSpec((count, cut), lambda j: (0, j))
    return pl.pallas_call(
        kernel,
        grid=(units // cut,),
        in_specs=[
            pl.BlockSpec((count, width), lambda j: (0, 0)),
            pl.BlockSpec((width, cut), lambda j: (0, j)),
            pl.BlockSpec((width, cut), lambda j: (0, j + units // cut)),
        ],
        out_specs=[out] * 3,
        out_shape=[
            jax.ShapeDtypeStruct((count, units), F32),
            jax.ShapeDtypeStruct((count, units), F32),
            jax.ShapeDtypeStruct((count, units), BF),
        ],
        compiler_params=kernel_params(),
        cost_estimate=pl.CostEstimate(
            flops=4 * count * width * units,
            bytes_accessed=4 * width * units + 10 * count * units,
            transcendentals=count * units,
        ),
    )(x, weights, weights)


def ffn_down(hidden, weights):
    count, units = hidden.shape
    width = weights.shape[0]
    cut = cut_of(width)

    def kernel(x_ref, w_ref, out_ref):
        out_ref[...] = right_dot(x_ref[...], w_ref[...]).astype(BF)

    return pl.pallas_call(
        kernel,
        grid=(width // cut,),
        in_specs=[
            pl.BlockSpec((count, units), lambda j: (0, 0)),
            pl.BlockSpec((cut, units), lambda j: (j, 2)),
        ],
        out_specs=pl.BlockSpec((count, cut), lambda j: (0, j)),
        out_shape=jax.ShapeDtypeStruct((count, width), BF),
        compiler_params=kernel_params(),
        cost_estimate=pl.CostEstimate(
            flops=2 * count * width * units, bytes_accessed=2 * width * units, transcendentals=0
        ),
    )(hidden, weights)


def ffn_hidden_back(dffn, weights, gate, up):
    count, width = dffn.shape
    units = gate.shape[1]
    cut = cut_of(units)

    def kernel(d_ref, w_ref, gate_ref, up_ref, dgate_ref, dup_ref):
        dhidden = plain_dot(d_ref[...], w_ref[...])
        value, slope = gelu_parts(gate_ref[...])
        dgate_ref[...] = (dhidden * up_ref[...] * slope).astype(BF)
        dup_ref[...] = (dhidden * value).astype(BF)

    out = pl.BlockSpec((count, cut), lambda j: (0, j))
    return pl.pallas_call(
        kernel,
        grid=(units // cut,),
        in_specs=[
            pl.BlockSpec((count, width), lambda j: (0, 0)),
            pl.BlockSpec((width, cut), lambda j: (0, j + 2 * (units // cut))),
            out,
            out,
        ],
        out_specs=[out] * 2,
        out_shape=[jax.ShapeDtypeStruct((count, units), BF)] * 2,
        compiler_params=kernel_params(),
        cost_estimate=pl.CostEstimate(
            flops=2 * count * width * units,
            bytes_accessed=2 * width * units + 12 * count * units,
            transcendentals=count * units,
        ),
    )(dffn, weights, gate, up)


def ffn_input_back(dgate, dup, weights):
    count, units = dgate.shape
    width = weights.shape[0]
    cut = cut_of(width)

    def kernel(dgate_ref, dup_ref, gate_w, up_w, out_ref):
        out_ref[...] = (
            right_dot(dgate_ref[...], gate_w[...]) + right_dot(dup_ref[...], up_w[...])
        ).astype(BF)

    whole = pl.BlockSpec((count, units), lambda j: (0, 0))
    return pl.pallas_call(
        kernel,
        grid=(width // cut,),
        in_specs=[
            whole,
            whole,
            pl.BlockSpec((cut, units), lambda j: (j, 0)),
            pl.BlockSpec((cut, units), lambda j: (j, 1)),
        ],
        out_specs=pl.BlockSpec((count, cut), lambda j: (0, j)),
        out_shape=jax.ShapeDtypeStruct((count, width), BF),
        compiler_params=kernel_params(),
        cost_estimate=pl.CostEstimate(
            flops=4 * count * width * units, bytes_accessed=4 * width * units, transcendentals=0
        ),
    )(dgate, dup, weights, weights)


def weight_grad(rows, rows_far, cols, cols_far, joined=False):
    count, half_width = rows_far.shape
    width = cols.shape[1]
    cut = cut_of(width)
    half = half_width // 8
    place = jnp.stack([lax.axis_index("fsdp"), lax.axis_index("ctx")]).astype(jnp.int32)
    sizes = (4 * half, 2 * half, 2 * half) if joined else (4 * half,) + (half,) * 4

    def kernel(
        place_ref, near_ref, far_ref, cols_ref, cols_far_ref, *rest
    ):
        outs, (near_t, far_t, total) = rest[: len(sizes)], rest[len(sizes) :]

        @pl.when(pl.program_id(0) == 0)
        def _():
            near_t[...] = near_ref[...].T
            far_t[...] = far_ref[...].T

        total[...] = plain_dot(near_t[...], cols_ref[...]) + plain_dot(
            far_t[...], cols_far_ref[...]
        )
        for index, (k, low) in enumerate(ORDER):
            start = (lax.bitwise_xor(place_ref[1], k) * 2 + low) * half
            block = total[pl.ds(pl.multiple_of(start, 16), half), :].astype(BF)
            if index < 4:
                out, at = outs[0], index
            elif joined:
                out, at = outs[1 + (index - 4) // 2], index % 2
            else:
                out, at = outs[index - 3], 0
            out[at * half : (at + 1) * half, :] = block

    by_cut = pl.BlockSpec((count, cut), lambda j, place: (0, j))
    return pl.pallas_call(
        kernel,
        grid_spec=pltpu.PrefetchScalarGridSpec(
            num_scalar_prefetch=1,
            grid=(width // cut,),
            in_specs=[
                pl.BlockSpec((count, half_width), lambda j, place: (0, place[0])),
                pl.BlockSpec((count, half_width), lambda j, place: (0, 0)),
                by_cut,
                by_cut,
            ],
            out_specs=[pl.BlockSpec((size, cut), lambda j, place: (0, j)) for size in sizes],
            scratch_shapes=[
                pltpu.VMEM((half_width, count), BF),
                pltpu.VMEM((half_width, count), BF),
                pltpu.VMEM((half_width, cut), F32),
            ],
        ),
        out_shape=[jax.ShapeDtypeStruct((size, width), BF) for size in sizes],
        compiler_params=kernel_params(),
        cost_estimate=pl.CostEstimate(
            flops=4 * count * half_width * width,
            bytes_accessed=2 * half_width * width + 4 * count * (width + half_width),
            transcendentals=0,
        ),
    )(place, rows, rows_far, cols, cols_far)


def attention_back(query, dattended, attended, kv, logsum, length):
    tokens, columns = query.shape
    heads, blocks = columns // HEAD_SIZE, kv.shape[0] // tokens
    scalars = jnp.stack([lax.axis_index("ctx").astype(jnp.int32), length])

    def kernel(scalars_ref, q_ref, d_ref, a_ref, kv_ref, log_ref, dq_ref, dkv_ref, dq, dk, dv):
        block, head = pl.program_id(0), pl.program_id(1)
        q, d = q_ref[...], d_ref[...]
        key, value = kv_ref[:, :HEAD_SIZE], kv_ref[:, HEAD_SIZE:]
        me = scalars_ref[0]
        bent = jnp.tanh(right_dot(q, key) * (QSCALE / CAP))
        shape = (tokens, tokens)
        key_pos = lax.bitwise_xor(me, block) * tokens + lax.broadcasted_iota(jnp.int32, shape, 1)
        query_pos = me * tokens + lax.broadcasted_iota(jnp.int32, shape, 0)
        allowed = (key_pos <= query_pos) & (key_pos < scalars_ref[1])
        probs = jnp.where(allowed, jnp.exp(CAP * bent - log_ref[...]), 0.0)
        weighted = jnp.sum(d.astype(F32) * a_ref[...].astype(F32), -1, keepdims=True)
        draw = (probs * (right_dot(d, value) - weighted) * (1.0 - bent * bent)).astype(BF)
        dk_part, dv_part = left_dot(draw, q), left_dot(probs.astype(BF), d)
        dq_part = plain_dot(draw, key)

        @pl.when(head == 0)
        def _():
            dk[...] = dk_part
            dv[...] = dv_part

        @pl.when(head > 0)
        def _():
            dk[...] += dk_part
            dv[...] += dv_part

        @pl.when(block == 0)
        def _():
            dq[head] = dq_part

        @pl.when(block > 0)
        def _():
            dq[head] += dq_part

        @pl.when(head == heads - 1)
        def _():
            dkv_ref[:, :HEAD_SIZE] = (dk[...] * QSCALE).astype(BF)
            dkv_ref[:, HEAD_SIZE:] = dv[...].astype(BF)

        @pl.when((block == blocks - 1) & (head == heads - 1))
        def _():
            for i in range(heads):
                dq_ref[:, i * HEAD_SIZE : (i + 1) * HEAD_SIZE] = (dq[i] * QSCALE).astype(BF)

    by_head = pl.BlockSpec((tokens, HEAD_SIZE), lambda b, h, scalars: (0, h))
    return pl.pallas_call(
        kernel,
        grid_spec=pltpu.PrefetchScalarGridSpec(
            num_scalar_prefetch=1,
            grid=(blocks, heads),
            in_specs=[
                by_head,
                by_head,
                by_head,
                pl.BlockSpec((tokens, 2 * HEAD_SIZE), lambda b, h, scalars: (b, 0)),
                pl.BlockSpec((None, tokens, 1), lambda b, h, scalars: (h, 0, 0)),
            ],
            out_specs=[
                pl.BlockSpec((tokens, columns), lambda b, h, scalars: (0, 0)),
                pl.BlockSpec((None, tokens, 2 * HEAD_SIZE), lambda b, h, scalars: (b, 0, 0)),
            ],
            scratch_shapes=[
                pltpu.VMEM((heads, tokens, HEAD_SIZE), F32),
                pltpu.VMEM((tokens, HEAD_SIZE), F32),
                pltpu.VMEM((tokens, HEAD_SIZE), F32),
            ],
        ),
        out_shape=[
            jax.ShapeDtypeStruct((tokens, columns), BF),
            jax.ShapeDtypeStruct((blocks, tokens, 2 * HEAD_SIZE), BF),
        ],
        compiler_params=kernel_params(),
        cost_estimate=pl.CostEstimate(
            flops=10 * tokens * tokens * blocks * columns,
            bytes_accessed=8 * tokens * columns * blocks,
            transcendentals=2 * tokens * tokens * blocks * heads,
        ),
    )(scalars, query, dattended, attended, kv, logsum)


def residual_rows(attn, hidden, scale_two, scale_three):
    attn, hidden = attn.astype(F32), hidden.astype(F32)
    after = hidden + normalize(attn)[0] * scale_two
    return after, normalize(after)[0] * scale_three


def output_rows(ffn_out, after, cot, scale_four):
    normed, factor = normalize(ffn_out.astype(F32))
    cot = cot.astype(F32)
    return (
        after + normed * scale_four,
        norm_back(cot * scale_four, normed, factor),
        cot * normed,
    )


def residual_back_rows(dffn_in, after, attn, cot, scale_three, scale_two):
    dffn_in = dffn_in.astype(F32)
    normed, factor = normalize(after)
    dafter = cot.astype(F32) + norm_back(dffn_in * scale_three, normed, factor)
    normed_two, factor_two = normalize(attn.astype(F32))
    dattn = norm_back(dafter * scale_two, normed_two, factor_two)
    return dafter, dattn, dffn_in * normed, dafter * normed_two


def plane_body(
    hidden_in,
    lengths,
    query_weight,
    key_weight,
    value_weight,
    w_out,
    w_gate,
    w_up,
    w_down,
    gain_attn_in,
    gain_attn_out,
    gain_ffn_in,
    gain_ffn_out,
    cotangent,
):
    seqs_here, tok_here, width = hidden_in.shape
    row_count = seqs_here * tok_here
    head_groups = QUERY_HEADS // KEY_VALUE_HEADS
    half_width = width // 2
    q_cols, kv_cols = query_weight.shape[1], key_weight.shape[1]
    size = lax.axis_size("tp")
    kv_local = kv_cols // HEAD_SIZE
    planes, me = lax.axis_size("ctx"), lax.axis_index("ctx")

    core = lax.axis_index("fsdp")

    def gather(shard):
        return lax.all_gather(shard, ("fsdp", "ctx"), axis=0, tiled=True)

    def far_half(rows):
        return send("core", lax.dynamic_slice_in_dim(rows, (1 - core) * half_width, half_width, 1))

    attention_shards = jnp.concatenate([query_weight, key_weight, value_weight, w_out.T], 1)
    attention_w = gather(attention_shards)
    ffn_shards = jnp.concatenate([w_gate, w_up, w_down.T], 1)
    gains = jnp.stack([gain_attn_in, gain_attn_out, gain_ffn_in, gain_ffn_out])[None]
    gains = jnp.broadcast_to(gains, (2 * planes,) + gains.shape[1:])
    gains = lax.all_to_all(gains, ("fsdp", "ctx"), 0, 0, tiled=True)
    gains = gains.transpose(1, 0, 2).reshape(4, width).astype(F32)
    scale_one, scale_two, scale_three, scale_four = (1.0 + gains[i][None] for i in range(4))
    flat_in = hidden_in.astype(F32).reshape(row_count, width)
    normed_one, factor_one = normalize(flat_in)
    attention_input = (normed_one * scale_one).astype(BF)

    attention_w, attention_input, ffn_shards = tied(attention_w, attention_input, ffn_shards)
    ffn_w = gather(ffn_shards)
    qkv_cols = q_cols + 2 * kv_cols
    qkv_w, out_w = attention_w[:, :qkv_cols], attention_w[:, qkv_cols:]
    run = jnp.arange(tok_here, dtype=jnp.int32)
    query_pos = me * tok_here + run
    key_pos = jnp.concatenate([(me ^ k) * tok_here + run for k in range(planes)])
    valid = query_pos[None, :] < lengths[:, None]
    allowed = (
        (key_pos[None, None, :] <= query_pos[None, :, None])
        & (key_pos[None, None, :] < lengths[:, None, None])
    )[:, None, None]
    qkv = plain_dot(attention_input, qkv_w).astype(BF)
    query_b = qkv[:, :q_cols]
    kv = qkv[:, q_cols:].reshape(seqs_here, tok_here, 2 * kv_cols)
    kv_all = jnp.concatenate([kv, send("x", kv), send("y", kv), send("diagonal", kv)], 1)
    query_five = query_b.reshape(seqs_here, tok_here, kv_local, head_groups, HEAD_SIZE)
    key_four = kv_all[:, :, :kv_cols].reshape(seqs_here, SEQUENCE_SLOTS, kv_local, HEAD_SIZE)
    value_four = kv_all[:, :, kv_cols:].reshape(seqs_here, SEQUENCE_SLOTS, kv_local, HEAD_SIZE)
    raw = jnp.einsum("stkgd,sukd->skgtu", query_five, key_four, preferred_element_type=F32) * QSCALE
    bent = jnp.tanh(raw / CAP)
    masked = jnp.where(allowed, CAP * bent, NEG)
    largest = jnp.max(masked, -1, keepdims=True)
    logsum = largest + jnp.log(jnp.sum(jnp.exp(masked - largest), -1, keepdims=True))
    probs = jnp.exp(masked - logsum)
    probs_b = probs.astype(BF)
    attended = (
        jnp.einsum("skgtu,sukd->stkgd", probs_b, value_four, preferred_element_type=F32)
        .astype(BF)
        .reshape(row_count, -1)
    )
    attn = right_dot(attended, out_w).astype(BF)
    ring = Ring(attn, 2)
    for _ in range(2 * size - 3):
        ring.go()
    attn = ring.finish()
    hidden_rows = hidden_in.reshape(row_count, width)
    after_attn, ffn_in = rowwise(
        residual_rows, [attn, hidden_rows], [scale_two, scale_three], [F32, BF]
    )
    gate, upward, hidden_b = ffn_hidden(ffn_in, ffn_w)
    ffn_out = ffn_down(hidden_b, ffn_w)
    ffn_out, hidden_b, attended, ffn_in, attention_input, cotangent = tied(
        ffn_out, hidden_b, attended, ffn_in, attention_input, cotangent
    )
    ring = Ring(ffn_out, 2)

    hidden_far, attended_far = send("core", hidden_b), send("core", attended)
    ffn_in_far, attention_input_far = far_half(ffn_in), far_half(attention_input)
    cot = jnp.where(
        valid.reshape(row_count, 1), cotangent.reshape(row_count, width), jnp.zeros((), BF)
    )
    ring.go()
    ring.going, hidden_far, attended_far, ffn_in_far, attention_input_far, cot = tied(
        ring.going, hidden_far, attended_far, ffn_in_far, attention_input_far, cot
    )
    ffn_out = ring.finish()
    output, dffn_b, gain_four_rows = rowwise(
        output_rows, [ffn_out, after_attn, cot], [scale_four], [BF, BF], 1
    )
    dgate_b, dup_b = ffn_hidden_back(dffn_b, ffn_w, gate, upward)
    dffn_in = ffn_input_back(dgate_b, dup_b, ffn_w)
    dffn_far = far_half(dffn_b)

    dffn_in, dffn_far, dgate_b, dup_b = tied(dffn_in, dffn_far, dgate_b, dup_b)
    ring = Ring(dffn_in)
    dgate_far = send("core", dgate_b)
    down_s = Scatter(weight_grad(dffn_b, dffn_far, hidden_b, hidden_far))
    ring.going, down_s.blocks, dgate_far = tied(ring.going, down_s.blocks, dgate_far)
    ring.go()
    down_s.diagonal()
    dup_far = send("core", dup_b)
    gate_s = Scatter(weight_grad(ffn_in, ffn_in_far, dgate_b, dgate_far))
    ring.going, gate_s.blocks, dup_far, down_s.first = tied(
        ring.going, gate_s.blocks, dup_far, down_s.first
    )
    ring.go()
    down_s.direct()
    up_s = Scatter(weight_grad(ffn_in, ffn_in_far, dup_b, dup_far))
    ring.going, up_s.blocks, down_s.middle = tied(ring.going, up_s.blocks, down_s.middle)
    ring.go()
    down_s.sums()
    ring.going, down_s.last, gate_s.blocks = tied(ring.going, down_s.last, gate_s.blocks)
    ring.go()
    gate_s.diagonal()
    grad_down = down_s.result().T
    ring.going, gate_s.first, grad_down = tied(ring.going, gate_s.first, grad_down)
    ring.go()
    gate_s.direct()
    dffn_in, up_s.blocks, gate_s.first, gate_s.middle = tied(
        ring.finish(), up_s.blocks, gate_s.first, gate_s.middle
    )
    gate_s.sums()
    up_s.diagonal()
    dafter, dattn_b, gain_three_rows, gain_two_rows = rowwise(
        residual_back_rows,
        [dffn_in, after_attn, attn, cot],
        [scale_three, scale_two],
        [F32, BF],
        2,
    )
    dattended = plain_dot(dattn_b, out_w).astype(BF)
    dattn_far = far_half(dattn_b)
    dattended, gate_s.last, up_s.first, up_s.blocks = tied(
        dattended, gate_s.last, up_s.first, up_s.blocks
    )
    up_s.direct()
    dquery_b, dkv = attention_back(
        query_b, dattended, attended, kv_all[0], logsum.reshape(head_groups, row_count, 1), lengths[0]
    )
    dkv, dattn_far, up_s.middle = tied(dkv, dattn_far, up_s.middle)
    dkv = [dkv[0], send("x", dkv[1]), send("y", dkv[2]), send("diagonal", dkv[3])]
    out_s = Scatter(weight_grad(dattn_b, dattn_far, attended, attended_far, True))
    grad_gate = gate_s.result()
    dkv, dquery_b, out_s.blocks, grad_gate, up_s.blocks = tied(
        dkv, dquery_b, out_s.blocks, grad_gate, up_s.blocks
    )
    dkv_b = sum(part.astype(F32) for part in dkv).astype(BF)
    dqkv_b = jnp.concatenate([dquery_b, dkv_b], 1)
    dattn_in = right_dot(dqkv_b, qkv_w)
    dattn_in, dqkv_b, dafter, up_s.blocks = tied(
        dattn_in.astype(BF), dqkv_b, dafter, up_s.blocks
    )

    ring = Ring(dattn_in)
    dqkv_far = send("core", dqkv_b)
    qkv_s = Scatter(
        weight_grad(attention_input, attention_input_far, dqkv_b, dqkv_far, True)
    )
    up_s.sums()
    gain_rows = gain_two_rows, gain_three_rows, gain_four_rows
    ring.going, qkv_s.blocks, up_s.last, gain_rows = tied(
        ring.going, qkv_s.blocks, up_s.last, gain_rows
    )
    ring.go()
    qkv_s.both()
    grad_gain_one = jnp.sum(dattn_in.astype(F32) * normed_one, 0)
    grad_gains = jnp.stack([grad_gain_one] + [jnp.sum(rows, 0) / size for rows in gain_rows])
    grad_gains = grad_gains.reshape(4, 2 * planes, 1, -1).transpose(1, 2, 0, 3)
    grad_gains = jnp.broadcast_to(grad_gains, (2 * planes, size) + grad_gains.shape[2:])
    grad_gains = grad_gains.reshape((-1,) + grad_gains.shape[2:])
    ring.going, qkv_s.first, qkv_s.middle, out_s.blocks = tied(
        ring.going, qkv_s.first, qkv_s.middle, out_s.blocks
    )
    ring.go()
    qkv_s.sums()
    out_s.both()
    grad_up = up_s.result()
    ring.going, qkv_s.last, out_s.first, out_s.middle, grad_up, grad_gains = tied(
        ring.going, qkv_s.last, out_s.first, out_s.middle, grad_up, grad_gains
    )
    ring.go()
    out_s.sums()
    grad_gains = lax.all_to_all(grad_gains, ("fsdp", "ctx", "tp"), 0, 0, tiled=True)
    grad_qkv = qkv_s.result()
    ring.going, out_s.last, grad_qkv = tied(ring.going, out_s.last, grad_qkv)
    ring.go()
    grad_out = out_s.result().T
    ring.going, grad_out = tied(ring.going, grad_out)
    ring.go()
    dattn_in, grad_gains = tied(ring.finish(), grad_gains)
    grad_gains = jnp.sum(grad_gains, 0)
    dattn_in = dattn_in.astype(F32)
    grad_input = dafter + norm_back(dattn_in * scale_one, normed_one, factor_one)
    grad_input = grad_input.astype(BF)
    return (
        output.reshape(hidden_in.shape),
        grad_input.reshape(hidden_in.shape),
        grad_qkv[:, :q_cols],
        grad_qkv[:, q_cols : q_cols + kv_cols],
        grad_qkv[:, q_cols + kv_cols :],
        grad_out,
        grad_gate,
        grad_up,
        grad_down,
        grad_gains[0],
        grad_gains[1],
        grad_gains[2],
        grad_gains[3],
    )


def general_body(
    hidden_in,
    lengths,
    query_weight,
    key_weight,
    value_weight,
    w_out,
    w_gate,
    w_up,
    w_down,
    gain_attn_in,
    gain_attn_out,
    gain_ffn_in,
    gain_ffn_out,
    cotangent,
):
    seqs_here, tok_here, width = hidden_in.shape
    row_count = seqs_here * tok_here
    head_groups = QUERY_HEADS // KEY_VALUE_HEADS
    gathered = (
        lax.all_gather(query_weight, ("fsdp", "ctx"), axis=0, tiled=True),
        lax.all_gather(key_weight, ("fsdp", "ctx"), axis=0, tiled=True),
        lax.all_gather(value_weight, ("fsdp", "ctx"), axis=0, tiled=True),
        lax.all_gather(w_out, ("fsdp", "ctx"), axis=1, tiled=True),
        lax.all_gather(w_gate, ("fsdp", "ctx"), axis=0, tiled=True),
        lax.all_gather(w_up, ("fsdp", "ctx"), axis=0, tiled=True),
        lax.all_gather(w_down, ("fsdp", "ctx"), axis=1, tiled=True),
        lax.all_gather(gain_attn_in, ("fsdp", "ctx"), axis=0, tiled=True),
        lax.all_gather(gain_attn_out, ("fsdp", "ctx"), axis=0, tiled=True),
        lax.all_gather(gain_ffn_in, ("fsdp", "ctx"), axis=0, tiled=True),
        lax.all_gather(gain_ffn_out, ("fsdp", "ctx"), axis=0, tiled=True),
    )
    query_full, key_full, value_full, out_full, gate_full, up_full, down_full = gathered[:7]
    scale_one = 1.0 + gathered[7].astype(jnp.float32)
    scale_two = 1.0 + gathered[8].astype(jnp.float32)
    scale_three = 1.0 + gathered[9].astype(jnp.float32)
    scale_four = 1.0 + gathered[10].astype(jnp.float32)
    kv_local = key_full.shape[1] // HEAD_SIZE
    own_start = lax.axis_index("ctx") * tok_here
    query_pos = own_start + jnp.arange(tok_here, dtype=jnp.int32)
    key_pos = jnp.arange(SEQUENCE_SLOTS, dtype=jnp.int32)
    valid = query_pos[None, :] < lengths[:, None]
    allowed = (
        (key_pos[None, None, :] <= query_pos[None, :, None])
        & (key_pos[None, None, :] < lengths[:, None, None])
    )[:, None, None]
    flat_in = hidden_in.astype(jnp.float32).reshape(row_count, width)
    normed_one, factor_one = normalize(flat_in)
    attention_input = (normed_one * scale_one).astype(jnp.bfloat16)
    query_b = plain_dot(attention_input, query_full).astype(jnp.bfloat16)
    key_b = (
        plain_dot(attention_input, key_full)
        .astype(jnp.bfloat16)
        .reshape(seqs_here, tok_here, kv_local * HEAD_SIZE)
    )
    value_b = (
        plain_dot(attention_input, value_full)
        .astype(jnp.bfloat16)
        .reshape(seqs_here, tok_here, kv_local * HEAD_SIZE)
    )
    key_all, value_all = (
        lax.all_gather(key_b, "ctx", axis=1, tiled=True),
        lax.all_gather(value_b, "ctx", axis=1, tiled=True),
    )
    query_five = query_b.reshape(seqs_here, tok_here, kv_local, head_groups, HEAD_SIZE)
    key_four = key_all.reshape(seqs_here, SEQUENCE_SLOTS, kv_local, HEAD_SIZE)
    value_four = value_all.reshape(seqs_here, SEQUENCE_SLOTS, kv_local, HEAD_SIZE)
    raw = (
        jnp.einsum("stkgd,sukd->skgtu", query_five, key_four, preferred_element_type=jnp.float32)
        * QSCALE
    )
    bent = jnp.tanh(raw / CAP)
    masked = jnp.where(allowed, CAP * bent, NEG)
    largest = jnp.max(masked, -1, keepdims=True)
    logsum = largest + jnp.log(jnp.sum(jnp.exp(masked - largest), -1, keepdims=True))
    probs = jnp.exp(masked - logsum)
    probs_b = probs.astype(jnp.bfloat16)
    attended = (
        jnp.einsum("skgtu,sukd->stkgd", probs_b, value_four, preferred_element_type=jnp.float32)
        .astype(jnp.bfloat16)
        .reshape(row_count, -1)
    )
    attn = lax.psum(plain_dot(attended, out_full).astype(jnp.bfloat16), "tp").astype(jnp.float32)
    normed_two, factor_two = normalize(attn)
    after_attn = flat_in + normed_two * scale_two
    normed_three, factor_three = normalize(after_attn)
    ffn_in = (normed_three * scale_three).astype(jnp.bfloat16)
    gate = plain_dot(ffn_in, gate_full)
    upward = plain_dot(ffn_in, up_full)
    activated, gelu_pull = jax.vjp(gelu_tanh, gate)
    hidden_b = (activated * upward).astype(jnp.bfloat16)
    ffn_out = lax.psum(plain_dot(hidden_b, down_full).astype(jnp.bfloat16), "tp").astype(
        jnp.float32
    )
    normed_four, factor_four = normalize(ffn_out)
    result = after_attn + normed_four * scale_four
    cot = cotangent.astype(jnp.float32).reshape(row_count, width) * valid.reshape(
        row_count, 1
    ).astype(jnp.float32)
    query_back, key_back, value_back, out_back, gate_back, up_back, down_back = (
        lax.all_gather(query_weight, ("fsdp", "ctx"), axis=0, tiled=True),
        lax.all_gather(key_weight, ("fsdp", "ctx"), axis=0, tiled=True),
        lax.all_gather(value_weight, ("fsdp", "ctx"), axis=0, tiled=True),
        lax.all_gather(w_out, ("fsdp", "ctx"), axis=1, tiled=True),
        lax.all_gather(w_gate, ("fsdp", "ctx"), axis=0, tiled=True),
        lax.all_gather(w_up, ("fsdp", "ctx"), axis=0, tiled=True),
        lax.all_gather(w_down, ("fsdp", "ctx"), axis=1, tiled=True),
    )
    grad_gain_four = jnp.sum(cot * normed_four, 0)
    dffn_b = norm_back(cot * scale_four, normed_four, factor_four).astype(jnp.bfloat16)
    grad_down = left_dot(hidden_b, dffn_b)
    dhidden = right_dot(dffn_b, down_back)
    dgate_b = gelu_pull(dhidden * upward)[0].astype(jnp.bfloat16)
    dup_b = (dhidden * activated).astype(jnp.bfloat16)
    grad_gate = left_dot(ffn_in, dgate_b)
    grad_up = left_dot(ffn_in, dup_b)
    dffn_in = lax.psum(
        (right_dot(dgate_b, gate_back) + right_dot(dup_b, up_back)).astype(jnp.bfloat16), "tp"
    ).astype(jnp.float32)
    grad_gain_three = jnp.sum(dffn_in * normed_three, 0)
    dafter = cot + norm_back(dffn_in * scale_three, normed_three, factor_three)
    grad_gain_two = jnp.sum(dafter * normed_two, 0)
    dattn_b = norm_back(dafter * scale_two, normed_two, factor_two).astype(jnp.bfloat16)
    grad_out = left_dot(attended, dattn_b)
    dattended = right_dot(dattn_b, out_back).astype(jnp.bfloat16).reshape(query_five.shape)
    dprobs = jnp.einsum(
        "stkgd,sukd->skgtu", dattended, value_four, preferred_element_type=jnp.float32
    )
    weighted = jnp.sum(probs * dprobs, -1, keepdims=True)
    draw_b = (probs * (dprobs - weighted) * (1.0 - bent * bent)).astype(jnp.bfloat16)
    dquery_b = (
        (
            jnp.einsum("skgtu,sukd->stkgd", draw_b, key_four, preferred_element_type=jnp.float32)
            * QSCALE
        )
        .astype(jnp.bfloat16)
        .reshape(row_count, -1)
    )
    dvalue_part = jnp.einsum(
        "skgtu,stkgd->sukd", probs_b, dattended, preferred_element_type=jnp.float32
    )
    dkey_part = (
        jnp.einsum("skgtu,stkgd->sukd", draw_b, query_five, preferred_element_type=jnp.float32)
        * QSCALE
    )
    dkey, dvalue = (
        lax.psum_scatter(
            dkey_part.astype(jnp.bfloat16), "ctx", scatter_dimension=1, tiled=True
        ).astype(jnp.float32),
        lax.psum_scatter(
            dvalue_part.astype(jnp.bfloat16), "ctx", scatter_dimension=1, tiled=True
        ).astype(jnp.float32),
    )
    dkey_b = dkey.astype(jnp.bfloat16).reshape(row_count, -1)
    dvalue_b = dvalue.astype(jnp.bfloat16).reshape(row_count, -1)
    grad_query = left_dot(attention_input, dquery_b)
    grad_key = left_dot(attention_input, dkey_b)
    grad_value = left_dot(attention_input, dvalue_b)
    dattn_in = lax.psum(
        (
            right_dot(dquery_b, query_back)
            + right_dot(dkey_b, key_back)
            + right_dot(dvalue_b, value_back)
        ).astype(jnp.bfloat16),
        "tp",
    ).astype(jnp.float32)
    grad_gain_one = jnp.sum(dattn_in * normed_one, 0)
    grad_input = dafter + norm_back(dattn_in * scale_one, normed_one, factor_one)
    summed = (
        lax.psum_scatter(
            grad_query.astype(jnp.bfloat16), ("fsdp", "ctx"), scatter_dimension=0, tiled=True
        ).astype(jnp.float32),
        lax.psum_scatter(
            grad_key.astype(jnp.bfloat16), ("fsdp", "ctx"), scatter_dimension=0, tiled=True
        ).astype(jnp.float32),
        lax.psum_scatter(
            grad_value.astype(jnp.bfloat16), ("fsdp", "ctx"), scatter_dimension=0, tiled=True
        ).astype(jnp.float32),
        lax.psum_scatter(
            grad_out.astype(jnp.bfloat16), ("fsdp", "ctx"), scatter_dimension=1, tiled=True
        ).astype(jnp.float32),
        lax.psum_scatter(
            grad_gate.astype(jnp.bfloat16), ("fsdp", "ctx"), scatter_dimension=0, tiled=True
        ).astype(jnp.float32),
        lax.psum_scatter(
            grad_up.astype(jnp.bfloat16), ("fsdp", "ctx"), scatter_dimension=0, tiled=True
        ).astype(jnp.float32),
        lax.psum_scatter(
            grad_down.astype(jnp.bfloat16), ("fsdp", "ctx"), scatter_dimension=1, tiled=True
        ).astype(jnp.float32),
        lax.psum_scatter(
            grad_gain_one.astype(jnp.bfloat16), ("fsdp", "ctx"), scatter_dimension=0, tiled=True
        ).astype(jnp.float32),
        lax.psum_scatter(
            grad_gain_two.astype(jnp.bfloat16), ("fsdp", "ctx"), scatter_dimension=0, tiled=True
        ).astype(jnp.float32),
        lax.psum_scatter(
            grad_gain_three.astype(jnp.bfloat16), ("fsdp", "ctx"), scatter_dimension=0, tiled=True
        ).astype(jnp.float32),
        lax.psum_scatter(
            grad_gain_four.astype(jnp.bfloat16), ("fsdp", "ctx"), scatter_dimension=0, tiled=True
        ).astype(jnp.float32),
    )
    return (
        result.astype(jnp.bfloat16).reshape(hidden_in.shape),
        grad_input.astype(jnp.bfloat16).reshape(hidden_in.shape),
        summed[0],
        summed[1],
        summed[2],
        summed[3],
        summed[4],
        summed[5],
        summed[6],
        summed[7],
        summed[8],
        summed[9],
        summed[10],
    )


def solution(mesh):
    square = mesh.shape["ctx"] == 4 and mesh.shape["fsdp"] == 2
    return jax.shard_map(
        plane_body if square else general_body,
        mesh=mesh,
        in_specs=(
            P("fsdp", "ctx", None),
            P("fsdp"),
            P(("fsdp", "ctx"), "tp"),
            P(("fsdp", "ctx"), "tp"),
            P(("fsdp", "ctx"), "tp"),
            P("tp", ("fsdp", "ctx")),
            P(("fsdp", "ctx"), "tp"),
            P(("fsdp", "ctx"), "tp"),
            P("tp", ("fsdp", "ctx")),
            P(("fsdp", "ctx")),
            P(("fsdp", "ctx")),
            P(("fsdp", "ctx")),
            P(("fsdp", "ctx")),
            P("fsdp", "ctx", None),
        ),
        out_specs=(
            P("fsdp", "ctx", None),
            P("fsdp", "ctx", None),
            P(("fsdp", "ctx"), "tp"),
            P(("fsdp", "ctx"), "tp"),
            P(("fsdp", "ctx"), "tp"),
            P("tp", ("fsdp", "ctx")),
            P(("fsdp", "ctx"), "tp"),
            P(("fsdp", "ctx"), "tp"),
            P("tp", ("fsdp", "ctx")),
            P(("fsdp", "ctx")),
            P(("fsdp", "ctx")),
            P(("fsdp", "ctx")),
            P(("fsdp", "ctx")),
        ),
        check_vma=False,
    )
```

```python
import jax
import jax.numpy as jnp
from jax import lax
from jax.experimental import pallas as pl
from jax.experimental.pallas import tpu as pltpu
from jax.sharding import PartitionSpec as P

QUERY_HEADS = 8
KEY_VALUE_HEADS = 4
HEAD_SIZE = 256
SEQUENCE_SLOTS = 2048


EPS = 1e-06
CAP = 50.0
QSCALE = 0.0625
NEG = -1e30


def normalize(value_rows):
    factor = lax.rsqrt(jnp.mean(value_rows * value_rows, -1, keepdims=True) + EPS)
    return (value_rows * factor, factor)


def norm_back(grad_hat, normed, factor):
    return factor * (grad_hat - normed * jnp.mean(grad_hat * normed, -1, keepdims=True))


def plain_dot(first, second):
    return jnp.dot(first, second, preferred_element_type=jnp.float32)


def left_dot(first, second):
    return lax.dot_general(
        first, second, (((0,), (0,)), ((), ())), preferred_element_type=jnp.float32
    )


def right_dot(first, second):
    return lax.dot_general(
        first, second, (((1,), (1,)), ((), ())), preferred_element_type=jnp.float32
    )


def gelu_tanh(value_rows):
    return jax.nn.gelu(value_rows, approximate=True)


BF = jnp.bfloat16
F32 = jnp.float32

LINKS = {
    "x": ("ctx", [(0, 1), (1, 0), (2, 3), (3, 2)]),
    "y": ("ctx", [(0, 2), (2, 0), (1, 3), (3, 1)]),
    "diagonal": ("ctx", [(0, 3), (3, 0), (1, 2), (2, 1)]),
    "core": ("fsdp", [(0, 1), (1, 0)]),
}
ORDER = [(0, 0), (0, 1), (1, 1), (2, 0), (1, 0), (3, 0), (3, 1), (2, 1)]


def tied(*values):
    return lax.optimization_barrier(values)


def send(link, value):
    return lax.ppermute(value, *LINKS[link])


def around(value, by=1):
    size = lax.axis_size("tp")
    return lax.ppermute(value, "tp", [(i, (i + by) % size) for i in range(size)])


def place(pieces, starts):
    rows = sum(piece.shape[0] for piece in pieces)
    whole = jnp.zeros((rows,) + pieces[0].shape[1:], pieces[0].dtype)
    for piece, start in zip(pieces, starts):
        whole = lax.dynamic_update_slice_in_dim(whole, piece, start, 0)
    return whole


def halves(block):
    half = block.shape[0] // 2
    return block[:half], block[half:]


class Scatter:
    def __init__(self, blocks):
        self.blocks = blocks
        self.half = blocks[1].shape[0]

    def diagonal(self):
        self.first = (send("x", self.blocks[2]), send("y", self.blocks[3]))

    def both(self):
        half = self.half = self.blocks[1].shape[0] // 2
        from_x, from_y = send("x", self.blocks[1]), send("y", self.blocks[2])
        self.first, self.middle = (from_x[half:], from_y[:half]), (from_x[:half], from_y[half:])

    def direct(self):
        self.middle = (send("x", self.blocks[1]), send("y", self.blocks[4]))

    def sums(self):
        half, kept, (d_top, d_low) = self.half, self.blocks[0], self.first
        x_low, y_top = kept[2 * half : 3 * half], kept[3 * half :]
        self.last = (
            send("x", (x_low.astype(F32) + d_low.astype(F32)).astype(BF)),
            send("y", (y_top.astype(F32) + d_top.astype(F32)).astype(BF)),
        )

    def result(self):
        half, kept = self.half, self.blocks[0]
        (x_top, y_low), (x_low, y_top) = self.middle, self.last
        top = kept[:half].astype(F32) + x_top.astype(F32) + y_top.astype(F32)
        low = kept[half : 2 * half].astype(F32) + y_low.astype(F32) + x_low.astype(F32)
        return jnp.concatenate([top, low], 0)


class Ring:
    def __init__(self, value, parts=1):
        self.value, self.step, self.parts = value, 0, parts
        self.size, self.me = lax.axis_size("tp"), lax.axis_index("tp")
        self.rows = value.shape[0] // (parts * self.size)
        self.whole = jnp.zeros_like(value)
        self.sent = [self.block(part, self.me - 1) for part in range(parts)]
        self.going = [around(sent) for sent in self.sent]

    def start(self, part, index):
        return (part * self.size + (index + self.size) % self.size) * self.rows

    def block(self, part, index):
        return lax.dynamic_slice_in_dim(self.value, self.start(part, index), self.rows, 0)

    def go(self):
        self.step += 1
        for part in range(self.parts):
            going = self.going[part]
            if self.parts > 1:
                going, _ = tied(going, self.sent[1 - part])
            if self.step < self.size:
                own = self.block(part, self.me - 1 - self.step)
                going = (going.astype(F32) + own.astype(F32)).astype(BF)
            if self.step >= self.size - 1:
                at = self.start(part, self.me - self.step + self.size - 1)
                self.whole = lax.dynamic_update_slice_in_dim(self.whole, going, at, 0)
            if self.step < 2 * self.size - 2:
                self.sent[part] = going
                self.going[part] = around(going)

    def finish(self):
        while self.step < 2 * self.size - 2:
            self.go()
        return self.whole


VMEM_BYTES = 56 * 2**20


def kernel_params():
    return pltpu.CompilerParams(vmem_limit_bytes=VMEM_BYTES)


def cut_of(size):
    return next((cut for cut in (768, 512) if size % cut == 0), size)


def rowwise(fn, rows, vectors, dtypes, sums=0, block=128):
    count, width = rows[0].shape
    n_in, n_out = len(rows) + len(vectors), len(dtypes)

    def kernel(*refs):
        results = fn(*(ref[...] for ref in refs[:n_in]))
        for ref, value in zip(refs[n_in : n_in + n_out], results):
            ref[...] = value.astype(ref.dtype)
        for ref, value in zip(refs[n_in + n_out :], results[n_out:]):
            part = jnp.sum(value.reshape(block // 8, 8, width), 0)

            @pl.when(pl.program_id(0) == 0)
            def _():
                ref[...] = part

            @pl.when(pl.program_id(0) > 0)
            def _():
                ref[...] += part

    by_row = pl.BlockSpec((block, width), lambda i: (i, 0))
    return pl.pallas_call(
        kernel,
        grid=(count // block,),
        in_specs=[by_row] * len(rows) + [pl.BlockSpec((1, width), lambda i: (0, 0))] * len(vectors),
        out_specs=[by_row] * n_out + [pl.BlockSpec((8, width), lambda i: (0, 0))] * sums,
        out_shape=[jax.ShapeDtypeStruct((count, width), dtype) for dtype in dtypes]
        + [jax.ShapeDtypeStruct((8, width), F32)] * sums,
        compiler_params=kernel_params(),
        cost_estimate=pl.CostEstimate(
            flops=20 * count * width, bytes_accessed=4 * count * width * n_in, transcendentals=0
        ),
    )(*rows, *vectors)


ROOT = 0.7978845608028654


def gelu_parts(z):
    bend = jnp.tanh(ROOT * (z + 0.044715 * (z * z * z)))
    value = 0.5 * z * (1.0 + bend)
    slope = 0.5 * (1.0 + bend) + 0.5 * z * (1.0 - bend * bend) * (
        ROOT * (1.0 + (3.0 * 0.044715) * (z * z))
    )
    return value, slope


def ffn_forward(x, weights, down_rest):
    count, width = x.shape
    cut, out_cut = down_rest.shape[1], cut_of(width)
    units = (weights.shape[1] + cut) // 3
    first = units // cut

    def kernel(x_ref, gate_w, up_w, down_w, rest_w, gate_ref, up_ref, hidden_ref, out_ref, kept):
        step = pl.program_id(0)

        @pl.when(step < first)
        def _():
            gate = plain_dot(x_ref[...], gate_w[...])
            up = plain_dot(x_ref[...], up_w[...])
            hidden = (gelu_parts(gate)[0] * up).astype(BF)
            gate_ref[...] = gate
            up_ref[...] = up
            hidden_ref[...] = hidden
            kept[step] = hidden

        @pl.when(step >= first)
        def _():
            total = right_dot(kept[first - 1], rest_w[...])
            for i in range(first - 1):
                total += right_dot(kept[i], down_w[:, i * cut : (i + 1) * cut])
            out_ref[...] = total.astype(BF)

    def early(j):
        return jnp.minimum(j, first - 1)

    def late(j):
        return jnp.maximum(j - first, 0)

    out = pl.BlockSpec((count, cut), lambda j: (0, early(j)))
    return pl.pallas_call(
        kernel,
        grid=(first + width // out_cut,),
        in_specs=[
            pl.BlockSpec((count, width), lambda j: (0, 0)),
            pl.BlockSpec((width, cut), lambda j: (0, early(j))),
            pl.BlockSpec((width, cut), lambda j: (0, early(j) + first)),
            pl.BlockSpec((out_cut, units - cut), lambda j: (late(j), 3)),
            pl.BlockSpec((out_cut, cut), lambda j: (late(j), 0)),
        ],
        out_specs=[out] * 3 + [pl.BlockSpec((count, out_cut), lambda j: (0, late(j)))],
        out_shape=[
            jax.ShapeDtypeStruct((count, units), F32),
            jax.ShapeDtypeStruct((count, units), F32),
            jax.ShapeDtypeStruct((count, units), BF),
            jax.ShapeDtypeStruct((count, width), BF),
        ],
        scratch_shapes=[pltpu.VMEM((first, count, cut), BF)],
        compiler_params=kernel_params(),
        cost_estimate=pl.CostEstimate(
            flops=6 * count * width * units,
            bytes_accessed=6 * width * units + 10 * count * units,
            transcendentals=count * units,
        ),
    )(x, weights, weights, weights, down_rest)


def ffn_backward(dffn, weights, down_rest, gate, up):
    count, width = dffn.shape
    units = gate.shape[1]
    cut, out_cut = down_rest.shape[1], cut_of(width)
    first = units // cut

    def kernel(
        d_ref,
        down_w,
        rest_w,
        gate_ref,
        up_ref,
        gate_w,
        up_w,
        dgate_ref,
        dup_ref,
        out_ref,
        kept,
        kept_up,
    ):
        step = pl.program_id(0)

        def make(weight):
            dhidden = plain_dot(d_ref[...], weight[...])
            value, slope = gelu_parts(gate_ref[...])
            dgate = (dhidden * up_ref[...] * slope).astype(BF)
            dup = (dhidden * value).astype(BF)
            dgate_ref[...] = dgate
            dup_ref[...] = dup
            kept[step] = dgate
            kept_up[step] = dup

        pl.when(step < first - 1)(lambda: make(down_w))
        pl.when(step == first - 1)(lambda: make(rest_w))

        @pl.when(step >= first)
        def _():
            out_ref[...] = sum(
                right_dot(terms[i], weight[:, i * cut : (i + 1) * cut])
                for i in range(first)
                for terms, weight in ((kept, gate_w), (kept_up, up_w))
            ).astype(BF)

    def early(j):
        return jnp.minimum(j, first - 1)

    def late(j):
        return jnp.maximum(j - first, 0)

    by_cut = pl.BlockSpec((count, cut), lambda j: (0, early(j)))
    return pl.pallas_call(
        kernel,
        grid=(first + width // out_cut,),
        in_specs=[
            pl.BlockSpec((count, width), lambda j: (0, 0)),
            pl.BlockSpec((width, cut), lambda j: (0, jnp.minimum(j, first - 2) + 2 * first)),
            pl.BlockSpec((width, cut), lambda j: (0, 0)),
            by_cut,
            by_cut,
            pl.BlockSpec((out_cut, units), lambda j: (late(j), 0)),
            pl.BlockSpec((out_cut, units), lambda j: (late(j), 1)),
        ],
        out_specs=[by_cut] * 2 + [pl.BlockSpec((count, out_cut), lambda j: (0, late(j)))],
        out_shape=[jax.ShapeDtypeStruct((count, units), BF)] * 2
        + [jax.ShapeDtypeStruct((count, width), BF)],
        scratch_shapes=[pltpu.VMEM((first, count, cut), BF)] * 2,
        compiler_params=kernel_params(),
        cost_estimate=pl.CostEstimate(
            flops=6 * count * width * units,
            bytes_accessed=6 * width * units + 12 * count * units,
            transcendentals=count * units,
        ),
    )(dffn, weights, down_rest, gate, up, weights, weights)


def weight_grad(rows, rows_far, cols, cols_far, joined=False):
    count, half_width = rows_far.shape
    width = cols.shape[1]
    cut = cut_of(width)
    half = half_width // 8
    place = jnp.stack([lax.axis_index("fsdp"), lax.axis_index("ctx")]).astype(jnp.int32)
    sizes = (4 * half, 2 * half, 2 * half) if joined else (4 * half,) + (half,) * 4

    def kernel(
        place_ref, near_ref, far_ref, cols_ref, cols_far_ref, *rest
    ):
        outs, (near_t, far_t, total) = rest[: len(sizes)], rest[len(sizes) :]

        @pl.when(pl.program_id(0) == 0)
        def _():
            near_t[...] = near_ref[...].T
            far_t[...] = far_ref[...].T

        total[...] = plain_dot(near_t[...], cols_ref[...]) + plain_dot(
            far_t[...], cols_far_ref[...]
        )
        for index, (k, low) in enumerate(ORDER):
            start = (lax.bitwise_xor(place_ref[1], k) * 2 + low) * half
            block = total[pl.ds(pl.multiple_of(start, 16), half), :].astype(BF)
            if index < 4:
                out, at = outs[0], index
            elif joined:
                out, at = outs[1 + (index - 4) // 2], index % 2
            else:
                out, at = outs[index - 3], 0
            out[at * half : (at + 1) * half, :] = block

    by_cut = pl.BlockSpec((count, cut), lambda j, place: (0, j))
    return pl.pallas_call(
        kernel,
        grid_spec=pltpu.PrefetchScalarGridSpec(
            num_scalar_prefetch=1,
            grid=(width // cut,),
            in_specs=[
                pl.BlockSpec((count, half_width), lambda j, place: (0, place[0])),
                pl.BlockSpec((count, half_width), lambda j, place: (0, 0)),
                by_cut,
                by_cut,
            ],
            out_specs=[pl.BlockSpec((size, cut), lambda j, place: (0, j)) for size in sizes],
            scratch_shapes=[
                pltpu.VMEM((half_width, count), BF),
                pltpu.VMEM((half_width, count), BF),
                pltpu.VMEM((half_width, cut), F32),
            ],
        ),
        out_shape=[jax.ShapeDtypeStruct((size, width), BF) for size in sizes],
        compiler_params=kernel_params(),
        cost_estimate=pl.CostEstimate(
            flops=4 * count * half_width * width,
            bytes_accessed=2 * half_width * width + 4 * count * (width + half_width),
            transcendentals=0,
        ),
    )(place, rows, rows_far, cols, cols_far)


def attention_back(query, dattended, attended, kv, logsum, length):
    tokens, columns = query.shape
    heads, blocks = columns // HEAD_SIZE, kv.shape[0] // tokens
    scalars = jnp.stack([lax.axis_index("ctx").astype(jnp.int32), length])

    def kernel(scalars_ref, q_ref, d_ref, a_ref, kv_ref, log_ref, dq_ref, dkv_ref, dq, dk, dv):
        block, head = pl.program_id(0), pl.program_id(1)
        q, d = q_ref[...], d_ref[...]
        key, value = kv_ref[:, :HEAD_SIZE], kv_ref[:, HEAD_SIZE:]
        me = scalars_ref[0]
        bent = jnp.tanh(right_dot(q, key) * (QSCALE / CAP))
        shape = (tokens, tokens)
        key_pos = lax.bitwise_xor(me, block) * tokens + lax.broadcasted_iota(jnp.int32, shape, 1)
        query_pos = me * tokens + lax.broadcasted_iota(jnp.int32, shape, 0)
        allowed = (key_pos <= query_pos) & (key_pos < scalars_ref[1])
        probs = jnp.where(allowed, jnp.exp(CAP * bent - log_ref[...]), 0.0)
        weighted = jnp.sum(d.astype(F32) * a_ref[...].astype(F32), -1, keepdims=True)
        draw = (probs * (right_dot(d, value) - weighted) * (1.0 - bent * bent)).astype(BF)
        dk_part, dv_part = left_dot(draw, q), left_dot(probs.astype(BF), d)
        dq_part = plain_dot(draw, key)

        @pl.when(head == 0)
        def _():
            dk[...] = dk_part
            dv[...] = dv_part

        @pl.when(head > 0)
        def _():
            dk[...] += dk_part
            dv[...] += dv_part

        @pl.when(block == 0)
        def _():
            dq[head] = dq_part

        @pl.when(block > 0)
        def _():
            dq[head] += dq_part

        @pl.when(head == heads - 1)
        def _():
            dkv_ref[:, :HEAD_SIZE] = (dk[...] * QSCALE).astype(BF)
            dkv_ref[:, HEAD_SIZE:] = dv[...].astype(BF)

        @pl.when((block == blocks - 1) & (head == heads - 1))
        def _():
            for i in range(heads):
                dq_ref[:, i * HEAD_SIZE : (i + 1) * HEAD_SIZE] = (dq[i] * QSCALE).astype(BF)

    by_head = pl.BlockSpec((tokens, HEAD_SIZE), lambda b, h, scalars: (0, h))
    return pl.pallas_call(
        kernel,
        grid_spec=pltpu.PrefetchScalarGridSpec(
            num_scalar_prefetch=1,
            grid=(blocks, heads),
            in_specs=[
                by_head,
                by_head,
                by_head,
                pl.BlockSpec((tokens, 2 * HEAD_SIZE), lambda b, h, scalars: (b, 0)),
                pl.BlockSpec((None, tokens, 1), lambda b, h, scalars: (h, 0, 0)),
            ],
            out_specs=[
                pl.BlockSpec((tokens, columns), lambda b, h, scalars: (0, 0)),
                pl.BlockSpec((None, tokens, 2 * HEAD_SIZE), lambda b, h, scalars: (b, 0, 0)),
            ],
            scratch_shapes=[
                pltpu.VMEM((heads, tokens, HEAD_SIZE), F32),
                pltpu.VMEM((tokens, HEAD_SIZE), F32),
                pltpu.VMEM((tokens, HEAD_SIZE), F32),
            ],
        ),
        out_shape=[
            jax.ShapeDtypeStruct((tokens, columns), BF),
            jax.ShapeDtypeStruct((blocks, tokens, 2 * HEAD_SIZE), BF),
        ],
        compiler_params=kernel_params(),
        cost_estimate=pl.CostEstimate(
            flops=10 * tokens * tokens * blocks * columns,
            bytes_accessed=8 * tokens * columns * blocks,
            transcendentals=2 * tokens * tokens * blocks * heads,
        ),
    )(scalars, query, dattended, attended, kv, logsum)


def residual_rows(attn, hidden, scale_two, scale_three):
    attn, hidden = attn.astype(F32), hidden.astype(F32)
    after = hidden + normalize(attn)[0] * scale_two
    return after, normalize(after)[0] * scale_three


def output_rows(ffn_out, after, cot, scale_four):
    normed, factor = normalize(ffn_out.astype(F32))
    cot = cot.astype(F32)
    return (
        after + normed * scale_four,
        norm_back(cot * scale_four, normed, factor),
        cot * normed,
    )


def residual_back_rows(dffn_in, after, attn, cot, scale_three, scale_two):
    dffn_in = dffn_in.astype(F32)
    normed, factor = normalize(after)
    dafter = cot.astype(F32) + norm_back(dffn_in * scale_three, normed, factor)
    normed_two, factor_two = normalize(attn.astype(F32))
    dattn = norm_back(dafter * scale_two, normed_two, factor_two)
    return dafter, dattn, dffn_in * normed, dafter * normed_two


def plane_body(
    hidden_in,
    lengths,
    query_weight,
    key_weight,
    value_weight,
    w_out,
    w_gate,
    w_up,
    w_down,
    gain_attn_in,
    gain_attn_out,
    gain_ffn_in,
    gain_ffn_out,
    cotangent,
):
    seqs_here, tok_here, width = hidden_in.shape
    row_count = seqs_here * tok_here
    head_groups = QUERY_HEADS // KEY_VALUE_HEADS
    half_width = width // 2
    q_cols, kv_cols = query_weight.shape[1], key_weight.shape[1]
    size = lax.axis_size("tp")
    kv_local = kv_cols // HEAD_SIZE
    planes, me = lax.axis_size("ctx"), lax.axis_index("ctx")

    core = lax.axis_index("fsdp")

    def gather(shard):
        return lax.all_gather(shard, ("fsdp", "ctx"), axis=0, tiled=True)

    def far_half(rows):
        return send("core", lax.dynamic_slice_in_dim(rows, (1 - core) * half_width, half_width, 1))

    attention_shards = jnp.concatenate([query_weight, key_weight, value_weight, w_out.T], 1)
    attention_w = gather(attention_shards)
    late = w_down.shape[0] - cut_of(w_down.shape[0])
    ffn_shards = jnp.concatenate([w_gate, w_up, w_down[:late].T], 1)
    rest_t = w_down[late:].T
    rest_x, rest_y = send("x", rest_t), send("y", rest_t)
    gains = jnp.stack([gain_attn_in, gain_attn_out, gain_ffn_in, gain_ffn_out])[None]
    gains = jnp.broadcast_to(gains, (2 * planes,) + gains.shape[1:])
    gains = lax.all_to_all(gains, ("fsdp", "ctx"), 0, 0, tiled=True)
    gains = gains.transpose(1, 0, 2).reshape(4, width).astype(F32)
    scale_one, scale_two, scale_three, scale_four = (1.0 + gains[i][None] for i in range(4))
    flat_in = hidden_in.astype(F32).reshape(row_count, width)
    normed_one, factor_one = normalize(flat_in)
    attention_input = (normed_one * scale_one).astype(BF)

    attention_w, attention_input, ffn_shards, rest_x, rest_y = tied(
        attention_w, attention_input, ffn_shards, rest_x, rest_y
    )
    ffn_w = gather(ffn_shards)
    qkv_cols = q_cols + 2 * kv_cols
    qkv_w, out_w = attention_w[:, :qkv_cols], attention_w[:, qkv_cols:]
    run = jnp.arange(tok_here, dtype=jnp.int32)
    query_pos = me * tok_here + run
    key_pos = jnp.concatenate([(me ^ k) * tok_here + run for k in range(planes)])
    valid = query_pos[None, :] < lengths[:, None]
    allowed = (
        (key_pos[None, None, :] <= query_pos[None, :, None])
        & (key_pos[None, None, :] < lengths[:, None, None])
    )[:, None, None]
    qkv = plain_dot(attention_input, qkv_w).astype(BF)
    query_b = qkv[:, :q_cols]
    kv = qkv[:, q_cols:].reshape(seqs_here, tok_here, 2 * kv_cols)
    kv_all = jnp.concatenate([kv, send("x", kv), send("y", kv), send("diagonal", kv)], 1)
    kv_all, rest_x, rest_y = tied(kv_all, rest_x, rest_y)
    rest_last = [send("y", halves(rest_x)[0]), send("x", halves(rest_y)[1])]
    query_five = query_b.reshape(seqs_here, tok_here, kv_local, head_groups, HEAD_SIZE)
    key_four = kv_all[:, :, :kv_cols].reshape(seqs_here, SEQUENCE_SLOTS, kv_local, HEAD_SIZE)
    value_four = kv_all[:, :, kv_cols:].reshape(seqs_here, SEQUENCE_SLOTS, kv_local, HEAD_SIZE)
    raw = jnp.einsum("stkgd,sukd->skgtu", query_five, key_four, preferred_element_type=F32) * QSCALE
    bent = jnp.tanh(raw / CAP)
    masked = jnp.where(allowed, CAP * bent, NEG)
    largest = jnp.max(masked, -1, keepdims=True)
    logsum = largest + jnp.log(jnp.sum(jnp.exp(masked - largest), -1, keepdims=True))
    probs = jnp.exp(masked - logsum)
    probs_b = probs.astype(BF)
    attended = (
        jnp.einsum("skgtu,sukd->stkgd", probs_b, value_four, preferred_element_type=F32)
        .astype(BF)
        .reshape(row_count, -1)
    )
    attended, rest_last = tied(attended, rest_last)
    attn = right_dot(attended, out_w).astype(BF)
    ring = Ring(attn, 2)
    ring.go()
    rows, start = rest_t.shape[0], [(me ^ k) * rest_t.shape[0] for k in range(4)]
    rest_near = place([rest_t, rest_x, rest_y, *rest_last], [*start, start[3] + rows // 2])
    ring.go()
    ring.going, rest_near = tied(ring.going, rest_near)
    rest_far = send("core", rest_near)
    ring.go()
    ring.go()
    ring.going, rest_far = tied(ring.going, rest_far)
    ring.go()
    down_rest = place([rest_near, rest_far], [core * half_width, (1 - core) * half_width])
    attn = ring.finish()
    hidden_rows = hidden_in.reshape(row_count, width)
    after_attn, ffn_in = rowwise(
        residual_rows, [attn, hidden_rows], [scale_two, scale_three], [F32, BF]
    )
    gate, upward, hidden_b, ffn_out = ffn_forward(ffn_in, ffn_w, down_rest)
    ffn_out, hidden_b, attended, ffn_in, attention_input, cotangent = tied(
        ffn_out, hidden_b, attended, ffn_in, attention_input, cotangent
    )
    ring = Ring(ffn_out, 2)

    hidden_far, attended_far = send("core", hidden_b), send("core", attended)
    ffn_in_far, attention_input_far = far_half(ffn_in), far_half(attention_input)
    cot = jnp.where(
        valid.reshape(row_count, 1), cotangent.reshape(row_count, width), jnp.zeros((), BF)
    )
    ring.go()
    ring.going, hidden_far, attended_far, ffn_in_far, attention_input_far, cot = tied(
        ring.going, hidden_far, attended_far, ffn_in_far, attention_input_far, cot
    )
    ffn_out = ring.finish()
    output, dffn_b, gain_four_rows = rowwise(
        output_rows, [ffn_out, after_attn, cot], [scale_four], [BF, BF], 1
    )
    dgate_b, dup_b, dffn_in = ffn_backward(
        dffn_b, ffn_w, down_rest, gate, upward
    )
    dffn_far = far_half(dffn_b)

    dffn_in, dffn_far, dgate_b, dup_b = tied(dffn_in, dffn_far, dgate_b, dup_b)
    ring = Ring(dffn_in)
    dgate_far = send("core", dgate_b)
    down_s = Scatter(weight_grad(dffn_b, dffn_far, hidden_b, hidden_far))
    ring.going, down_s.blocks, dgate_far = tied(ring.going, down_s.blocks, dgate_far)
    ring.go()
    down_s.diagonal()
    dup_far = send("core", dup_b)
    gate_s = Scatter(weight_grad(ffn_in, ffn_in_far, dgate_b, dgate_far))
    ring.going, gate_s.blocks, dup_far, down_s.first = tied(
        ring.going, gate_s.blocks, dup_far, down_s.first
    )
    ring.go()
    down_s.direct()
    up_s = Scatter(weight_grad(ffn_in, ffn_in_far, dup_b, dup_far))
    ring.going, up_s.blocks, down_s.middle = tied(ring.going, up_s.blocks, down_s.middle)
    ring.go()
    down_s.sums()
    ring.going, down_s.last, gate_s.blocks = tied(ring.going, down_s.last, gate_s.blocks)
    ring.go()
    gate_s.diagonal()
    grad_down = down_s.result().T
    ring.going, gate_s.first, grad_down = tied(ring.going, gate_s.first, grad_down)
    ring.go()
    gate_s.direct()
    dffn_in, up_s.blocks, gate_s.first, gate_s.middle = tied(
        ring.finish(), up_s.blocks, gate_s.first, gate_s.middle
    )
    gate_s.sums()
    up_s.diagonal()
    dafter, dattn_b, gain_three_rows, gain_two_rows = rowwise(
        residual_back_rows,
        [dffn_in, after_attn, attn, cot],
        [scale_three, scale_two],
        [F32, BF],
        2,
    )
    dattended = plain_dot(dattn_b, out_w).astype(BF)
    dattn_far = far_half(dattn_b)
    dattended, gate_s.last, up_s.first, up_s.blocks = tied(
        dattended, gate_s.last, up_s.first, up_s.blocks
    )
    up_s.direct()
    dquery_b, dkv = attention_back(
        query_b, dattended, attended, kv_all[0], logsum.reshape(head_groups, row_count, 1), lengths[0]
    )
    dkv, dattn_far, up_s.middle = tied(dkv, dattn_far, up_s.middle)
    dkv = [dkv[0], send("x", dkv[1]), send("y", dkv[2]), send("diagonal", dkv[3])]
    out_s = Scatter(weight_grad(dattn_b, dattn_far, attended, attended_far, True))
    grad_gate = gate_s.result()
    dkv, dquery_b, out_s.blocks, grad_gate, up_s.blocks = tied(
        dkv, dquery_b, out_s.blocks, grad_gate, up_s.blocks
    )
    dkv_b = sum(part.astype(F32) for part in dkv).astype(BF)
    dqkv_b = jnp.concatenate([dquery_b, dkv_b], 1)
    dattn_in = right_dot(dqkv_b, qkv_w)
    dattn_in, dqkv_b, dafter, up_s.blocks = tied(
        dattn_in.astype(BF), dqkv_b, dafter, up_s.blocks
    )

    ring = Ring(dattn_in)
    dqkv_far = send("core", dqkv_b)
    qkv_s = Scatter(
        weight_grad(attention_input, attention_input_far, dqkv_b, dqkv_far, True)
    )
    up_s.sums()
    gain_rows = gain_two_rows, gain_three_rows, gain_four_rows
    ring.going, qkv_s.blocks, up_s.last, gain_rows = tied(
        ring.going, qkv_s.blocks, up_s.last, gain_rows
    )
    ring.go()
    qkv_s.both()
    grad_gain_one = jnp.sum(dattn_in.astype(F32) * normed_one, 0)
    grad_gains = jnp.stack([grad_gain_one] + [jnp.sum(rows, 0) / size for rows in gain_rows])
    grad_gains = grad_gains.reshape(4, 2 * planes, 1, -1).transpose(1, 2, 0, 3)
    grad_gains = jnp.broadcast_to(grad_gains, (2 * planes, size) + grad_gains.shape[2:])
    grad_gains = grad_gains.reshape((-1,) + grad_gains.shape[2:])
    ring.going, qkv_s.first, qkv_s.middle, out_s.blocks = tied(
        ring.going, qkv_s.first, qkv_s.middle, out_s.blocks
    )
    ring.go()
    qkv_s.sums()
    out_s.both()
    grad_up = up_s.result()
    ring.going, qkv_s.last, out_s.first, out_s.middle, grad_up, grad_gains = tied(
        ring.going, qkv_s.last, out_s.first, out_s.middle, grad_up, grad_gains
    )
    ring.go()
    out_s.sums()
    grad_gains = lax.all_to_all(grad_gains, ("fsdp", "ctx", "tp"), 0, 0, tiled=True)
    grad_qkv = qkv_s.result()
    ring.going, out_s.last, grad_qkv = tied(ring.going, out_s.last, grad_qkv)
    ring.go()
    grad_out = out_s.result().T
    ring.going, grad_out = tied(ring.going, grad_out)
    ring.go()
    dattn_in, grad_gains = tied(ring.finish(), grad_gains)
    grad_gains = jnp.sum(grad_gains, 0)
    dattn_in = dattn_in.astype(F32)
    grad_input = dafter + norm_back(dattn_in * scale_one, normed_one, factor_one)
    grad_input = grad_input.astype(BF)
    return (
        output.reshape(hidden_in.shape),
        grad_input.reshape(hidden_in.shape),
        grad_qkv[:, :q_cols],
        grad_qkv[:, q_cols : q_cols + kv_cols],
        grad_qkv[:, q_cols + kv_cols :],
        grad_out,
        grad_gate,
        grad_up,
        grad_down,
        grad_gains[0],
        grad_gains[1],
        grad_gains[2],
        grad_gains[3],
    )


def general_body(
    hidden_in,
    lengths,
    query_weight,
    key_weight,
    value_weight,
    w_out,
    w_gate,
    w_up,
    w_down,
    gain_attn_in,
    gain_attn_out,
    gain_ffn_in,
    gain_ffn_out,
    cotangent,
):
    seqs_here, tok_here, width = hidden_in.shape
    row_count = seqs_here * tok_here
    head_groups = QUERY_HEADS // KEY_VALUE_HEADS
    gathered = (
        lax.all_gather(query_weight, ("fsdp", "ctx"), axis=0, tiled=True),
        lax.all_gather(key_weight, ("fsdp", "ctx"), axis=0, tiled=True),
        lax.all_gather(value_weight, ("fsdp", "ctx"), axis=0, tiled=True),
        lax.all_gather(w_out, ("fsdp", "ctx"), axis=1, tiled=True),
        lax.all_gather(w_gate, ("fsdp", "ctx"), axis=0, tiled=True),
        lax.all_gather(w_up, ("fsdp", "ctx"), axis=0, tiled=True),
        lax.all_gather(w_down, ("fsdp", "ctx"), axis=1, tiled=True),
        lax.all_gather(gain_attn_in, ("fsdp", "ctx"), axis=0, tiled=True),
        lax.all_gather(gain_attn_out, ("fsdp", "ctx"), axis=0, tiled=True),
        lax.all_gather(gain_ffn_in, ("fsdp", "ctx"), axis=0, tiled=True),
        lax.all_gather(gain_ffn_out, ("fsdp", "ctx"), axis=0, tiled=True),
    )
    query_full, key_full, value_full, out_full, gate_full, up_full, down_full = gathered[:7]
    scale_one = 1.0 + gathered[7].astype(jnp.float32)
    scale_two = 1.0 + gathered[8].astype(jnp.float32)
    scale_three = 1.0 + gathered[9].astype(jnp.float32)
    scale_four = 1.0 + gathered[10].astype(jnp.float32)
    kv_local = key_full.shape[1] // HEAD_SIZE
    own_start = lax.axis_index("ctx") * tok_here
    query_pos = own_start + jnp.arange(tok_here, dtype=jnp.int32)
    key_pos = jnp.arange(SEQUENCE_SLOTS, dtype=jnp.int32)
    valid = query_pos[None, :] < lengths[:, None]
    allowed = (
        (key_pos[None, None, :] <= query_pos[None, :, None])
        & (key_pos[None, None, :] < lengths[:, None, None])
    )[:, None, None]
    flat_in = hidden_in.astype(jnp.float32).reshape(row_count, width)
    normed_one, factor_one = normalize(flat_in)
    attention_input = (normed_one * scale_one).astype(jnp.bfloat16)
    query_b = plain_dot(attention_input, query_full).astype(jnp.bfloat16)
    key_b = (
        plain_dot(attention_input, key_full)
        .astype(jnp.bfloat16)
        .reshape(seqs_here, tok_here, kv_local * HEAD_SIZE)
    )
    value_b = (
        plain_dot(attention_input, value_full)
        .astype(jnp.bfloat16)
        .reshape(seqs_here, tok_here, kv_local * HEAD_SIZE)
    )
    key_all, value_all = (
        lax.all_gather(key_b, "ctx", axis=1, tiled=True),
        lax.all_gather(value_b, "ctx", axis=1, tiled=True),
    )
    query_five = query_b.reshape(seqs_here, tok_here, kv_local, head_groups, HEAD_SIZE)
    key_four = key_all.reshape(seqs_here, SEQUENCE_SLOTS, kv_local, HEAD_SIZE)
    value_four = value_all.reshape(seqs_here, SEQUENCE_SLOTS, kv_local, HEAD_SIZE)
    raw = (
        jnp.einsum("stkgd,sukd->skgtu", query_five, key_four, preferred_element_type=jnp.float32)
        * QSCALE
    )
    bent = jnp.tanh(raw / CAP)
    masked = jnp.where(allowed, CAP * bent, NEG)
    largest = jnp.max(masked, -1, keepdims=True)
    logsum = largest + jnp.log(jnp.sum(jnp.exp(masked - largest), -1, keepdims=True))
    probs = jnp.exp(masked - logsum)
    probs_b = probs.astype(jnp.bfloat16)
    attended = (
        jnp.einsum("skgtu,sukd->stkgd", probs_b, value_four, preferred_element_type=jnp.float32)
        .astype(jnp.bfloat16)
        .reshape(row_count, -1)
    )
    attn = lax.psum(plain_dot(attended, out_full).astype(jnp.bfloat16), "tp").astype(jnp.float32)
    normed_two, factor_two = normalize(attn)
    after_attn = flat_in + normed_two * scale_two
    normed_three, factor_three = normalize(after_attn)
    ffn_in = (normed_three * scale_three).astype(jnp.bfloat16)
    gate = plain_dot(ffn_in, gate_full)
    upward = plain_dot(ffn_in, up_full)
    activated, gelu_pull = jax.vjp(gelu_tanh, gate)
    hidden_b = (activated * upward).astype(jnp.bfloat16)
    ffn_out = lax.psum(plain_dot(hidden_b, down_full).astype(jnp.bfloat16), "tp").astype(
        jnp.float32
    )
    normed_four, factor_four = normalize(ffn_out)
    result = after_attn + normed_four * scale_four
    cot = cotangent.astype(jnp.float32).reshape(row_count, width) * valid.reshape(
        row_count, 1
    ).astype(jnp.float32)
    query_back, key_back, value_back, out_back, gate_back, up_back, down_back = (
        lax.all_gather(query_weight, ("fsdp", "ctx"), axis=0, tiled=True),
        lax.all_gather(key_weight, ("fsdp", "ctx"), axis=0, tiled=True),
        lax.all_gather(value_weight, ("fsdp", "ctx"), axis=0, tiled=True),
        lax.all_gather(w_out, ("fsdp", "ctx"), axis=1, tiled=True),
        lax.all_gather(w_gate, ("fsdp", "ctx"), axis=0, tiled=True),
        lax.all_gather(w_up, ("fsdp", "ctx"), axis=0, tiled=True),
        lax.all_gather(w_down, ("fsdp", "ctx"), axis=1, tiled=True),
    )
    grad_gain_four = jnp.sum(cot * normed_four, 0)
    dffn_b = norm_back(cot * scale_four, normed_four, factor_four).astype(jnp.bfloat16)
    grad_down = left_dot(hidden_b, dffn_b)
    dhidden = right_dot(dffn_b, down_back)
    dgate_b = gelu_pull(dhidden * upward)[0].astype(jnp.bfloat16)
    dup_b = (dhidden * activated).astype(jnp.bfloat16)
    grad_gate = left_dot(ffn_in, dgate_b)
    grad_up = left_dot(ffn_in, dup_b)
    dffn_in = lax.psum(
        (right_dot(dgate_b, gate_back) + right_dot(dup_b, up_back)).astype(jnp.bfloat16), "tp"
    ).astype(jnp.float32)
    grad_gain_three = jnp.sum(dffn_in * normed_three, 0)
    dafter = cot + norm_back(dffn_in * scale_three, normed_three, factor_three)
    grad_gain_two = jnp.sum(dafter * normed_two, 0)
    dattn_b = norm_back(dafter * scale_two, normed_two, factor_two).astype(jnp.bfloat16)
    grad_out = left_dot(attended, dattn_b)
    dattended = right_dot(dattn_b, out_back).astype(jnp.bfloat16).reshape(query_five.shape)
    dprobs = jnp.einsum(
        "stkgd,sukd->skgtu", dattended, value_four, preferred_element_type=jnp.float32
    )
    weighted = jnp.sum(probs * dprobs, -1, keepdims=True)
    draw_b = (probs * (dprobs - weighted) * (1.0 - bent * bent)).astype(jnp.bfloat16)
    dquery_b = (
        (
            jnp.einsum("skgtu,sukd->stkgd", draw_b, key_four, preferred_element_type=jnp.float32)
            * QSCALE
        )
        .astype(jnp.bfloat16)
        .reshape(row_count, -1)
    )
    dvalue_part = jnp.einsum(
        "skgtu,stkgd->sukd", probs_b, dattended, preferred_element_type=jnp.float32
    )
    dkey_part = (
        jnp.einsum("skgtu,stkgd->sukd", draw_b, query_five, preferred_element_type=jnp.float32)
        * QSCALE
    )
    dkey, dvalue = (
        lax.psum_scatter(
            dkey_part.astype(jnp.bfloat16), "ctx", scatter_dimension=1, tiled=True
        ).astype(jnp.float32),
        lax.psum_scatter(
            dvalue_part.astype(jnp.bfloat16), "ctx", scatter_dimension=1, tiled=True
        ).astype(jnp.float32),
    )
    dkey_b = dkey.astype(jnp.bfloat16).reshape(row_count, -1)
    dvalue_b = dvalue.astype(jnp.bfloat16).reshape(row_count, -1)
    grad_query = left_dot(attention_input, dquery_b)
    grad_key = left_dot(attention_input, dkey_b)
    grad_value = left_dot(attention_input, dvalue_b)
    dattn_in = lax.psum(
        (
            right_dot(dquery_b, query_back)
            + right_dot(dkey_b, key_back)
            + right_dot(dvalue_b, value_back)
        ).astype(jnp.bfloat16),
        "tp",
    ).astype(jnp.float32)
    grad_gain_one = jnp.sum(dattn_in * normed_one, 0)
    grad_input = dafter + norm_back(dattn_in * scale_one, normed_one, factor_one)
    summed = (
        lax.psum_scatter(
            grad_query.astype(jnp.bfloat16), ("fsdp", "ctx"), scatter_dimension=0, tiled=True
        ).astype(jnp.float32),
        lax.psum_scatter(
            grad_key.astype(jnp.bfloat16), ("fsdp", "ctx"), scatter_dimension=0, tiled=True
        ).astype(jnp.float32),
        lax.psum_scatter(
            grad_value.astype(jnp.bfloat16), ("fsdp", "ctx"), scatter_dimension=0, tiled=True
        ).astype(jnp.float32),
        lax.psum_scatter(
            grad_out.astype(jnp.bfloat16), ("fsdp", "ctx"), scatter_dimension=1, tiled=True
        ).astype(jnp.float32),
        lax.psum_scatter(
            grad_gate.astype(jnp.bfloat16), ("fsdp", "ctx"), scatter_dimension=0, tiled=True
        ).astype(jnp.float32),
        lax.psum_scatter(
            grad_up.astype(jnp.bfloat16), ("fsdp", "ctx"), scatter_dimension=0, tiled=True
        ).astype(jnp.float32),
        lax.psum_scatter(
            grad_down.astype(jnp.bfloat16), ("fsdp", "ctx"), scatter_dimension=1, tiled=True
        ).astype(jnp.float32),
        lax.psum_scatter(
            grad_gain_one.astype(jnp.bfloat16), ("fsdp", "ctx"), scatter_dimension=0, tiled=True
        ).astype(jnp.float32),
        lax.psum_scatter(
            grad_gain_two.astype(jnp.bfloat16), ("fsdp", "ctx"), scatter_dimension=0, tiled=True
        ).astype(jnp.float32),
        lax.psum_scatter(
            grad_gain_three.astype(jnp.bfloat16), ("fsdp", "ctx"), scatter_dimension=0, tiled=True
        ).astype(jnp.float32),
        lax.psum_scatter(
            grad_gain_four.astype(jnp.bfloat16), ("fsdp", "ctx"), scatter_dimension=0, tiled=True
        ).astype(jnp.float32),
    )
    return (
        result.astype(jnp.bfloat16).reshape(hidden_in.shape),
        grad_input.astype(jnp.bfloat16).reshape(hidden_in.shape),
        summed[0],
        summed[1],
        summed[2],
        summed[3],
        summed[4],
        summed[5],
        summed[6],
        summed[7],
        summed[8],
        summed[9],
        summed[10],
    )


def solution(mesh):
    square = mesh.shape["ctx"] == 4 and mesh.shape["fsdp"] == 2
    return jax.shard_map(
        plane_body if square else general_body,
        mesh=mesh,
        in_specs=(
            P("fsdp", "ctx", None),
            P("fsdp"),
            P(("fsdp", "ctx"), "tp"),
            P(("fsdp", "ctx"), "tp"),
            P(("fsdp", "ctx"), "tp"),
            P("tp", ("fsdp", "ctx")),
            P(("fsdp", "ctx"), "tp"),
            P(("fsdp", "ctx"), "tp"),
            P("tp", ("fsdp", "ctx")),
            P(("fsdp", "ctx")),
            P(("fsdp", "ctx")),
            P(("fsdp", "ctx")),
            P(("fsdp", "ctx")),
            P("fsdp", "ctx", None),
        ),
        out_specs=(
            P("fsdp", "ctx", None),
            P("fsdp", "ctx", None),
            P(("fsdp", "ctx"), "tp"),
            P(("fsdp", "ctx"), "tp"),
            P(("fsdp", "ctx"), "tp"),
            P("tp", ("fsdp", "ctx")),
            P(("fsdp", "ctx"), "tp"),
            P(("fsdp", "ctx"), "tp"),
            P("tp", ("fsdp", "ctx")),
            P(("fsdp", "ctx")),
            P(("fsdp", "ctx")),
            P(("fsdp", "ctx")),
            P(("fsdp", "ctx")),
        ),
        check_vma=False,
    )
```

```python
import jax
import jax.numpy as jnp
from jax import lax
from jax.experimental import pallas as pl
from jax.experimental.pallas import tpu as pltpu
from jax.sharding import PartitionSpec as P

QUERY_HEADS = 8
KEY_VALUE_HEADS = 4
HEAD_SIZE = 256
SEQUENCE_SLOTS = 2048


EPS = 1e-06
CAP = 50.0
QSCALE = 0.0625
NEG = -1e30


def normalize(value_rows):
    factor = lax.rsqrt(jnp.mean(value_rows * value_rows, -1, keepdims=True) + EPS)
    return (value_rows * factor, factor)


def norm_back(grad_hat, normed, factor):
    return factor * (grad_hat - normed * jnp.mean(grad_hat * normed, -1, keepdims=True))


def plain_dot(first, second):
    return jnp.dot(first, second, preferred_element_type=jnp.float32)


def left_dot(first, second):
    return lax.dot_general(
        first, second, (((0,), (0,)), ((), ())), preferred_element_type=jnp.float32
    )


def right_dot(first, second):
    return lax.dot_general(
        first, second, (((1,), (1,)), ((), ())), preferred_element_type=jnp.float32
    )


def gelu_tanh(value_rows):
    return jax.nn.gelu(value_rows, approximate=True)


BF = jnp.bfloat16
F32 = jnp.float32

LINKS = {
    "x": ("ctx", [(0, 1), (1, 0), (2, 3), (3, 2)]),
    "y": ("ctx", [(0, 2), (2, 0), (1, 3), (3, 1)]),
    "diagonal": ("ctx", [(0, 3), (3, 0), (1, 2), (2, 1)]),
    "core": ("fsdp", [(0, 1), (1, 0)]),
}
ORDER = [(0, 0), (0, 1), (1, 1), (2, 0), (1, 0), (3, 0), (3, 1), (2, 1)]


def tied(*values):
    return lax.optimization_barrier(values)


def send(link, value):
    return lax.ppermute(value, *LINKS[link])


def around(value, by=1):
    size = lax.axis_size("tp")
    return lax.ppermute(value, "tp", [(i, (i + by) % size) for i in range(size)])


def place(pieces, starts):
    rows = sum(piece.shape[0] for piece in pieces)
    whole = jnp.zeros((rows,) + pieces[0].shape[1:], pieces[0].dtype)
    for piece, start in zip(pieces, starts):
        whole = lax.dynamic_update_slice_in_dim(whole, piece, start, 0)
    return whole


def halves(block):
    half = block.shape[0] // 2
    return block[:half], block[half:]


class Scatter:
    def __init__(self, blocks):
        self.blocks = blocks
        self.half = blocks[1].shape[0]

    def diagonal(self):
        self.first = (send("x", self.blocks[2]), send("y", self.blocks[3]))

    def both(self):
        half = self.half = self.blocks[1].shape[0] // 2
        from_x, from_y = send("x", self.blocks[1]), send("y", self.blocks[2])
        self.first, self.middle = (from_x[half:], from_y[:half]), (from_x[:half], from_y[half:])

    def direct(self):
        self.middle = (send("x", self.blocks[1]), send("y", self.blocks[4]))

    def sums(self):
        half, kept, (d_top, d_low) = self.half, self.blocks[0], self.first
        x_low, y_top = kept[2 * half : 3 * half], kept[3 * half :]
        self.last = (
            send("x", (x_low.astype(F32) + d_low.astype(F32)).astype(BF)),
            send("y", (y_top.astype(F32) + d_top.astype(F32)).astype(BF)),
        )

    def result(self):
        half, kept = self.half, self.blocks[0]
        (x_top, y_low), (x_low, y_top) = self.middle, self.last
        top = kept[:half].astype(F32) + x_top.astype(F32) + y_top.astype(F32)
        low = kept[half : 2 * half].astype(F32) + y_low.astype(F32) + x_low.astype(F32)
        return jnp.concatenate([top, low], 0)


class Ring:
    def __init__(self, value, parts=1):
        self.value, self.step, self.parts = value, 0, parts
        self.size, self.me = lax.axis_size("tp"), lax.axis_index("tp")
        self.rows = value.shape[0] // (parts * self.size)
        self.whole = jnp.zeros_like(value)
        self.sent = [self.block(part, self.me - 1) for part in range(parts)]
        self.going = [around(sent) for sent in self.sent]

    def start(self, part, index):
        return (part * self.size + (index + self.size) % self.size) * self.rows

    def block(self, part, index):
        return lax.dynamic_slice_in_dim(self.value, self.start(part, index), self.rows, 0)

    def go(self):
        self.step += 1
        for part in range(self.parts):
            going = self.going[part]
            if self.parts > 1:
                going, _ = tied(going, self.sent[1 - part])
            if self.step < self.size:
                own = self.block(part, self.me - 1 - self.step)
                going = (going.astype(F32) + own.astype(F32)).astype(BF)
            if self.step >= self.size - 1:
                at = self.start(part, self.me - self.step + self.size - 1)
                self.whole = lax.dynamic_update_slice_in_dim(self.whole, going, at, 0)
            if self.step < 2 * self.size - 2:
                self.sent[part] = going
                self.going[part] = around(going)

    def finish(self):
        while self.step < 2 * self.size - 2:
            self.go()
        return self.whole


VMEM_BYTES = 56 * 2**20


def kernel_params():
    return pltpu.CompilerParams(vmem_limit_bytes=VMEM_BYTES)


def cut_of(size):
    return next((cut for cut in (768, 512) if size % cut == 0), size)


def rowwise(fn, rows, vectors, dtypes, sums=0, block=128):
    count, width = rows[0].shape
    n_in, n_out = len(rows) + len(vectors), len(dtypes)

    def kernel(*refs):
        results = fn(*(ref[...] for ref in refs[:n_in]))
        for ref, value in zip(refs[n_in : n_in + n_out], results):
            ref[...] = value.astype(ref.dtype)
        for ref, value in zip(refs[n_in + n_out :], results[n_out:]):
            part = jnp.sum(value.reshape(block // 8, 8, width), 0)

            @pl.when(pl.program_id(0) == 0)
            def _():
                ref[...] = part

            @pl.when(pl.program_id(0) > 0)
            def _():
                ref[...] += part

    by_row = pl.BlockSpec((block, width), lambda i: (i, 0))
    return pl.pallas_call(
        kernel,
        grid=(count // block,),
        in_specs=[by_row] * len(rows) + [pl.BlockSpec((1, width), lambda i: (0, 0))] * len(vectors),
        out_specs=[by_row] * n_out + [pl.BlockSpec((8, width), lambda i: (0, 0))] * sums,
        out_shape=[jax.ShapeDtypeStruct((count, width), dtype) for dtype in dtypes]
        + [jax.ShapeDtypeStruct((8, width), F32)] * sums,
        compiler_params=kernel_params(),
        cost_estimate=pl.CostEstimate(
            flops=20 * count * width, bytes_accessed=4 * count * width * n_in, transcendentals=0
        ),
    )(*rows, *vectors)


ROOT = 0.7978845608028654


def gelu_parts(z):
    bend = jnp.tanh(ROOT * (z + 0.044715 * (z * z * z)))
    value = 0.5 * z * (1.0 + bend)
    slope = 0.5 * (1.0 + bend) + 0.5 * z * (1.0 - bend * bend) * (
        ROOT * (1.0 + (3.0 * 0.044715) * (z * z))
    )
    return value, slope


def ffn_forward(x, weights, down_rest):
    count, width = x.shape
    cut, out_cut = down_rest.shape[1], cut_of(width)
    units = (weights.shape[1] + cut) // 3
    first = units // cut

    def kernel(x_ref, gate_w, up_w, down_w, rest_w, gate_ref, up_ref, hidden_ref, out_ref, kept):
        step = pl.program_id(0)

        @pl.when(step < first)
        def _():
            gate = plain_dot(x_ref[...], gate_w[...])
            up = plain_dot(x_ref[...], up_w[...])
            hidden = (gelu_parts(gate)[0] * up).astype(BF)
            gate_ref[...] = gate
            up_ref[...] = up
            hidden_ref[...] = hidden
            kept[step] = hidden

        @pl.when(step >= first)
        def _():
            total = right_dot(kept[first - 1], rest_w[...])
            for i in range(first - 1):
                total += right_dot(kept[i], down_w[:, i * cut : (i + 1) * cut])
            out_ref[...] = total.astype(BF)

    def early(j):
        return jnp.minimum(j, first - 1)

    def late(j):
        return jnp.maximum(j - first, 0)

    out = pl.BlockSpec((count, cut), lambda j: (0, early(j)))
    return pl.pallas_call(
        kernel,
        grid=(first + width // out_cut,),
        in_specs=[
            pl.BlockSpec((count, width), lambda j: (0, 0)),
            pl.BlockSpec((width, cut), lambda j: (0, early(j))),
            pl.BlockSpec((width, cut), lambda j: (0, early(j) + first)),
            pl.BlockSpec((out_cut, units - cut), lambda j: (late(j), 3)),
            pl.BlockSpec((out_cut, cut), lambda j: (late(j), 0)),
        ],
        out_specs=[out] * 3 + [pl.BlockSpec((count, out_cut), lambda j: (0, late(j)))],
        out_shape=[
            jax.ShapeDtypeStruct((count, units), F32),
            jax.ShapeDtypeStruct((count, units), F32),
            jax.ShapeDtypeStruct((count, units), BF),
            jax.ShapeDtypeStruct((count, width), BF),
        ],
        scratch_shapes=[pltpu.VMEM((first, count, cut), BF)],
        compiler_params=kernel_params(),
        cost_estimate=pl.CostEstimate(
            flops=6 * count * width * units,
            bytes_accessed=6 * width * units + 10 * count * units,
            transcendentals=count * units,
        ),
    )(x, weights, weights, weights, down_rest)


def ffn_backward(dffn, weights, down_rest, gate, up):
    count, width = dffn.shape
    units = gate.shape[1]
    cut, out_cut = down_rest.shape[1], cut_of(width)
    first = units // cut

    def kernel(
        d_ref,
        down_w,
        rest_w,
        gate_ref,
        up_ref,
        gate_w,
        up_w,
        dgate_ref,
        dup_ref,
        out_ref,
        kept,
        kept_up,
    ):
        step = pl.program_id(0)

        def make(weight):
            dhidden = plain_dot(d_ref[...], weight[...])
            value, slope = gelu_parts(gate_ref[...])
            dgate = (dhidden * up_ref[...] * slope).astype(BF)
            dup = (dhidden * value).astype(BF)
            dgate_ref[...] = dgate
            dup_ref[...] = dup
            kept[step] = dgate
            kept_up[step] = dup

        pl.when(step < first - 1)(lambda: make(down_w))
        pl.when(step == first - 1)(lambda: make(rest_w))

        @pl.when(step >= first)
        def _():
            out_ref[...] = sum(
                right_dot(terms[i], weight[:, i * cut : (i + 1) * cut])
                for i in range(first)
                for terms, weight in ((kept, gate_w), (kept_up, up_w))
            ).astype(BF)

    def early(j):
        return jnp.minimum(j, first - 1)

    def late(j):
        return jnp.maximum(j - first, 0)

    by_cut = pl.BlockSpec((count, cut), lambda j: (0, early(j)))
    return pl.pallas_call(
        kernel,
        grid=(first + width // out_cut,),
        in_specs=[
            pl.BlockSpec((count, width), lambda j: (0, 0)),
            pl.BlockSpec((width, cut), lambda j: (0, jnp.minimum(j, first - 2) + 2 * first)),
            pl.BlockSpec((width, cut), lambda j: (0, 0)),
            by_cut,
            by_cut,
            pl.BlockSpec((out_cut, units), lambda j: (late(j), 0)),
            pl.BlockSpec((out_cut, units), lambda j: (late(j), 1)),
        ],
        out_specs=[by_cut] * 2 + [pl.BlockSpec((count, out_cut), lambda j: (0, late(j)))],
        out_shape=[jax.ShapeDtypeStruct((count, units), BF)] * 2
        + [jax.ShapeDtypeStruct((count, width), BF)],
        scratch_shapes=[pltpu.VMEM((first, count, cut), BF)] * 2,
        compiler_params=kernel_params(),
        cost_estimate=pl.CostEstimate(
            flops=6 * count * width * units,
            bytes_accessed=6 * width * units + 12 * count * units,
            transcendentals=count * units,
        ),
    )(dffn, weights, down_rest, gate, up, weights, weights)


def weight_grad(rows, rows_far, cols, cols_far, joined=False):
    count, half_width = rows_far.shape
    width = cols.shape[1]
    cut = cut_of(width)
    half = half_width // 8
    place = jnp.stack([lax.axis_index("fsdp"), lax.axis_index("ctx")]).astype(jnp.int32)
    sizes = (4 * half, 2 * half, 2 * half) if joined else (4 * half,) + (half,) * 4

    def kernel(
        place_ref, near_ref, far_ref, cols_ref, cols_far_ref, *rest
    ):
        outs, (near_t, far_t, total) = rest[: len(sizes)], rest[len(sizes) :]

        @pl.when(pl.program_id(0) == 0)
        def _():
            near_t[...] = near_ref[...].T
            far_t[...] = far_ref[...].T

        total[...] = plain_dot(near_t[...], cols_ref[...]) + plain_dot(
            far_t[...], cols_far_ref[...]
        )
        for index, (k, low) in enumerate(ORDER):
            start = (lax.bitwise_xor(place_ref[1], k) * 2 + low) * half
            block = total[pl.ds(pl.multiple_of(start, 16), half), :].astype(BF)
            if index < 4:
                out, at = outs[0], index
            elif joined:
                out, at = outs[1 + (index - 4) // 2], index % 2
            else:
                out, at = outs[index - 3], 0
            out[at * half : (at + 1) * half, :] = block

    by_cut = pl.BlockSpec((count, cut), lambda j, place: (0, j))
    return pl.pallas_call(
        kernel,
        grid_spec=pltpu.PrefetchScalarGridSpec(
            num_scalar_prefetch=1,
            grid=(width // cut,),
            in_specs=[
                pl.BlockSpec((count, half_width), lambda j, place: (0, place[0])),
                pl.BlockSpec((count, half_width), lambda j, place: (0, 0)),
                by_cut,
                by_cut,
            ],
            out_specs=[pl.BlockSpec((size, cut), lambda j, place: (0, j)) for size in sizes],
            scratch_shapes=[
                pltpu.VMEM((half_width, count), BF),
                pltpu.VMEM((half_width, count), BF),
                pltpu.VMEM((half_width, cut), F32),
            ],
        ),
        out_shape=[jax.ShapeDtypeStruct((size, width), BF) for size in sizes],
        compiler_params=kernel_params(),
        cost_estimate=pl.CostEstimate(
            flops=4 * count * half_width * width,
            bytes_accessed=2 * half_width * width + 4 * count * (width + half_width),
            transcendentals=0,
        ),
    )(place, rows, rows_far, cols, cols_far)


def attention_back(query, dattended, attended, kv, logsum, length):
    tokens, columns = query.shape
    heads, blocks = columns // HEAD_SIZE, kv.shape[0] // tokens
    scalars = jnp.stack([lax.axis_index("ctx").astype(jnp.int32), length])

    def kernel(scalars_ref, q_ref, d_ref, a_ref, kv_ref, log_ref, dq_ref, dkv_ref, dq, dk, dv):
        block, head = pl.program_id(0), pl.program_id(1)
        q, d = q_ref[...], d_ref[...]
        key, value = kv_ref[:, :HEAD_SIZE], kv_ref[:, HEAD_SIZE:]
        me = scalars_ref[0]
        bent = jnp.tanh(right_dot(q, key) * (QSCALE / CAP))
        shape = (tokens, tokens)
        key_pos = lax.bitwise_xor(me, block) * tokens + lax.broadcasted_iota(jnp.int32, shape, 1)
        query_pos = me * tokens + lax.broadcasted_iota(jnp.int32, shape, 0)
        allowed = (key_pos <= query_pos) & (key_pos < scalars_ref[1])
        probs = jnp.where(allowed, jnp.exp(CAP * bent - log_ref[...]), 0.0)
        weighted = jnp.sum(d.astype(F32) * a_ref[...].astype(F32), -1, keepdims=True)
        draw = (probs * (right_dot(d, value) - weighted) * (1.0 - bent * bent)).astype(BF)
        dk_part, dv_part = left_dot(draw, q), left_dot(probs.astype(BF), d)
        dq_part = plain_dot(draw, key)

        @pl.when(head == 0)
        def _():
            dk[...] = dk_part
            dv[...] = dv_part

        @pl.when(head > 0)
        def _():
            dk[...] += dk_part
            dv[...] += dv_part

        @pl.when(block == 0)
        def _():
            dq[head] = dq_part

        @pl.when(block > 0)
        def _():
            dq[head] += dq_part

        @pl.when(head == heads - 1)
        def _():
            dkv_ref[:, :HEAD_SIZE] = (dk[...] * QSCALE).astype(BF)
            dkv_ref[:, HEAD_SIZE:] = dv[...].astype(BF)

        @pl.when((block == blocks - 1) & (head == heads - 1))
        def _():
            for i in range(heads):
                dq_ref[:, i * HEAD_SIZE : (i + 1) * HEAD_SIZE] = (dq[i] * QSCALE).astype(BF)

    by_head = pl.BlockSpec((tokens, HEAD_SIZE), lambda b, h, scalars: (0, h))
    return pl.pallas_call(
        kernel,
        grid_spec=pltpu.PrefetchScalarGridSpec(
            num_scalar_prefetch=1,
            grid=(blocks, heads),
            in_specs=[
                by_head,
                by_head,
                by_head,
                pl.BlockSpec((tokens, 2 * HEAD_SIZE), lambda b, h, scalars: (b, 0)),
                pl.BlockSpec((None, tokens, 1), lambda b, h, scalars: (h, 0, 0)),
            ],
            out_specs=[
                pl.BlockSpec((tokens, columns), lambda b, h, scalars: (0, 0)),
                pl.BlockSpec((None, tokens, 2 * HEAD_SIZE), lambda b, h, scalars: (b, 0, 0)),
            ],
            scratch_shapes=[
                pltpu.VMEM((heads, tokens, HEAD_SIZE), F32),
                pltpu.VMEM((tokens, HEAD_SIZE), F32),
                pltpu.VMEM((tokens, HEAD_SIZE), F32),
            ],
        ),
        out_shape=[
            jax.ShapeDtypeStruct((tokens, columns), BF),
            jax.ShapeDtypeStruct((blocks, tokens, 2 * HEAD_SIZE), BF),
        ],
        compiler_params=kernel_params(),
        cost_estimate=pl.CostEstimate(
            flops=10 * tokens * tokens * blocks * columns,
            bytes_accessed=8 * tokens * columns * blocks,
            transcendentals=2 * tokens * tokens * blocks * heads,
        ),
    )(scalars, query, dattended, attended, kv, logsum)


def residual_rows(attn, hidden, scale_two, scale_three):
    attn, hidden = attn.astype(F32), hidden.astype(F32)
    after = hidden + normalize(attn)[0] * scale_two
    return after, normalize(after)[0] * scale_three


def output_rows(ffn_out, after, cot, scale_four):
    normed, factor = normalize(ffn_out.astype(F32))
    cot = cot.astype(F32)
    return (
        after + normed * scale_four,
        norm_back(cot * scale_four, normed, factor),
        cot * normed,
    )


def residual_back_rows(dffn_in, after, attn, cot, scale_three, scale_two):
    dffn_in = dffn_in.astype(F32)
    normed, factor = normalize(after)
    dafter = cot.astype(F32) + norm_back(dffn_in * scale_three, normed, factor)
    normed_two, factor_two = normalize(attn.astype(F32))
    dattn = norm_back(dafter * scale_two, normed_two, factor_two)
    return dafter, dattn, dffn_in * normed, dafter * normed_two


def input_back_rows(dattn_in, hidden, dafter, scale_one):
    normed, factor = normalize(hidden.astype(F32))
    return (dafter + norm_back(dattn_in.astype(F32) * scale_one, normed, factor),)


def plane_body(
    hidden_in,
    lengths,
    query_weight,
    key_weight,
    value_weight,
    w_out,
    w_gate,
    w_up,
    w_down,
    gain_attn_in,
    gain_attn_out,
    gain_ffn_in,
    gain_ffn_out,
    cotangent,
):
    seqs_here, tok_here, width = hidden_in.shape
    row_count = seqs_here * tok_here
    head_groups = QUERY_HEADS // KEY_VALUE_HEADS
    half_width = width // 2
    q_cols, kv_cols = query_weight.shape[1], key_weight.shape[1]
    size = lax.axis_size("tp")
    kv_local = kv_cols // HEAD_SIZE
    planes, me = lax.axis_size("ctx"), lax.axis_index("ctx")

    core = lax.axis_index("fsdp")

    def gather(shard):
        return lax.all_gather(shard, ("fsdp", "ctx"), axis=0, tiled=True)

    def far_half(rows):
        return send("core", lax.dynamic_slice_in_dim(rows, (1 - core) * half_width, half_width, 1))

    attention_shards = jnp.concatenate([query_weight, key_weight, value_weight, w_out.T], 1)
    attention_w = gather(attention_shards)
    late = w_down.shape[0] - cut_of(w_down.shape[0])
    ffn_shards = jnp.concatenate([w_gate, w_up, w_down[:late].T], 1)
    rest_t = w_down[late:].T
    rest_x, rest_y = send("x", rest_t), send("y", rest_t)
    gains = jnp.stack([gain_attn_in, gain_attn_out, gain_ffn_in, gain_ffn_out])[None]
    gains = jnp.broadcast_to(gains, (2 * planes,) + gains.shape[1:])
    gains = lax.all_to_all(gains, ("fsdp", "ctx"), 0, 0, tiled=True)
    gains = gains.transpose(1, 0, 2).reshape(4, width).astype(F32)
    scale_one, scale_two, scale_three, scale_four = (1.0 + gains[i][None] for i in range(4))
    flat_in = hidden_in.astype(F32).reshape(row_count, width)
    normed_one, factor_one = normalize(flat_in)
    attention_input = (normed_one * scale_one).astype(BF)

    attention_w, attention_input, ffn_shards, rest_x, rest_y = tied(
        attention_w, attention_input, ffn_shards, rest_x, rest_y
    )
    ffn_w = gather(ffn_shards)
    qkv_cols = q_cols + 2 * kv_cols
    qkv_w, out_w = attention_w[:, :qkv_cols], attention_w[:, qkv_cols:]
    run = jnp.arange(tok_here, dtype=jnp.int32)
    query_pos = me * tok_here + run
    key_pos = jnp.concatenate([(me ^ k) * tok_here + run for k in range(planes)])
    valid = query_pos[None, :] < lengths[:, None]
    allowed = (
        (key_pos[None, None, :] <= query_pos[None, :, None])
        & (key_pos[None, None, :] < lengths[:, None, None])
    )[:, None, None]
    qkv = plain_dot(attention_input, qkv_w).astype(BF)
    query_b = qkv[:, :q_cols]
    kv = qkv[:, q_cols:].reshape(seqs_here, tok_here, 2 * kv_cols)
    kv_all = jnp.concatenate([kv, send("x", kv), send("y", kv), send("diagonal", kv)], 1)
    kv_all, rest_x, rest_y = tied(kv_all, rest_x, rest_y)
    rest_last = [send("y", halves(rest_x)[0]), send("x", halves(rest_y)[1])]
    query_five = query_b.reshape(seqs_here, tok_here, kv_local, head_groups, HEAD_SIZE)
    key_four = kv_all[:, :, :kv_cols].reshape(seqs_here, SEQUENCE_SLOTS, kv_local, HEAD_SIZE)
    value_four = kv_all[:, :, kv_cols:].reshape(seqs_here, SEQUENCE_SLOTS, kv_local, HEAD_SIZE)
    raw = jnp.einsum("stkgd,sukd->skgtu", query_five, key_four, preferred_element_type=F32) * QSCALE
    bent = jnp.tanh(raw / CAP)
    masked = jnp.where(allowed, CAP * bent, NEG)
    largest = jnp.max(masked, -1, keepdims=True)
    logsum = largest + jnp.log(jnp.sum(jnp.exp(masked - largest), -1, keepdims=True))
    probs = jnp.exp(masked - logsum)
    probs_b = probs.astype(BF)
    attended = (
        jnp.einsum("skgtu,sukd->stkgd", probs_b, value_four, preferred_element_type=F32)
        .astype(BF)
        .reshape(row_count, -1)
    )
    attended, rest_last = tied(attended, rest_last)
    attn = right_dot(attended, out_w).astype(BF)
    ring = Ring(attn, 2)
    ring.go()
    rows, start = rest_t.shape[0], [(me ^ k) * rest_t.shape[0] for k in range(4)]
    rest_near = place([rest_t, rest_x, rest_y, *rest_last], [*start, start[3] + rows // 2])
    ring.go()
    ring.going, rest_near = tied(ring.going, rest_near)
    rest_far = send("core", rest_near)
    ring.go()
    ring.go()
    ring.going[1], rest_far = tied(ring.going[1], rest_far)
    ring.go()
    down_rest = place([rest_near, rest_far], [core * half_width, (1 - core) * half_width])
    attn = ring.finish()
    hidden_rows = hidden_in.reshape(row_count, width)
    after_attn, ffn_in = rowwise(
        residual_rows, [attn, hidden_rows], [scale_two, scale_three], [F32, BF]
    )
    gate, upward, hidden_b, ffn_out = ffn_forward(ffn_in, ffn_w, down_rest)
    ffn_out, hidden_b, attended, ffn_in, attention_input, cotangent = tied(
        ffn_out, hidden_b, attended, ffn_in, attention_input, cotangent
    )
    ring = Ring(ffn_out, 2)

    hidden_far, attended_far = send("core", hidden_b), send("core", attended)
    ffn_in_far, attention_input_far = far_half(ffn_in), far_half(attention_input)
    cot = jnp.where(
        valid.reshape(row_count, 1), cotangent.reshape(row_count, width), jnp.zeros((), BF)
    )
    ring.go()
    ring.going[0], hidden_far, attended_far, ffn_in_far, attention_input_far, cot = tied(
        ring.going[0], hidden_far, attended_far, ffn_in_far, attention_input_far, cot
    )
    ffn_out = ring.finish()
    output, dffn_b, gain_four_rows = rowwise(
        output_rows, [ffn_out, after_attn, cot], [scale_four], [BF, BF], 1
    )
    dgate_b, dup_b, dffn_in = ffn_backward(
        dffn_b, ffn_w, down_rest, gate, upward
    )
    dffn_far = far_half(dffn_b)

    dffn_in, dffn_far, dgate_b, dup_b = tied(dffn_in, dffn_far, dgate_b, dup_b)
    ring = Ring(dffn_in)
    dgate_far = send("core", dgate_b)
    down_s = Scatter(weight_grad(dffn_b, dffn_far, hidden_b, hidden_far))
    ring.going, down_s.blocks, dgate_far = tied(ring.going, down_s.blocks, dgate_far)
    ring.go()
    down_s.diagonal()
    dup_far = send("core", dup_b)
    gate_s = Scatter(weight_grad(ffn_in, ffn_in_far, dgate_b, dgate_far))
    ring.going, gate_s.blocks, dup_far, down_s.first = tied(
        ring.going, gate_s.blocks, dup_far, down_s.first
    )
    ring.go()
    down_s.direct()
    up_s = Scatter(weight_grad(ffn_in, ffn_in_far, dup_b, dup_far))
    ring.going, up_s.blocks, down_s.middle = tied(ring.going, up_s.blocks, down_s.middle)
    ring.go()
    down_s.sums()
    ring.going, down_s.last, gate_s.blocks = tied(ring.going, down_s.last, gate_s.blocks)
    ring.go()
    gate_s.diagonal()
    grad_down = down_s.result().T
    ring.going, gate_s.first, grad_down = tied(ring.going, gate_s.first, grad_down)
    ring.go()
    gate_s.direct()
    dffn_in, up_s.blocks, gate_s.first, gate_s.middle = tied(
        ring.finish(), up_s.blocks, gate_s.first, gate_s.middle
    )
    gate_s.sums()
    up_s.diagonal()
    dafter, dattn_b, gain_three_rows, gain_two_rows = rowwise(
        residual_back_rows,
        [dffn_in, after_attn, attn, cot],
        [scale_three, scale_two],
        [F32, BF],
        2,
    )
    dattended = plain_dot(dattn_b, out_w).astype(BF)
    dattn_far = far_half(dattn_b)
    dattended, gate_s.last, up_s.first, up_s.blocks = tied(
        dattended, gate_s.last, up_s.first, up_s.blocks
    )
    up_s.direct()
    dquery_b, dkv = attention_back(
        query_b, dattended, attended, kv_all[0], logsum.reshape(head_groups, row_count, 1), lengths[0]
    )
    dkv, dattn_far, up_s.middle = tied(dkv, dattn_far, up_s.middle)
    dkv = [dkv[0], send("x", dkv[1]), send("y", dkv[2]), send("diagonal", dkv[3])]
    out_s = Scatter(weight_grad(dattn_b, dattn_far, attended, attended_far, True))
    grad_gate = gate_s.result()
    dkv, dquery_b, out_s.blocks, grad_gate, up_s.blocks = tied(
        dkv, dquery_b, out_s.blocks, grad_gate, up_s.blocks
    )
    dkv_b = sum(part.astype(F32) for part in dkv).astype(BF)
    dqkv_b = jnp.concatenate([dquery_b, dkv_b], 1)
    dattn_in = right_dot(dqkv_b, qkv_w)
    dattn_in, dqkv_b, dafter, up_s.blocks = tied(
        dattn_in.astype(BF), dqkv_b, dafter, up_s.blocks
    )

    ring = Ring(dattn_in)
    dqkv_far = send("core", dqkv_b)
    qkv_s = Scatter(
        weight_grad(attention_input, attention_input_far, dqkv_b, dqkv_far, True)
    )
    up_s.sums()
    gain_rows = gain_two_rows, gain_three_rows, gain_four_rows
    ring.going, qkv_s.blocks, up_s.last, gain_rows = tied(
        ring.going, qkv_s.blocks, up_s.last, gain_rows
    )
    ring.go()
    qkv_s.both()
    grad_gain_one = jnp.sum(dattn_in.astype(F32) * normed_one, 0)
    grad_gains = jnp.stack([grad_gain_one] + [jnp.sum(rows, 0) / size for rows in gain_rows])
    grad_gains = grad_gains.reshape(4, 2 * planes, 1, -1).transpose(1, 2, 0, 3)
    grad_gains = jnp.broadcast_to(grad_gains, (2 * planes, size) + grad_gains.shape[2:])
    grad_gains = grad_gains.reshape((-1,) + grad_gains.shape[2:])
    ring.going, qkv_s.first, qkv_s.middle, out_s.blocks = tied(
        ring.going, qkv_s.first, qkv_s.middle, out_s.blocks
    )
    ring.go()
    qkv_s.sums()
    out_s.both()
    grad_up = up_s.result()
    ring.going, qkv_s.last, out_s.first, out_s.middle, grad_up, grad_gains = tied(
        ring.going, qkv_s.last, out_s.first, out_s.middle, grad_up, grad_gains
    )
    ring.go()
    out_s.sums()
    grad_gains = lax.all_to_all(grad_gains, ("fsdp", "ctx", "tp"), 0, 0, tiled=True)
    grad_qkv = qkv_s.result()
    ring.going, out_s.last, grad_qkv = tied(ring.going, out_s.last, grad_qkv)
    ring.go()
    grad_out = out_s.result().T
    ring.going, grad_out = tied(ring.going, grad_out)
    ring.go()
    dattn_in, grad_gains = tied(ring.finish(), grad_gains)
    grad_gains = jnp.sum(grad_gains, 0)
    (grad_input,) = rowwise(input_back_rows, [dattn_in, hidden_rows, dafter], [scale_one], [BF])
    return (
        output.reshape(hidden_in.shape),
        grad_input.reshape(hidden_in.shape),
        grad_qkv[:, :q_cols],
        grad_qkv[:, q_cols : q_cols + kv_cols],
        grad_qkv[:, q_cols + kv_cols :],
        grad_out,
        grad_gate,
        grad_up,
        grad_down,
        grad_gains[0],
        grad_gains[1],
        grad_gains[2],
        grad_gains[3],
    )


def general_body(
    hidden_in,
    lengths,
    query_weight,
    key_weight,
    value_weight,
    w_out,
    w_gate,
    w_up,
    w_down,
    gain_attn_in,
    gain_attn_out,
    gain_ffn_in,
    gain_ffn_out,
    cotangent,
):
    seqs_here, tok_here, width = hidden_in.shape
    row_count = seqs_here * tok_here
    head_groups = QUERY_HEADS // KEY_VALUE_HEADS
    gathered = (
        lax.all_gather(query_weight, ("fsdp", "ctx"), axis=0, tiled=True),
        lax.all_gather(key_weight, ("fsdp", "ctx"), axis=0, tiled=True),
        lax.all_gather(value_weight, ("fsdp", "ctx"), axis=0, tiled=True),
        lax.all_gather(w_out, ("fsdp", "ctx"), axis=1, tiled=True),
        lax.all_gather(w_gate, ("fsdp", "ctx"), axis=0, tiled=True),
        lax.all_gather(w_up, ("fsdp", "ctx"), axis=0, tiled=True),
        lax.all_gather(w_down, ("fsdp", "ctx"), axis=1, tiled=True),
        lax.all_gather(gain_attn_in, ("fsdp", "ctx"), axis=0, tiled=True),
        lax.all_gather(gain_attn_out, ("fsdp", "ctx"), axis=0, tiled=True),
        lax.all_gather(gain_ffn_in, ("fsdp", "ctx"), axis=0, tiled=True),
        lax.all_gather(gain_ffn_out, ("fsdp", "ctx"), axis=0, tiled=True),
    )
    query_full, key_full, value_full, out_full, gate_full, up_full, down_full = gathered[:7]
    scale_one = 1.0 + gathered[7].astype(jnp.float32)
    scale_two = 1.0 + gathered[8].astype(jnp.float32)
    scale_three = 1.0 + gathered[9].astype(jnp.float32)
    scale_four = 1.0 + gathered[10].astype(jnp.float32)
    kv_local = key_full.shape[1] // HEAD_SIZE
    own_start = lax.axis_index("ctx") * tok_here
    query_pos = own_start + jnp.arange(tok_here, dtype=jnp.int32)
    key_pos = jnp.arange(SEQUENCE_SLOTS, dtype=jnp.int32)
    valid = query_pos[None, :] < lengths[:, None]
    allowed = (
        (key_pos[None, None, :] <= query_pos[None, :, None])
        & (key_pos[None, None, :] < lengths[:, None, None])
    )[:, None, None]
    flat_in = hidden_in.astype(jnp.float32).reshape(row_count, width)
    normed_one, factor_one = normalize(flat_in)
    attention_input = (normed_one * scale_one).astype(jnp.bfloat16)
    query_b = plain_dot(attention_input, query_full).astype(jnp.bfloat16)
    key_b = (
        plain_dot(attention_input, key_full)
        .astype(jnp.bfloat16)
        .reshape(seqs_here, tok_here, kv_local * HEAD_SIZE)
    )
    value_b = (
        plain_dot(attention_input, value_full)
        .astype(jnp.bfloat16)
        .reshape(seqs_here, tok_here, kv_local * HEAD_SIZE)
    )
    key_all, value_all = (
        lax.all_gather(key_b, "ctx", axis=1, tiled=True),
        lax.all_gather(value_b, "ctx", axis=1, tiled=True),
    )
    query_five = query_b.reshape(seqs_here, tok_here, kv_local, head_groups, HEAD_SIZE)
    key_four = key_all.reshape(seqs_here, SEQUENCE_SLOTS, kv_local, HEAD_SIZE)
    value_four = value_all.reshape(seqs_here, SEQUENCE_SLOTS, kv_local, HEAD_SIZE)
    raw = (
        jnp.einsum("stkgd,sukd->skgtu", query_five, key_four, preferred_element_type=jnp.float32)
        * QSCALE
    )
    bent = jnp.tanh(raw / CAP)
    masked = jnp.where(allowed, CAP * bent, NEG)
    largest = jnp.max(masked, -1, keepdims=True)
    logsum = largest + jnp.log(jnp.sum(jnp.exp(masked - largest), -1, keepdims=True))
    probs = jnp.exp(masked - logsum)
    probs_b = probs.astype(jnp.bfloat16)
    attended = (
        jnp.einsum("skgtu,sukd->stkgd", probs_b, value_four, preferred_element_type=jnp.float32)
        .astype(jnp.bfloat16)
        .reshape(row_count, -1)
    )
    attn = lax.psum(plain_dot(attended, out_full).astype(jnp.bfloat16), "tp").astype(jnp.float32)
    normed_two, factor_two = normalize(attn)
    after_attn = flat_in + normed_two * scale_two
    normed_three, factor_three = normalize(after_attn)
    ffn_in = (normed_three * scale_three).astype(jnp.bfloat16)
    gate = plain_dot(ffn_in, gate_full)
    upward = plain_dot(ffn_in, up_full)
    activated, gelu_pull = jax.vjp(gelu_tanh, gate)
    hidden_b = (activated * upward).astype(jnp.bfloat16)
    ffn_out = lax.psum(plain_dot(hidden_b, down_full).astype(jnp.bfloat16), "tp").astype(
        jnp.float32
    )
    normed_four, factor_four = normalize(ffn_out)
    result = after_attn + normed_four * scale_four
    cot = cotangent.astype(jnp.float32).reshape(row_count, width) * valid.reshape(
        row_count, 1
    ).astype(jnp.float32)
    query_back, key_back, value_back, out_back, gate_back, up_back, down_back = (
        lax.all_gather(query_weight, ("fsdp", "ctx"), axis=0, tiled=True),
        lax.all_gather(key_weight, ("fsdp", "ctx"), axis=0, tiled=True),
        lax.all_gather(value_weight, ("fsdp", "ctx"), axis=0, tiled=True),
        lax.all_gather(w_out, ("fsdp", "ctx"), axis=1, tiled=True),
        lax.all_gather(w_gate, ("fsdp", "ctx"), axis=0, tiled=True),
        lax.all_gather(w_up, ("fsdp", "ctx"), axis=0, tiled=True),
        lax.all_gather(w_down, ("fsdp", "ctx"), axis=1, tiled=True),
    )
    grad_gain_four = jnp.sum(cot * normed_four, 0)
    dffn_b = norm_back(cot * scale_four, normed_four, factor_four).astype(jnp.bfloat16)
    grad_down = left_dot(hidden_b, dffn_b)
    dhidden = right_dot(dffn_b, down_back)
    dgate_b = gelu_pull(dhidden * upward)[0].astype(jnp.bfloat16)
    dup_b = (dhidden * activated).astype(jnp.bfloat16)
    grad_gate = left_dot(ffn_in, dgate_b)
    grad_up = left_dot(ffn_in, dup_b)
    dffn_in = lax.psum(
        (right_dot(dgate_b, gate_back) + right_dot(dup_b, up_back)).astype(jnp.bfloat16), "tp"
    ).astype(jnp.float32)
    grad_gain_three = jnp.sum(dffn_in * normed_three, 0)
    dafter = cot + norm_back(dffn_in * scale_three, normed_three, factor_three)
    grad_gain_two = jnp.sum(dafter * normed_two, 0)
    dattn_b = norm_back(dafter * scale_two, normed_two, factor_two).astype(jnp.bfloat16)
    grad_out = left_dot(attended, dattn_b)
    dattended = right_dot(dattn_b, out_back).astype(jnp.bfloat16).reshape(query_five.shape)
    dprobs = jnp.einsum(
        "stkgd,sukd->skgtu", dattended, value_four, preferred_element_type=jnp.float32
    )
    weighted = jnp.sum(probs * dprobs, -1, keepdims=True)
    draw_b = (probs * (dprobs - weighted) * (1.0 - bent * bent)).astype(jnp.bfloat16)
    dquery_b = (
        (
            jnp.einsum("skgtu,sukd->stkgd", draw_b, key_four, preferred_element_type=jnp.float32)
            * QSCALE
        )
        .astype(jnp.bfloat16)
        .reshape(row_count, -1)
    )
    dvalue_part = jnp.einsum(
        "skgtu,stkgd->sukd", probs_b, dattended, preferred_element_type=jnp.float32
    )
    dkey_part = (
        jnp.einsum("skgtu,stkgd->sukd", draw_b, query_five, preferred_element_type=jnp.float32)
        * QSCALE
    )
    dkey, dvalue = (
        lax.psum_scatter(
            dkey_part.astype(jnp.bfloat16), "ctx", scatter_dimension=1, tiled=True
        ).astype(jnp.float32),
        lax.psum_scatter(
            dvalue_part.astype(jnp.bfloat16), "ctx", scatter_dimension=1, tiled=True
        ).astype(jnp.float32),
    )
    dkey_b = dkey.astype(jnp.bfloat16).reshape(row_count, -1)
    dvalue_b = dvalue.astype(jnp.bfloat16).reshape(row_count, -1)
    grad_query = left_dot(attention_input, dquery_b)
    grad_key = left_dot(attention_input, dkey_b)
    grad_value = left_dot(attention_input, dvalue_b)
    dattn_in = lax.psum(
        (
            right_dot(dquery_b, query_back)
            + right_dot(dkey_b, key_back)
            + right_dot(dvalue_b, value_back)
        ).astype(jnp.bfloat16),
        "tp",
    ).astype(jnp.float32)
    grad_gain_one = jnp.sum(dattn_in * normed_one, 0)
    grad_input = dafter + norm_back(dattn_in * scale_one, normed_one, factor_one)
    summed = (
        lax.psum_scatter(
            grad_query.astype(jnp.bfloat16), ("fsdp", "ctx"), scatter_dimension=0, tiled=True
        ).astype(jnp.float32),
        lax.psum_scatter(
            grad_key.astype(jnp.bfloat16), ("fsdp", "ctx"), scatter_dimension=0, tiled=True
        ).astype(jnp.float32),
        lax.psum_scatter(
            grad_value.astype(jnp.bfloat16), ("fsdp", "ctx"), scatter_dimension=0, tiled=True
        ).astype(jnp.float32),
        lax.psum_scatter(
            grad_out.astype(jnp.bfloat16), ("fsdp", "ctx"), scatter_dimension=1, tiled=True
        ).astype(jnp.float32),
        lax.psum_scatter(
            grad_gate.astype(jnp.bfloat16), ("fsdp", "ctx"), scatter_dimension=0, tiled=True
        ).astype(jnp.float32),
        lax.psum_scatter(
            grad_up.astype(jnp.bfloat16), ("fsdp", "ctx"), scatter_dimension=0, tiled=True
        ).astype(jnp.float32),
        lax.psum_scatter(
            grad_down.astype(jnp.bfloat16), ("fsdp", "ctx"), scatter_dimension=1, tiled=True
        ).astype(jnp.float32),
        lax.psum_scatter(
            grad_gain_one.astype(jnp.bfloat16), ("fsdp", "ctx"), scatter_dimension=0, tiled=True
        ).astype(jnp.float32),
        lax.psum_scatter(
            grad_gain_two.astype(jnp.bfloat16), ("fsdp", "ctx"), scatter_dimension=0, tiled=True
        ).astype(jnp.float32),
        lax.psum_scatter(
            grad_gain_three.astype(jnp.bfloat16), ("fsdp", "ctx"), scatter_dimension=0, tiled=True
        ).astype(jnp.float32),
        lax.psum_scatter(
            grad_gain_four.astype(jnp.bfloat16), ("fsdp", "ctx"), scatter_dimension=0, tiled=True
        ).astype(jnp.float32),
    )
    return (
        result.astype(jnp.bfloat16).reshape(hidden_in.shape),
        grad_input.astype(jnp.bfloat16).reshape(hidden_in.shape),
        summed[0],
        summed[1],
        summed[2],
        summed[3],
        summed[4],
        summed[5],
        summed[6],
        summed[7],
        summed[8],
        summed[9],
        summed[10],
    )


def solution(mesh):
    square = mesh.shape["ctx"] == 4 and mesh.shape["fsdp"] == 2
    return jax.shard_map(
        plane_body if square else general_body,
        mesh=mesh,
        in_specs=(
            P("fsdp", "ctx", None),
            P("fsdp"),
            P(("fsdp", "ctx"), "tp"),
            P(("fsdp", "ctx"), "tp"),
            P(("fsdp", "ctx"), "tp"),
            P("tp", ("fsdp", "ctx")),
            P(("fsdp", "ctx"), "tp"),
            P(("fsdp", "ctx"), "tp"),
            P("tp", ("fsdp", "ctx")),
            P(("fsdp", "ctx")),
            P(("fsdp", "ctx")),
            P(("fsdp", "ctx")),
            P(("fsdp", "ctx")),
            P("fsdp", "ctx", None),
        ),
        out_specs=(
            P("fsdp", "ctx", None),
            P("fsdp", "ctx", None),
            P(("fsdp", "ctx"), "tp"),
            P(("fsdp", "ctx"), "tp"),
            P(("fsdp", "ctx"), "tp"),
            P("tp", ("fsdp", "ctx")),
            P(("fsdp", "ctx"), "tp"),
            P(("fsdp", "ctx"), "tp"),
            P("tp", ("fsdp", "ctx")),
            P(("fsdp", "ctx")),
            P(("fsdp", "ctx")),
            P(("fsdp", "ctx")),
            P(("fsdp", "ctx")),
        ),
        check_vma=False,
    )
```

```python
import jax
import jax.numpy as jnp
from jax import lax
from jax.experimental import pallas as pl
from jax.experimental.pallas import tpu as pltpu
from jax.sharding import PartitionSpec as P

QUERY_HEADS = 8
KEY_VALUE_HEADS = 4
HEAD_SIZE = 256
SEQUENCE_SLOTS = 2048


EPS = 1e-06
CAP = 50.0
QSCALE = 0.0625
NEG = -1e30


def normalize(value_rows):
    factor = lax.rsqrt(jnp.mean(value_rows * value_rows, -1, keepdims=True) + EPS)
    return (value_rows * factor, factor)


def norm_back(grad_hat, normed, factor):
    return factor * (grad_hat - normed * jnp.mean(grad_hat * normed, -1, keepdims=True))


def plain_dot(first, second):
    return jnp.dot(first, second, preferred_element_type=jnp.float32)


def left_dot(first, second):
    return lax.dot_general(
        first, second, (((0,), (0,)), ((), ())), preferred_element_type=jnp.float32
    )


def right_dot(first, second):
    return lax.dot_general(
        first, second, (((1,), (1,)), ((), ())), preferred_element_type=jnp.float32
    )


def gelu_tanh(value_rows):
    return jax.nn.gelu(value_rows, approximate=True)


BF = jnp.bfloat16
F32 = jnp.float32

LINKS = {
    "x": ("ctx", [(0, 1), (1, 0), (2, 3), (3, 2)]),
    "y": ("ctx", [(0, 2), (2, 0), (1, 3), (3, 1)]),
    "diagonal": ("ctx", [(0, 3), (3, 0), (1, 2), (2, 1)]),
    "core": ("fsdp", [(0, 1), (1, 0)]),
}
ORDER = [(0, 0), (0, 1), (1, 1), (2, 0), (1, 0), (3, 0), (3, 1), (2, 1)]


def tied(*values):
    return lax.optimization_barrier(values)


def send(link, value):
    return lax.ppermute(value, *LINKS[link])


def around(value, by=1):
    size = lax.axis_size("tp")
    return lax.ppermute(value, "tp", [(i, (i + by) % size) for i in range(size)])


def place(pieces, starts):
    rows = sum(piece.shape[0] for piece in pieces)
    whole = jnp.zeros((rows,) + pieces[0].shape[1:], pieces[0].dtype)
    for piece, start in zip(pieces, starts):
        whole = lax.dynamic_update_slice_in_dim(whole, piece, start, 0)
    return whole


def halves(block):
    half = block.shape[0] // 2
    return block[:half], block[half:]


class Scatter:
    def __init__(self, blocks):
        self.blocks = blocks
        self.half = blocks[1].shape[0]

    def diagonal(self):
        self.first = (send("x", self.blocks[2]), send("y", self.blocks[3]))

    def both(self):
        half = self.half = self.blocks[1].shape[0] // 2
        from_x, from_y = send("x", self.blocks[1]), send("y", self.blocks[2])
        self.first, self.middle = (from_x[half:], from_y[:half]), (from_x[:half], from_y[half:])

    def direct(self):
        self.middle = (send("x", self.blocks[1]), send("y", self.blocks[4]))

    def sums(self):
        half, kept, (d_top, d_low) = self.half, self.blocks[0], self.first
        x_low, y_top = kept[2 * half : 3 * half], kept[3 * half :]
        self.last = (
            send("x", (x_low.astype(F32) + d_low.astype(F32)).astype(BF)),
            send("y", (y_top.astype(F32) + d_top.astype(F32)).astype(BF)),
        )

    def result(self):
        half, kept = self.half, self.blocks[0]
        (x_top, y_low), (x_low, y_top) = self.middle, self.last
        top = kept[:half].astype(F32) + x_top.astype(F32) + y_top.astype(F32)
        low = kept[half : 2 * half].astype(F32) + y_low.astype(F32) + x_low.astype(F32)
        return jnp.concatenate([top, low], 0)


class Ring:
    def __init__(self, value, parts=1):
        self.value, self.step, self.parts = value, 0, parts
        self.size, self.me = lax.axis_size("tp"), lax.axis_index("tp")
        self.rows = value.shape[0] // (parts * self.size)
        self.whole = jnp.zeros_like(value)
        self.sent = [self.block(part, self.me - 1) for part in range(parts)]
        self.going = [around(sent) for sent in self.sent]

    def start(self, part, index):
        return (part * self.size + (index + self.size) % self.size) * self.rows

    def block(self, part, index):
        return lax.dynamic_slice_in_dim(self.value, self.start(part, index), self.rows, 0)

    def go(self):
        self.step += 1
        for part in range(self.parts):
            going = self.going[part]
            if self.parts > 1:
                going, _ = tied(going, self.sent[1 - part])
            if self.step < self.size:
                own = self.block(part, self.me - 1 - self.step)
                going = (going.astype(F32) + own.astype(F32)).astype(BF)
            if self.step >= self.size - 1:
                at = self.start(part, self.me - self.step + self.size - 1)
                self.whole = lax.dynamic_update_slice_in_dim(self.whole, going, at, 0)
            if self.step < 2 * self.size - 2:
                self.sent[part] = going
                self.going[part] = around(going)

    def finish(self):
        while self.step < 2 * self.size - 2:
            self.go()
        return self.whole


VMEM_BYTES = 56 * 2**20


def kernel_params():
    return pltpu.CompilerParams(vmem_limit_bytes=VMEM_BYTES)


def cut_of(size):
    return next((cut for cut in (768, 512) if size % cut == 0), size)


def rowwise(fn, rows, vectors, dtypes, sums=0, block=128):
    count, width = rows[0].shape
    n_in, n_out = len(rows) + len(vectors), len(dtypes)

    def kernel(*refs):
        results = fn(*(ref[...] for ref in refs[:n_in]))
        for ref, value in zip(refs[n_in : n_in + n_out], results):
            ref[...] = value.astype(ref.dtype)
        for ref, value in zip(refs[n_in + n_out :], results[n_out:]):
            part = jnp.sum(value.reshape(block // 8, 8, width), 0)

            @pl.when(pl.program_id(0) == 0)
            def _():
                ref[...] = part

            @pl.when(pl.program_id(0) > 0)
            def _():
                ref[...] += part

    by_row = pl.BlockSpec((block, width), lambda i: (i, 0))
    return pl.pallas_call(
        kernel,
        grid=(count // block,),
        in_specs=[by_row] * len(rows) + [pl.BlockSpec((1, width), lambda i: (0, 0))] * len(vectors),
        out_specs=[by_row] * n_out + [pl.BlockSpec((8, width), lambda i: (0, 0))] * sums,
        out_shape=[jax.ShapeDtypeStruct((count, width), dtype) for dtype in dtypes]
        + [jax.ShapeDtypeStruct((8, width), F32)] * sums,
        compiler_params=kernel_params(),
        cost_estimate=pl.CostEstimate(
            flops=20 * count * width, bytes_accessed=4 * count * width * n_in, transcendentals=0
        ),
    )(*rows, *vectors)


ROOT = 0.7978845608028654


def gelu_parts(z):
    bend = jnp.tanh(ROOT * (z + 0.044715 * (z * z * z)))
    value = 0.5 * z * (1.0 + bend)
    slope = 0.5 * (1.0 + bend) + 0.5 * z * (1.0 - bend * bend) * (
        ROOT * (1.0 + (3.0 * 0.044715) * (z * z))
    )
    return value, slope


def ffn_forward(x, weights, down_rest):
    count, width = x.shape
    cut, out_cut = down_rest.shape[1], cut_of(width)
    units = (weights.shape[1] + cut) // 3
    first = units // cut

    def kernel(x_ref, gate_w, up_w, down_w, rest_w, gate_ref, up_ref, hidden_ref, out_ref, kept):
        step = pl.program_id(0)

        @pl.when(step < first)
        def _():
            gate = plain_dot(x_ref[...], gate_w[...])
            up = plain_dot(x_ref[...], up_w[...])
            hidden = (gelu_parts(gate)[0] * up).astype(BF)
            gate_ref[...] = gate
            up_ref[...] = up
            hidden_ref[...] = hidden
            kept[step] = hidden

        @pl.when(step >= first)
        def _():
            total = right_dot(kept[first - 1], rest_w[...])
            for i in range(first - 1):
                total += right_dot(kept[i], down_w[:, i * cut : (i + 1) * cut])
            out_ref[...] = total.astype(BF)

    def early(j):
        return jnp.minimum(j, first - 1)

    def late(j):
        return jnp.maximum(j - first, 0)

    out = pl.BlockSpec((count, cut), lambda j: (0, early(j)))
    return pl.pallas_call(
        kernel,
        grid=(first + width // out_cut,),
        in_specs=[
            pl.BlockSpec((count, width), lambda j: (0, 0)),
            pl.BlockSpec((width, cut), lambda j: (0, early(j))),
            pl.BlockSpec((width, cut), lambda j: (0, early(j) + first)),
            pl.BlockSpec((out_cut, units - cut), lambda j: (late(j), 3)),
            pl.BlockSpec((out_cut, cut), lambda j: (late(j), 0)),
        ],
        out_specs=[out] * 3 + [pl.BlockSpec((count, out_cut), lambda j: (0, late(j)))],
        out_shape=[
            jax.ShapeDtypeStruct((count, units), F32),
            jax.ShapeDtypeStruct((count, units), F32),
            jax.ShapeDtypeStruct((count, units), BF),
            jax.ShapeDtypeStruct((count, width), BF),
        ],
        scratch_shapes=[pltpu.VMEM((first, count, cut), BF)],
        compiler_params=kernel_params(),
        cost_estimate=pl.CostEstimate(
            flops=6 * count * width * units,
            bytes_accessed=6 * width * units + 10 * count * units,
            transcendentals=count * units,
        ),
    )(x, weights, weights, weights, down_rest)


def ffn_backward(dffn, weights, down_rest, gate, up):
    count, width = dffn.shape
    units = gate.shape[1]
    cut, out_cut = down_rest.shape[1], cut_of(width)
    first = units // cut

    def kernel(
        d_ref,
        down_w,
        rest_w,
        gate_ref,
        up_ref,
        gate_w,
        up_w,
        dgate_ref,
        dup_ref,
        out_ref,
        kept,
        kept_up,
    ):
        step = pl.program_id(0)

        def make(weight):
            dhidden = plain_dot(d_ref[...], weight[...])
            value, slope = gelu_parts(gate_ref[...])
            dgate = (dhidden * up_ref[...] * slope).astype(BF)
            dup = (dhidden * value).astype(BF)
            dgate_ref[...] = dgate
            dup_ref[...] = dup
            kept[step] = dgate
            kept_up[step] = dup

        pl.when(step < first - 1)(lambda: make(down_w))
        pl.when(step == first - 1)(lambda: make(rest_w))

        @pl.when(step >= first)
        def _():
            out_ref[...] = sum(
                right_dot(terms[i], weight[:, i * cut : (i + 1) * cut])
                for i in range(first)
                for terms, weight in ((kept, gate_w), (kept_up, up_w))
            ).astype(BF)

    def early(j):
        return jnp.minimum(j, first - 1)

    def late(j):
        return jnp.maximum(j - first, 0)

    by_cut = pl.BlockSpec((count, cut), lambda j: (0, early(j)))
    return pl.pallas_call(
        kernel,
        grid=(first + width // out_cut,),
        in_specs=[
            pl.BlockSpec((count, width), lambda j: (0, 0)),
            pl.BlockSpec((width, cut), lambda j: (0, jnp.minimum(j, first - 2) + 2 * first)),
            pl.BlockSpec((width, cut), lambda j: (0, 0)),
            by_cut,
            by_cut,
            pl.BlockSpec((out_cut, units), lambda j: (late(j), 0)),
            pl.BlockSpec((out_cut, units), lambda j: (late(j), 1)),
        ],
        out_specs=[by_cut] * 2 + [pl.BlockSpec((count, out_cut), lambda j: (0, late(j)))],
        out_shape=[jax.ShapeDtypeStruct((count, units), BF)] * 2
        + [jax.ShapeDtypeStruct((count, width), BF)],
        scratch_shapes=[pltpu.VMEM((first, count, cut), BF)] * 2,
        compiler_params=kernel_params(),
        cost_estimate=pl.CostEstimate(
            flops=6 * count * width * units,
            bytes_accessed=6 * width * units + 12 * count * units,
            transcendentals=count * units,
        ),
    )(dffn, weights, down_rest, gate, up, weights, weights)


def weight_grad(rows, rows_far, cols, cols_far, joined=False):
    count, half_width = rows_far.shape
    width = cols.shape[1]
    cut = cut_of(width)
    half = half_width // 8
    place = jnp.stack([lax.axis_index("fsdp"), lax.axis_index("ctx")]).astype(jnp.int32)
    sizes = (4 * half, 2 * half, 2 * half) if joined else (4 * half,) + (half,) * 4

    def kernel(
        place_ref, near_ref, far_ref, cols_ref, cols_far_ref, *rest
    ):
        outs, (near_t, far_t, total) = rest[: len(sizes)], rest[len(sizes) :]

        @pl.when(pl.program_id(0) == 0)
        def _():
            near_t[...] = near_ref[...].T
            far_t[...] = far_ref[...].T

        total[...] = plain_dot(near_t[...], cols_ref[...]) + plain_dot(
            far_t[...], cols_far_ref[...]
        )
        for index, (k, low) in enumerate(ORDER):
            start = (lax.bitwise_xor(place_ref[1], k) * 2 + low) * half
            block = total[pl.ds(pl.multiple_of(start, 16), half), :].astype(BF)
            if index < 4:
                out, at = outs[0], index
            elif joined:
                out, at = outs[1 + (index - 4) // 2], index % 2
            else:
                out, at = outs[index - 3], 0
            out[at * half : (at + 1) * half, :] = block

    by_cut = pl.BlockSpec((count, cut), lambda j, place: (0, j))
    return pl.pallas_call(
        kernel,
        grid_spec=pltpu.PrefetchScalarGridSpec(
            num_scalar_prefetch=1,
            grid=(width // cut,),
            in_specs=[
                pl.BlockSpec((count, half_width), lambda j, place: (0, place[0])),
                pl.BlockSpec((count, half_width), lambda j, place: (0, 0)),
                by_cut,
                by_cut,
            ],
            out_specs=[pl.BlockSpec((size, cut), lambda j, place: (0, j)) for size in sizes],
            scratch_shapes=[
                pltpu.VMEM((half_width, count), BF),
                pltpu.VMEM((half_width, count), BF),
                pltpu.VMEM((half_width, cut), F32),
            ],
        ),
        out_shape=[jax.ShapeDtypeStruct((size, width), BF) for size in sizes],
        compiler_params=kernel_params(),
        cost_estimate=pl.CostEstimate(
            flops=4 * count * half_width * width,
            bytes_accessed=2 * half_width * width + 4 * count * (width + half_width),
            transcendentals=0,
        ),
    )(place, rows, rows_far, cols, cols_far)


def attention_back(query, dattended, attended, kv, logsum, length):
    tokens, columns = query.shape
    heads, blocks = columns // HEAD_SIZE, kv.shape[0] // tokens
    scalars = jnp.stack([lax.axis_index("ctx").astype(jnp.int32), length])

    def kernel(scalars_ref, q_ref, d_ref, a_ref, kv_ref, log_ref, dq_ref, dkv_ref, dq, dk, dv):
        block, head = pl.program_id(0), pl.program_id(1)
        q, d = q_ref[...], d_ref[...]
        key, value = kv_ref[:, :HEAD_SIZE], kv_ref[:, HEAD_SIZE:]
        me = scalars_ref[0]
        bent = jnp.tanh(right_dot(q, key) * (QSCALE / CAP))
        shape = (tokens, tokens)
        key_pos = lax.bitwise_xor(me, block) * tokens + lax.broadcasted_iota(jnp.int32, shape, 1)
        query_pos = me * tokens + lax.broadcasted_iota(jnp.int32, shape, 0)
        allowed = (key_pos <= query_pos) & (key_pos < scalars_ref[1])
        probs = jnp.where(allowed, jnp.exp(CAP * bent - log_ref[...]), 0.0)
        weighted = jnp.sum(d.astype(F32) * a_ref[...].astype(F32), -1, keepdims=True)
        draw = (probs * (right_dot(d, value) - weighted) * (1.0 - bent * bent)).astype(BF)
        dk_part, dv_part = left_dot(draw, q), left_dot(probs.astype(BF), d)
        dq_part = plain_dot(draw, key)

        @pl.when(head == 0)
        def _():
            dk[...] = dk_part
            dv[...] = dv_part

        @pl.when(head > 0)
        def _():
            dk[...] += dk_part
            dv[...] += dv_part

        @pl.when(block == 0)
        def _():
            dq[head] = dq_part

        @pl.when(block > 0)
        def _():
            dq[head] += dq_part

        @pl.when(head == heads - 1)
        def _():
            dkv_ref[:, :HEAD_SIZE] = (dk[...] * QSCALE).astype(BF)
            dkv_ref[:, HEAD_SIZE:] = dv[...].astype(BF)

        @pl.when((block == blocks - 1) & (head == heads - 1))
        def _():
            for i in range(heads):
                dq_ref[:, i * HEAD_SIZE : (i + 1) * HEAD_SIZE] = (dq[i] * QSCALE).astype(BF)

    by_head = pl.BlockSpec((tokens, HEAD_SIZE), lambda b, h, scalars: (0, h))
    return pl.pallas_call(
        kernel,
        grid_spec=pltpu.PrefetchScalarGridSpec(
            num_scalar_prefetch=1,
            grid=(blocks, heads),
            in_specs=[
                by_head,
                by_head,
                by_head,
                pl.BlockSpec((tokens, 2 * HEAD_SIZE), lambda b, h, scalars: (b, 0)),
                pl.BlockSpec((None, tokens, 1), lambda b, h, scalars: (h, 0, 0)),
            ],
            out_specs=[
                pl.BlockSpec((tokens, columns), lambda b, h, scalars: (0, 0)),
                pl.BlockSpec((None, tokens, 2 * HEAD_SIZE), lambda b, h, scalars: (b, 0, 0)),
            ],
            scratch_shapes=[
                pltpu.VMEM((heads, tokens, HEAD_SIZE), F32),
                pltpu.VMEM((tokens, HEAD_SIZE), F32),
                pltpu.VMEM((tokens, HEAD_SIZE), F32),
            ],
        ),
        out_shape=[
            jax.ShapeDtypeStruct((tokens, columns), BF),
            jax.ShapeDtypeStruct((blocks, tokens, 2 * HEAD_SIZE), BF),
        ],
        compiler_params=kernel_params(),
        cost_estimate=pl.CostEstimate(
            flops=10 * tokens * tokens * blocks * columns,
            bytes_accessed=8 * tokens * columns * blocks,
            transcendentals=2 * tokens * tokens * blocks * heads,
        ),
    )(scalars, query, dattended, attended, kv, logsum)


def residual_rows(attn, hidden, scale_two, scale_three):
    attn, hidden = attn.astype(F32), hidden.astype(F32)
    after = hidden + normalize(attn)[0] * scale_two
    return after, normalize(after)[0] * scale_three


def output_rows(ffn_out, after, cot, scale_four):
    normed, factor = normalize(ffn_out.astype(F32))
    cot = cot.astype(F32)
    return (
        after + normed * scale_four,
        norm_back(cot * scale_four, normed, factor),
        cot * normed,
    )


def residual_back_rows(dffn_in, after, attn, cot, scale_three, scale_two):
    dffn_in = dffn_in.astype(F32)
    normed, factor = normalize(after)
    dafter = cot.astype(F32) + norm_back(dffn_in * scale_three, normed, factor)
    normed_two, factor_two = normalize(attn.astype(F32))
    dattn = norm_back(dafter * scale_two, normed_two, factor_two)
    return dafter, dattn, dffn_in * normed, dafter * normed_two


def input_back_rows(dattn_in, hidden, dafter, scale_one):
    normed, factor = normalize(hidden.astype(F32))
    return (dafter + norm_back(dattn_in.astype(F32) * scale_one, normed, factor),)


def plane_body(
    hidden_in,
    lengths,
    query_weight,
    key_weight,
    value_weight,
    w_out,
    w_gate,
    w_up,
    w_down,
    gain_attn_in,
    gain_attn_out,
    gain_ffn_in,
    gain_ffn_out,
    cotangent,
):
    seqs_here, tok_here, width = hidden_in.shape
    row_count = seqs_here * tok_here
    head_groups = QUERY_HEADS // KEY_VALUE_HEADS
    half_width = width // 2
    q_cols, kv_cols = query_weight.shape[1], key_weight.shape[1]
    size = lax.axis_size("tp")
    kv_local = kv_cols // HEAD_SIZE
    planes, me = lax.axis_size("ctx"), lax.axis_index("ctx")

    core = lax.axis_index("fsdp")

    def gather(shard):
        return lax.all_gather(shard, ("fsdp", "ctx"), axis=0, tiled=True)

    def far_half(rows):
        return send("core", lax.dynamic_slice_in_dim(rows, (1 - core) * half_width, half_width, 1))

    attention_shards = jnp.concatenate([query_weight, key_weight, value_weight, w_out.T], 1)
    attention_w = gather(attention_shards)
    late = w_down.shape[0] - cut_of(w_down.shape[0])
    ffn_shards = jnp.concatenate([w_gate, w_up, w_down[:late].T], 1)
    rest_t = w_down[late:].T
    rest_x, rest_y = send("x", rest_t), send("y", rest_t)
    gains = jnp.stack([gain_attn_in, gain_attn_out, gain_ffn_in, gain_ffn_out])[None]
    gains = jnp.broadcast_to(gains, (2 * planes,) + gains.shape[1:])
    gains = lax.all_to_all(gains, ("fsdp", "ctx"), 0, 0, tiled=True)
    gains = gains.transpose(1, 0, 2).reshape(4, width).astype(F32)
    scale_one, scale_two, scale_three, scale_four = (1.0 + gains[i][None] for i in range(4))
    flat_in = hidden_in.astype(F32).reshape(row_count, width)
    normed_one, factor_one = normalize(flat_in)
    attention_input = (normed_one * scale_one).astype(BF)

    attention_w, attention_input, ffn_shards, rest_x, rest_y = tied(
        attention_w, attention_input, ffn_shards, rest_x, rest_y
    )
    ffn_w = gather(ffn_shards)
    qkv_cols = q_cols + 2 * kv_cols
    qkv_w, out_w = attention_w[:, :qkv_cols], attention_w[:, qkv_cols:]
    run = jnp.arange(tok_here, dtype=jnp.int32)
    query_pos = me * tok_here + run
    key_pos = jnp.concatenate([(me ^ k) * tok_here + run for k in range(planes)])
    valid = query_pos[None, :] < lengths[:, None]
    allowed = (
        (key_pos[None, None, :] <= query_pos[None, :, None])
        & (key_pos[None, None, :] < lengths[:, None, None])
    )[:, None, None]
    qkv = plain_dot(attention_input, qkv_w).astype(BF)
    query_b = qkv[:, :q_cols]
    kv = qkv[:, q_cols:].reshape(seqs_here, tok_here, 2 * kv_cols)
    kv_all = jnp.concatenate([kv, send("x", kv), send("y", kv), send("diagonal", kv)], 1)
    kv_all, rest_x, rest_y = tied(kv_all, rest_x, rest_y)
    rest_last = [send("y", halves(rest_x)[0]), send("x", halves(rest_y)[1])]
    query_five = query_b.reshape(seqs_here, tok_here, kv_local, head_groups, HEAD_SIZE)
    key_four = kv_all[:, :, :kv_cols].reshape(seqs_here, SEQUENCE_SLOTS, kv_local, HEAD_SIZE)
    value_four = kv_all[:, :, kv_cols:].reshape(seqs_here, SEQUENCE_SLOTS, kv_local, HEAD_SIZE)
    raw = jnp.einsum("stkgd,sukd->skgtu", query_five, key_four, preferred_element_type=F32) * QSCALE
    bent = jnp.tanh(raw / CAP)
    masked = jnp.where(allowed, CAP * bent, NEG)
    largest = jnp.max(masked, -1, keepdims=True)
    logsum = largest + jnp.log(jnp.sum(jnp.exp(masked - largest), -1, keepdims=True))
    probs = jnp.exp(masked - logsum)
    probs_b = probs.astype(BF)
    attended = (
        jnp.einsum("skgtu,sukd->stkgd", probs_b, value_four, preferred_element_type=F32)
        .astype(BF)
        .reshape(row_count, -1)
    )
    attended, rest_last = tied(attended, rest_last)
    attn = right_dot(attended, out_w).astype(BF)
    ring = Ring(attn, 2)
    ring.go()
    rows, start = rest_t.shape[0], [(me ^ k) * rest_t.shape[0] for k in range(4)]
    rest_near = place([rest_t, rest_x, rest_y, *rest_last], [*start, start[3] + rows // 2])
    ring.go()
    ring.going, rest_near = tied(ring.going, rest_near)
    rest_far = send("core", rest_near)
    ring.go()
    ring.go()
    ring.going[1], rest_far = tied(ring.going[1], rest_far)
    ring.go()
    down_rest = place([rest_near, rest_far], [core * half_width, (1 - core) * half_width])
    attn = ring.finish()
    hidden_rows = hidden_in.reshape(row_count, width)
    after_attn, ffn_in = rowwise(
        residual_rows, [attn, hidden_rows], [scale_two, scale_three], [F32, BF]
    )
    gate, upward, hidden_b, ffn_out = ffn_forward(ffn_in, ffn_w, down_rest)
    ffn_out, hidden_b, attended, ffn_in, attention_input, cotangent = tied(
        ffn_out, hidden_b, attended, ffn_in, attention_input, cotangent
    )
    ring = Ring(ffn_out, 2)

    hidden_far, attended_far = send("core", hidden_b), send("core", attended)
    ffn_in_far, attention_input_far = far_half(ffn_in), far_half(attention_input)
    cot = jnp.where(
        valid.reshape(row_count, 1), cotangent.reshape(row_count, width), jnp.zeros((), BF)
    )
    ring.go()
    ring.going[0], hidden_far, attended_far, ffn_in_far, attention_input_far, cot = tied(
        ring.going[0], hidden_far, attended_far, ffn_in_far, attention_input_far, cot
    )
    ffn_out = ring.finish()
    output, dffn_b, gain_four_rows = rowwise(
        output_rows, [ffn_out, after_attn, cot], [scale_four], [BF, BF], 1
    )
    dgate_b, dup_b, dffn_in = ffn_backward(
        dffn_b, ffn_w, down_rest, gate, upward
    )
    dffn_far = far_half(dffn_b)

    dffn_in, dffn_far, dgate_b, dup_b = tied(dffn_in, dffn_far, dgate_b, dup_b)
    ring = Ring(dffn_in, 2)
    dgate_far = send("core", dgate_b)
    down_s = Scatter(weight_grad(dffn_b, dffn_far, hidden_b, hidden_far))
    ring.going[0], down_s.blocks, dgate_far = tied(ring.going[0], down_s.blocks, dgate_far)
    ring.go()
    down_s.diagonal()
    dup_far = send("core", dup_b)
    gate_s = Scatter(weight_grad(ffn_in, ffn_in_far, dgate_b, dgate_far))
    ring.going[0], gate_s.blocks, dup_far, down_s.first = tied(
        ring.going[0], gate_s.blocks, dup_far, down_s.first
    )
    ring.go()
    down_s.direct()
    up_s = Scatter(weight_grad(ffn_in, ffn_in_far, dup_b, dup_far))
    ring.going[0], up_s.blocks, down_s.middle = tied(ring.going[0], up_s.blocks, down_s.middle)
    ring.go()
    down_s.sums()
    ring.going[0], down_s.last, gate_s.blocks = tied(ring.going[0], down_s.last, gate_s.blocks)
    ring.go()
    gate_s.diagonal()
    grad_down = down_s.result().T
    ring.going[0], gate_s.first, grad_down = tied(ring.going[0], gate_s.first, grad_down)
    ring.go()
    gate_s.direct()
    dffn_in, up_s.blocks, gate_s.first, gate_s.middle = tied(
        ring.finish(), up_s.blocks, gate_s.first, gate_s.middle
    )
    gate_s.sums()
    up_s.diagonal()
    dafter, dattn_b, gain_three_rows, gain_two_rows = rowwise(
        residual_back_rows,
        [dffn_in, after_attn, attn, cot],
        [scale_three, scale_two],
        [F32, BF],
        2,
    )
    dattended = plain_dot(dattn_b, out_w).astype(BF)
    dattn_far = far_half(dattn_b)
    dattended, gate_s.last, up_s.first, up_s.blocks = tied(
        dattended, gate_s.last, up_s.first, up_s.blocks
    )
    up_s.direct()
    dquery_b, dkv = attention_back(
        query_b, dattended, attended, kv_all[0], logsum.reshape(head_groups, row_count, 1), lengths[0]
    )
    dkv, dattn_far, up_s.middle = tied(dkv, dattn_far, up_s.middle)
    dkv = [dkv[0], send("x", dkv[1]), send("y", dkv[2]), send("diagonal", dkv[3])]
    out_s = Scatter(weight_grad(dattn_b, dattn_far, attended, attended_far, True))
    grad_gate = gate_s.result()
    dkv, dquery_b, out_s.blocks, grad_gate, up_s.blocks = tied(
        dkv, dquery_b, out_s.blocks, grad_gate, up_s.blocks
    )
    dkv_b = sum(part.astype(F32) for part in dkv).astype(BF)
    dqkv_b = jnp.concatenate([dquery_b, dkv_b], 1)
    dattn_in = right_dot(dqkv_b, qkv_w)
    dattn_in, dqkv_b, dafter, up_s.blocks = tied(
        dattn_in.astype(BF), dqkv_b, dafter, up_s.blocks
    )

    ring = Ring(dattn_in)
    dqkv_far = send("core", dqkv_b)
    qkv_s = Scatter(
        weight_grad(attention_input, attention_input_far, dqkv_b, dqkv_far, True)
    )
    up_s.sums()
    gain_rows = gain_two_rows, gain_three_rows, gain_four_rows
    ring.going, qkv_s.blocks, up_s.last, gain_rows = tied(
        ring.going, qkv_s.blocks, up_s.last, gain_rows
    )
    ring.go()
    qkv_s.both()
    grad_gain_one = jnp.sum(dattn_in.astype(F32) * normed_one, 0)
    grad_gains = jnp.stack([grad_gain_one] + [jnp.sum(rows, 0) / size for rows in gain_rows])
    grad_gains = grad_gains.reshape(4, 2 * planes, 1, -1).transpose(1, 2, 0, 3)
    grad_gains = jnp.broadcast_to(grad_gains, (2 * planes, size) + grad_gains.shape[2:])
    grad_gains = grad_gains.reshape((-1,) + grad_gains.shape[2:])
    ring.going, qkv_s.first, qkv_s.middle, out_s.blocks = tied(
        ring.going, qkv_s.first, qkv_s.middle, out_s.blocks
    )
    ring.go()
    qkv_s.sums()
    out_s.both()
    grad_up = up_s.result()
    ring.going, qkv_s.last, out_s.first, out_s.middle, grad_up, grad_gains = tied(
        ring.going, qkv_s.last, out_s.first, out_s.middle, grad_up, grad_gains
    )
    ring.go()
    out_s.sums()
    grad_gains = lax.all_to_all(grad_gains, ("fsdp", "ctx", "tp"), 0, 0, tiled=True)
    grad_qkv = qkv_s.result()
    ring.going, out_s.last, grad_qkv = tied(ring.going, out_s.last, grad_qkv)
    ring.go()
    grad_out = out_s.result().T
    ring.going, grad_out = tied(ring.going, grad_out)
    ring.go()
    dattn_in, grad_gains = tied(ring.finish(), grad_gains)
    grad_gains = jnp.sum(grad_gains, 0)
    (grad_input,) = rowwise(input_back_rows, [dattn_in, hidden_rows, dafter], [scale_one], [BF])
    return (
        output.reshape(hidden_in.shape),
        grad_input.reshape(hidden_in.shape),
        grad_qkv[:, :q_cols],
        grad_qkv[:, q_cols : q_cols + kv_cols],
        grad_qkv[:, q_cols + kv_cols :],
        grad_out,
        grad_gate,
        grad_up,
        grad_down,
        grad_gains[0],
        grad_gains[1],
        grad_gains[2],
        grad_gains[3],
    )


def general_body(
    hidden_in,
    lengths,
    query_weight,
    key_weight,
    value_weight,
    w_out,
    w_gate,
    w_up,
    w_down,
    gain_attn_in,
    gain_attn_out,
    gain_ffn_in,
    gain_ffn_out,
    cotangent,
):
    seqs_here, tok_here, width = hidden_in.shape
    row_count = seqs_here * tok_here
    head_groups = QUERY_HEADS // KEY_VALUE_HEADS
    gathered = (
        lax.all_gather(query_weight, ("fsdp", "ctx"), axis=0, tiled=True),
        lax.all_gather(key_weight, ("fsdp", "ctx"), axis=0, tiled=True),
        lax.all_gather(value_weight, ("fsdp", "ctx"), axis=0, tiled=True),
        lax.all_gather(w_out, ("fsdp", "ctx"), axis=1, tiled=True),
        lax.all_gather(w_gate, ("fsdp", "ctx"), axis=0, tiled=True),
        lax.all_gather(w_up, ("fsdp", "ctx"), axis=0, tiled=True),
        lax.all_gather(w_down, ("fsdp", "ctx"), axis=1, tiled=True),
        lax.all_gather(gain_attn_in, ("fsdp", "ctx"), axis=0, tiled=True),
        lax.all_gather(gain_attn_out, ("fsdp", "ctx"), axis=0, tiled=True),
        lax.all_gather(gain_ffn_in, ("fsdp", "ctx"), axis=0, tiled=True),
        lax.all_gather(gain_ffn_out, ("fsdp", "ctx"), axis=0, tiled=True),
    )
    query_full, key_full, value_full, out_full, gate_full, up_full, down_full = gathered[:7]
    scale_one = 1.0 + gathered[7].astype(jnp.float32)
    scale_two = 1.0 + gathered[8].astype(jnp.float32)
    scale_three = 1.0 + gathered[9].astype(jnp.float32)
    scale_four = 1.0 + gathered[10].astype(jnp.float32)
    kv_local = key_full.shape[1] // HEAD_SIZE
    own_start = lax.axis_index("ctx") * tok_here
    query_pos = own_start + jnp.arange(tok_here, dtype=jnp.int32)
    key_pos = jnp.arange(SEQUENCE_SLOTS, dtype=jnp.int32)
    valid = query_pos[None, :] < lengths[:, None]
    allowed = (
        (key_pos[None, None, :] <= query_pos[None, :, None])
        & (key_pos[None, None, :] < lengths[:, None, None])
    )[:, None, None]
    flat_in = hidden_in.astype(jnp.float32).reshape(row_count, width)
    normed_one, factor_one = normalize(flat_in)
    attention_input = (normed_one * scale_one).astype(jnp.bfloat16)
    query_b = plain_dot(attention_input, query_full).astype(jnp.bfloat16)
    key_b = (
        plain_dot(attention_input, key_full)
        .astype(jnp.bfloat16)
        .reshape(seqs_here, tok_here, kv_local * HEAD_SIZE)
    )
    value_b = (
        plain_dot(attention_input, value_full)
        .astype(jnp.bfloat16)
        .reshape(seqs_here, tok_here, kv_local * HEAD_SIZE)
    )
    key_all, value_all = (
        lax.all_gather(key_b, "ctx", axis=1, tiled=True),
        lax.all_gather(value_b, "ctx", axis=1, tiled=True),
    )
    query_five = query_b.reshape(seqs_here, tok_here, kv_local, head_groups, HEAD_SIZE)
    key_four = key_all.reshape(seqs_here, SEQUENCE_SLOTS, kv_local, HEAD_SIZE)
    value_four = value_all.reshape(seqs_here, SEQUENCE_SLOTS, kv_local, HEAD_SIZE)
    raw = (
        jnp.einsum("stkgd,sukd->skgtu", query_five, key_four, preferred_element_type=jnp.float32)
        * QSCALE
    )
    bent = jnp.tanh(raw / CAP)
    masked = jnp.where(allowed, CAP * bent, NEG)
    largest = jnp.max(masked, -1, keepdims=True)
    logsum = largest + jnp.log(jnp.sum(jnp.exp(masked - largest), -1, keepdims=True))
    probs = jnp.exp(masked - logsum)
    probs_b = probs.astype(jnp.bfloat16)
    attended = (
        jnp.einsum("skgtu,sukd->stkgd", probs_b, value_four, preferred_element_type=jnp.float32)
        .astype(jnp.bfloat16)
        .reshape(row_count, -1)
    )
    attn = lax.psum(plain_dot(attended, out_full).astype(jnp.bfloat16), "tp").astype(jnp.float32)
    normed_two, factor_two = normalize(attn)
    after_attn = flat_in + normed_two * scale_two
    normed_three, factor_three = normalize(after_attn)
    ffn_in = (normed_three * scale_three).astype(jnp.bfloat16)
    gate = plain_dot(ffn_in, gate_full)
    upward = plain_dot(ffn_in, up_full)
    activated, gelu_pull = jax.vjp(gelu_tanh, gate)
    hidden_b = (activated * upward).astype(jnp.bfloat16)
    ffn_out = lax.psum(plain_dot(hidden_b, down_full).astype(jnp.bfloat16), "tp").astype(
        jnp.float32
    )
    normed_four, factor_four = normalize(ffn_out)
    result = after_attn + normed_four * scale_four
    cot = cotangent.astype(jnp.float32).reshape(row_count, width) * valid.reshape(
        row_count, 1
    ).astype(jnp.float32)
    query_back, key_back, value_back, out_back, gate_back, up_back, down_back = (
        lax.all_gather(query_weight, ("fsdp", "ctx"), axis=0, tiled=True),
        lax.all_gather(key_weight, ("fsdp", "ctx"), axis=0, tiled=True),
        lax.all_gather(value_weight, ("fsdp", "ctx"), axis=0, tiled=True),
        lax.all_gather(w_out, ("fsdp", "ctx"), axis=1, tiled=True),
        lax.all_gather(w_gate, ("fsdp", "ctx"), axis=0, tiled=True),
        lax.all_gather(w_up, ("fsdp", "ctx"), axis=0, tiled=True),
        lax.all_gather(w_down, ("fsdp", "ctx"), axis=1, tiled=True),
    )
    grad_gain_four = jnp.sum(cot * normed_four, 0)
    dffn_b = norm_back(cot * scale_four, normed_four, factor_four).astype(jnp.bfloat16)
    grad_down = left_dot(hidden_b, dffn_b)
    dhidden = right_dot(dffn_b, down_back)
    dgate_b = gelu_pull(dhidden * upward)[0].astype(jnp.bfloat16)
    dup_b = (dhidden * activated).astype(jnp.bfloat16)
    grad_gate = left_dot(ffn_in, dgate_b)
    grad_up = left_dot(ffn_in, dup_b)
    dffn_in = lax.psum(
        (right_dot(dgate_b, gate_back) + right_dot(dup_b, up_back)).astype(jnp.bfloat16), "tp"
    ).astype(jnp.float32)
    grad_gain_three = jnp.sum(dffn_in * normed_three, 0)
    dafter = cot + norm_back(dffn_in * scale_three, normed_three, factor_three)
    grad_gain_two = jnp.sum(dafter * normed_two, 0)
    dattn_b = norm_back(dafter * scale_two, normed_two, factor_two).astype(jnp.bfloat16)
    grad_out = left_dot(attended, dattn_b)
    dattended = right_dot(dattn_b, out_back).astype(jnp.bfloat16).reshape(query_five.shape)
    dprobs = jnp.einsum(
        "stkgd,sukd->skgtu", dattended, value_four, preferred_element_type=jnp.float32
    )
    weighted = jnp.sum(probs * dprobs, -1, keepdims=True)
    draw_b = (probs * (dprobs - weighted) * (1.0 - bent * bent)).astype(jnp.bfloat16)
    dquery_b = (
        (
            jnp.einsum("skgtu,sukd->stkgd", draw_b, key_four, preferred_element_type=jnp.float32)
            * QSCALE
        )
        .astype(jnp.bfloat16)
        .reshape(row_count, -1)
    )
    dvalue_part = jnp.einsum(
        "skgtu,stkgd->sukd", probs_b, dattended, preferred_element_type=jnp.float32
    )
    dkey_part = (
        jnp.einsum("skgtu,stkgd->sukd", draw_b, query_five, preferred_element_type=jnp.float32)
        * QSCALE
    )
    dkey, dvalue = (
        lax.psum_scatter(
            dkey_part.astype(jnp.bfloat16), "ctx", scatter_dimension=1, tiled=True
        ).astype(jnp.float32),
        lax.psum_scatter(
            dvalue_part.astype(jnp.bfloat16), "ctx", scatter_dimension=1, tiled=True
        ).astype(jnp.float32),
    )
    dkey_b = dkey.astype(jnp.bfloat16).reshape(row_count, -1)
    dvalue_b = dvalue.astype(jnp.bfloat16).reshape(row_count, -1)
    grad_query = left_dot(attention_input, dquery_b)
    grad_key = left_dot(attention_input, dkey_b)
    grad_value = left_dot(attention_input, dvalue_b)
    dattn_in = lax.psum(
        (
            right_dot(dquery_b, query_back)
            + right_dot(dkey_b, key_back)
            + right_dot(dvalue_b, value_back)
        ).astype(jnp.bfloat16),
        "tp",
    ).astype(jnp.float32)
    grad_gain_one = jnp.sum(dattn_in * normed_one, 0)
    grad_input = dafter + norm_back(dattn_in * scale_one, normed_one, factor_one)
    summed = (
        lax.psum_scatter(
            grad_query.astype(jnp.bfloat16), ("fsdp", "ctx"), scatter_dimension=0, tiled=True
        ).astype(jnp.float32),
        lax.psum_scatter(
            grad_key.astype(jnp.bfloat16), ("fsdp", "ctx"), scatter_dimension=0, tiled=True
        ).astype(jnp.float32),
        lax.psum_scatter(
            grad_value.astype(jnp.bfloat16), ("fsdp", "ctx"), scatter_dimension=0, tiled=True
        ).astype(jnp.float32),
        lax.psum_scatter(
            grad_out.astype(jnp.bfloat16), ("fsdp", "ctx"), scatter_dimension=1, tiled=True
        ).astype(jnp.float32),
        lax.psum_scatter(
            grad_gate.astype(jnp.bfloat16), ("fsdp", "ctx"), scatter_dimension=0, tiled=True
        ).astype(jnp.float32),
        lax.psum_scatter(
            grad_up.astype(jnp.bfloat16), ("fsdp", "ctx"), scatter_dimension=0, tiled=True
        ).astype(jnp.float32),
        lax.psum_scatter(
            grad_down.astype(jnp.bfloat16), ("fsdp", "ctx"), scatter_dimension=1, tiled=True
        ).astype(jnp.float32),
        lax.psum_scatter(
            grad_gain_one.astype(jnp.bfloat16), ("fsdp", "ctx"), scatter_dimension=0, tiled=True
        ).astype(jnp.float32),
        lax.psum_scatter(
            grad_gain_two.astype(jnp.bfloat16), ("fsdp", "ctx"), scatter_dimension=0, tiled=True
        ).astype(jnp.float32),
        lax.psum_scatter(
            grad_gain_three.astype(jnp.bfloat16), ("fsdp", "ctx"), scatter_dimension=0, tiled=True
        ).astype(jnp.float32),
        lax.psum_scatter(
            grad_gain_four.astype(jnp.bfloat16), ("fsdp", "ctx"), scatter_dimension=0, tiled=True
        ).astype(jnp.float32),
    )
    return (
        result.astype(jnp.bfloat16).reshape(hidden_in.shape),
        grad_input.astype(jnp.bfloat16).reshape(hidden_in.shape),
        summed[0],
        summed[1],
        summed[2],
        summed[3],
        summed[4],
        summed[5],
        summed[6],
        summed[7],
        summed[8],
        summed[9],
        summed[10],
    )


def solution(mesh):
    square = mesh.shape["ctx"] == 4 and mesh.shape["fsdp"] == 2
    return jax.shard_map(
        plane_body if square else general_body,
        mesh=mesh,
        in_specs=(
            P("fsdp", "ctx", None),
            P("fsdp"),
            P(("fsdp", "ctx"), "tp"),
            P(("fsdp", "ctx"), "tp"),
            P(("fsdp", "ctx"), "tp"),
            P("tp", ("fsdp", "ctx")),
            P(("fsdp", "ctx"), "tp"),
            P(("fsdp", "ctx"), "tp"),
            P("tp", ("fsdp", "ctx")),
            P(("fsdp", "ctx")),
            P(("fsdp", "ctx")),
            P(("fsdp", "ctx")),
            P(("fsdp", "ctx")),
            P("fsdp", "ctx", None),
        ),
        out_specs=(
            P("fsdp", "ctx", None),
            P("fsdp", "ctx", None),
            P(("fsdp", "ctx"), "tp"),
            P(("fsdp", "ctx"), "tp"),
            P(("fsdp", "ctx"), "tp"),
            P("tp", ("fsdp", "ctx")),
            P(("fsdp", "ctx"), "tp"),
            P(("fsdp", "ctx"), "tp"),
            P("tp", ("fsdp", "ctx")),
            P(("fsdp", "ctx")),
            P(("fsdp", "ctx")),
            P(("fsdp", "ctx")),
            P(("fsdp", "ctx")),
        ),
        check_vma=False,
    )
```

```python
import jax
import jax.numpy as jnp
from jax import lax
from jax.experimental import pallas as pl
from jax.experimental.pallas import tpu as pltpu
from jax.sharding import PartitionSpec as P

QUERY_HEADS = 8
KEY_VALUE_HEADS = 4
HEAD_SIZE = 256
SEQUENCE_SLOTS = 2048


EPS = 1e-06
CAP = 50.0
QSCALE = 0.0625
NEG = -1e30


def normalize(value_rows):
    factor = lax.rsqrt(jnp.mean(value_rows * value_rows, -1, keepdims=True) + EPS)
    return (value_rows * factor, factor)


def norm_back(grad_hat, normed, factor):
    return factor * (grad_hat - normed * jnp.mean(grad_hat * normed, -1, keepdims=True))


def plain_dot(first, second):
    return jnp.dot(first, second, preferred_element_type=jnp.float32)


def left_dot(first, second):
    return lax.dot_general(
        first, second, (((0,), (0,)), ((), ())), preferred_element_type=jnp.float32
    )


def right_dot(first, second):
    return lax.dot_general(
        first, second, (((1,), (1,)), ((), ())), preferred_element_type=jnp.float32
    )


def gelu_tanh(value_rows):
    return jax.nn.gelu(value_rows, approximate=True)


BF = jnp.bfloat16
F32 = jnp.float32

LINKS = {
    "x": ("ctx", [(0, 1), (1, 0), (2, 3), (3, 2)]),
    "y": ("ctx", [(0, 2), (2, 0), (1, 3), (3, 1)]),
    "diagonal": ("ctx", [(0, 3), (3, 0), (1, 2), (2, 1)]),
    "core": ("fsdp", [(0, 1), (1, 0)]),
}
ORDER = [(0, 0), (0, 1), (1, 1), (2, 0), (1, 0), (3, 0), (3, 1), (2, 1)]


def tied(*values):
    return lax.optimization_barrier(values)


def send(link, value):
    return lax.ppermute(value, *LINKS[link])


def around(value, by=1):
    size = lax.axis_size("tp")
    return lax.ppermute(value, "tp", [(i, (i + by) % size) for i in range(size)])


def place(pieces, starts):
    rows = sum(piece.shape[0] for piece in pieces)
    whole = jnp.zeros((rows,) + pieces[0].shape[1:], pieces[0].dtype)
    for piece, start in zip(pieces, starts):
        whole = lax.dynamic_update_slice_in_dim(whole, piece, start, 0)
    return whole


def halves(block):
    half = block.shape[0] // 2
    return block[:half], block[half:]


class Scatter:
    def __init__(self, blocks):
        self.blocks = blocks
        self.half = blocks[1].shape[0]

    def diagonal(self):
        self.first = (send("x", self.blocks[2]), send("y", self.blocks[3]))

    def both(self):
        half = self.half = self.blocks[1].shape[0] // 2
        from_x, from_y = send("x", self.blocks[1]), send("y", self.blocks[2])
        self.first, self.middle = (from_x[half:], from_y[:half]), (from_x[:half], from_y[half:])

    def direct(self):
        self.middle = (send("x", self.blocks[1]), send("y", self.blocks[4]))

    def sums(self):
        half, kept, (d_top, d_low) = self.half, self.blocks[0], self.first
        x_low, y_top = kept[2 * half : 3 * half], kept[3 * half :]
        self.last = (
            send("x", (x_low.astype(F32) + d_low.astype(F32)).astype(BF)),
            send("y", (y_top.astype(F32) + d_top.astype(F32)).astype(BF)),
        )

    def result(self):
        half, kept = self.half, self.blocks[0]
        (x_top, y_low), (x_low, y_top) = self.middle, self.last
        top = kept[:half].astype(F32) + x_top.astype(F32) + y_top.astype(F32)
        low = kept[half : 2 * half].astype(F32) + y_low.astype(F32) + x_low.astype(F32)
        return jnp.concatenate([top, low], 0)


class Ring:
    def __init__(self, value, parts=1):
        self.value, self.step, self.parts = value, 0, parts
        self.size, self.me = lax.axis_size("tp"), lax.axis_index("tp")
        self.rows = value.shape[0] // (parts * self.size)
        self.whole = jnp.zeros_like(value)
        self.sent = [self.block(part, self.me - 1) for part in range(parts)]
        self.going = [around(sent) for sent in self.sent]

    def start(self, part, index):
        return (part * self.size + (index + self.size) % self.size) * self.rows

    def block(self, part, index):
        return lax.dynamic_slice_in_dim(self.value, self.start(part, index), self.rows, 0)

    def go(self):
        self.step += 1
        for part in range(self.parts):
            going = self.going[part]
            if self.parts > 1:
                going, _ = tied(going, self.sent[1 - part])
            if self.step < self.size:
                own = self.block(part, self.me - 1 - self.step)
                going = (going.astype(F32) + own.astype(F32)).astype(BF)
            if self.step >= self.size - 1:
                at = self.start(part, self.me - self.step + self.size - 1)
                self.whole = lax.dynamic_update_slice_in_dim(self.whole, going, at, 0)
            if self.step < 2 * self.size - 2:
                self.sent[part] = going
                self.going[part] = around(going)

    def finish(self):
        while self.step < 2 * self.size - 2:
            self.go()
        return self.whole


VMEM_BYTES = 56 * 2**20


def kernel_params():
    return pltpu.CompilerParams(vmem_limit_bytes=VMEM_BYTES)


def cut_of(size):
    return next((cut for cut in (768, 512) if size % cut == 0), size)


def rowwise(fn, rows, vectors, dtypes, sums=0, block=128):
    count, width = rows[0].shape
    n_in, n_out = len(rows) + len(vectors), len(dtypes)

    def kernel(*refs):
        results = fn(*(ref[...] for ref in refs[:n_in]))
        for ref, value in zip(refs[n_in : n_in + n_out], results):
            ref[...] = value.astype(ref.dtype)
        for ref, value in zip(refs[n_in + n_out :], results[n_out:]):
            part = jnp.sum(value.reshape(block // 8, 8, width), 0)

            @pl.when(pl.program_id(0) == 0)
            def _():
                ref[...] = part

            @pl.when(pl.program_id(0) > 0)
            def _():
                ref[...] += part

    by_row = pl.BlockSpec((block, width), lambda i: (i, 0))
    return pl.pallas_call(
        kernel,
        grid=(count // block,),
        in_specs=[by_row] * len(rows) + [pl.BlockSpec((1, width), lambda i: (0, 0))] * len(vectors),
        out_specs=[by_row] * n_out + [pl.BlockSpec((8, width), lambda i: (0, 0))] * sums,
        out_shape=[jax.ShapeDtypeStruct((count, width), dtype) for dtype in dtypes]
        + [jax.ShapeDtypeStruct((8, width), F32)] * sums,
        compiler_params=kernel_params(),
        cost_estimate=pl.CostEstimate(
            flops=20 * count * width, bytes_accessed=4 * count * width * n_in, transcendentals=0
        ),
    )(*rows, *vectors)


ROOT = 0.7978845608028654


def gelu_parts(z):
    bend = jnp.tanh(ROOT * (z + 0.044715 * (z * z * z)))
    value = 0.5 * z * (1.0 + bend)
    slope = 0.5 * (1.0 + bend) + 0.5 * z * (1.0 - bend * bend) * (
        ROOT * (1.0 + (3.0 * 0.044715) * (z * z))
    )
    return value, slope


def ffn_forward(x, weights, down_rest):
    count, width = x.shape
    cut, out_cut = down_rest.shape[1], cut_of(width)
    units = (weights.shape[1] + cut) // 3
    first = units // cut

    def kernel(x_ref, gate_w, up_w, down_w, rest_w, gate_ref, up_ref, hidden_ref, out_ref, kept):
        step = pl.program_id(0)

        @pl.when(step < first)
        def _():
            gate = plain_dot(x_ref[...], gate_w[...])
            up = plain_dot(x_ref[...], up_w[...])
            hidden = (gelu_parts(gate)[0] * up).astype(BF)
            gate_ref[...] = gate
            up_ref[...] = up
            hidden_ref[...] = hidden
            kept[step] = hidden

        @pl.when(step >= first)
        def _():
            total = right_dot(kept[first - 1], rest_w[...])
            for i in range(first - 1):
                total += right_dot(kept[i], down_w[:, i * cut : (i + 1) * cut])
            out_ref[...] = total.astype(BF)

    def early(j):
        return jnp.minimum(j, first - 1)

    def late(j):
        return jnp.maximum(j - first, 0)

    out = pl.BlockSpec((count, cut), lambda j: (0, early(j)))
    return pl.pallas_call(
        kernel,
        grid=(first + width // out_cut,),
        in_specs=[
            pl.BlockSpec((count, width), lambda j: (0, 0)),
            pl.BlockSpec((width, cut), lambda j: (0, early(j))),
            pl.BlockSpec((width, cut), lambda j: (0, early(j) + first)),
            pl.BlockSpec((out_cut, units - cut), lambda j: (late(j), 3)),
            pl.BlockSpec((out_cut, cut), lambda j: (late(j), 0)),
        ],
        out_specs=[out] * 3 + [pl.BlockSpec((count, out_cut), lambda j: (0, late(j)))],
        out_shape=[
            jax.ShapeDtypeStruct((count, units), F32),
            jax.ShapeDtypeStruct((count, units), F32),
            jax.ShapeDtypeStruct((count, units), BF),
            jax.ShapeDtypeStruct((count, width), BF),
        ],
        scratch_shapes=[pltpu.VMEM((first, count, cut), BF)],
        compiler_params=kernel_params(),
        cost_estimate=pl.CostEstimate(
            flops=6 * count * width * units,
            bytes_accessed=6 * width * units + 10 * count * units,
            transcendentals=count * units,
        ),
    )(x, weights, weights, weights, down_rest)


def ffn_backward(dffn, weights, down_rest, gate, up):
    count, width = dffn.shape
    units = gate.shape[1]
    cut, out_cut = down_rest.shape[1], cut_of(width)
    first = units // cut

    def kernel(
        d_ref,
        down_w,
        rest_w,
        gate_ref,
        up_ref,
        gate_w,
        up_w,
        dgate_ref,
        dup_ref,
        out_ref,
        kept,
        kept_up,
    ):
        step = pl.program_id(0)

        def make(weight):
            dhidden = plain_dot(d_ref[...], weight[...])
            value, slope = gelu_parts(gate_ref[...])
            dgate = (dhidden * up_ref[...] * slope).astype(BF)
            dup = (dhidden * value).astype(BF)
            dgate_ref[...] = dgate
            dup_ref[...] = dup
            kept[step] = dgate
            kept_up[step] = dup

        pl.when(step < first - 1)(lambda: make(down_w))
        pl.when(step == first - 1)(lambda: make(rest_w))

        @pl.when(step >= first)
        def _():
            out_ref[...] = sum(
                right_dot(terms[i], weight[:, i * cut : (i + 1) * cut])
                for i in range(first)
                for terms, weight in ((kept, gate_w), (kept_up, up_w))
            ).astype(BF)

    def early(j):
        return jnp.minimum(j, first - 1)

    def late(j):
        return jnp.maximum(j - first, 0)

    by_cut = pl.BlockSpec((count, cut), lambda j: (0, early(j)))
    return pl.pallas_call(
        kernel,
        grid=(first + width // out_cut,),
        in_specs=[
            pl.BlockSpec((count, width), lambda j: (0, 0)),
            pl.BlockSpec((width, cut), lambda j: (0, jnp.minimum(j, first - 2) + 2 * first)),
            pl.BlockSpec((width, cut), lambda j: (0, 0)),
            by_cut,
            by_cut,
            pl.BlockSpec((out_cut, units), lambda j: (late(j), 0)),
            pl.BlockSpec((out_cut, units), lambda j: (late(j), 1)),
        ],
        out_specs=[by_cut] * 2 + [pl.BlockSpec((count, out_cut), lambda j: (0, late(j)))],
        out_shape=[jax.ShapeDtypeStruct((count, units), BF)] * 2
        + [jax.ShapeDtypeStruct((count, width), BF)],
        scratch_shapes=[pltpu.VMEM((first, count, cut), BF)] * 2,
        compiler_params=kernel_params(),
        cost_estimate=pl.CostEstimate(
            flops=6 * count * width * units,
            bytes_accessed=6 * width * units + 12 * count * units,
            transcendentals=count * units,
        ),
    )(dffn, weights, down_rest, gate, up, weights, weights)


def weight_grad(rows, rows_far, cols, cols_far, joined=False):
    count, half_width = rows_far.shape
    width = cols.shape[1]
    cut = cut_of(width)
    half = half_width // 8
    place = jnp.stack([lax.axis_index("fsdp"), lax.axis_index("ctx")]).astype(jnp.int32)
    sizes = (4 * half, 2 * half, 2 * half) if joined else (4 * half,) + (half,) * 4

    def kernel(
        place_ref, near_ref, far_ref, cols_ref, cols_far_ref, *rest
    ):
        outs, (near_t, far_t, total) = rest[: len(sizes)], rest[len(sizes) :]

        @pl.when(pl.program_id(0) == 0)
        def _():
            near_t[...] = near_ref[...].T
            far_t[...] = far_ref[...].T

        total[...] = plain_dot(near_t[...], cols_ref[...]) + plain_dot(
            far_t[...], cols_far_ref[...]
        )
        for index, (k, low) in enumerate(ORDER):
            start = (lax.bitwise_xor(place_ref[1], k) * 2 + low) * half
            block = total[pl.ds(pl.multiple_of(start, 16), half), :].astype(BF)
            if index < 4:
                out, at = outs[0], index
            elif joined:
                out, at = outs[1 + (index - 4) // 2], index % 2
            else:
                out, at = outs[index - 3], 0
            out[at * half : (at + 1) * half, :] = block

    by_cut = pl.BlockSpec((count, cut), lambda j, place: (0, j))
    return pl.pallas_call(
        kernel,
        grid_spec=pltpu.PrefetchScalarGridSpec(
            num_scalar_prefetch=1,
            grid=(width // cut,),
            in_specs=[
                pl.BlockSpec((count, half_width), lambda j, place: (0, place[0])),
                pl.BlockSpec((count, half_width), lambda j, place: (0, 0)),
                by_cut,
                by_cut,
            ],
            out_specs=[pl.BlockSpec((size, cut), lambda j, place: (0, j)) for size in sizes],
            scratch_shapes=[
                pltpu.VMEM((half_width, count), BF),
                pltpu.VMEM((half_width, count), BF),
                pltpu.VMEM((half_width, cut), F32),
            ],
        ),
        out_shape=[jax.ShapeDtypeStruct((size, width), BF) for size in sizes],
        compiler_params=kernel_params(),
        cost_estimate=pl.CostEstimate(
            flops=4 * count * half_width * width,
            bytes_accessed=2 * half_width * width + 4 * count * (width + half_width),
            transcendentals=0,
        ),
    )(place, rows, rows_far, cols, cols_far)


def attention_back(query, dattended, attended, kv, logsum, length):
    tokens, columns = query.shape
    heads, blocks = columns // HEAD_SIZE, kv.shape[0] // tokens
    scalars = jnp.stack([lax.axis_index("ctx").astype(jnp.int32), length])

    def kernel(scalars_ref, q_ref, d_ref, a_ref, kv_ref, log_ref, dq_ref, dkv_ref, dq, dk, dv):
        block, head = pl.program_id(0), pl.program_id(1)
        q, d = q_ref[...], d_ref[...]
        key, value = kv_ref[:, :HEAD_SIZE], kv_ref[:, HEAD_SIZE:]
        me = scalars_ref[0]
        bent = jnp.tanh(right_dot(q, key) * (QSCALE / CAP))
        shape = (tokens, tokens)
        key_pos = lax.bitwise_xor(me, block) * tokens + lax.broadcasted_iota(jnp.int32, shape, 1)
        query_pos = me * tokens + lax.broadcasted_iota(jnp.int32, shape, 0)
        allowed = (key_pos <= query_pos) & (key_pos < scalars_ref[1])
        probs = jnp.where(allowed, jnp.exp(CAP * bent - log_ref[...]), 0.0)
        weighted = jnp.sum(d.astype(F32) * a_ref[...].astype(F32), -1, keepdims=True)
        draw = (probs * (right_dot(d, value) - weighted) * (1.0 - bent * bent)).astype(BF)
        dk_part, dv_part = left_dot(draw, q), left_dot(probs.astype(BF), d)
        dq_part = plain_dot(draw, key)

        @pl.when(head == 0)
        def _():
            dk[...] = dk_part
            dv[...] = dv_part

        @pl.when(head > 0)
        def _():
            dk[...] += dk_part
            dv[...] += dv_part

        @pl.when(block == 0)
        def _():
            dq[head] = dq_part

        @pl.when(block > 0)
        def _():
            dq[head] += dq_part

        @pl.when(head == heads - 1)
        def _():
            dkv_ref[:, :HEAD_SIZE] = (dk[...] * QSCALE).astype(BF)
            dkv_ref[:, HEAD_SIZE:] = dv[...].astype(BF)

        @pl.when((block == blocks - 1) & (head == heads - 1))
        def _():
            for i in range(heads):
                dq_ref[:, i * HEAD_SIZE : (i + 1) * HEAD_SIZE] = (dq[i] * QSCALE).astype(BF)

    by_head = pl.BlockSpec((tokens, HEAD_SIZE), lambda b, h, scalars: (0, h))
    return pl.pallas_call(
        kernel,
        grid_spec=pltpu.PrefetchScalarGridSpec(
            num_scalar_prefetch=1,
            grid=(blocks, heads),
            in_specs=[
                by_head,
                by_head,
                by_head,
                pl.BlockSpec((tokens, 2 * HEAD_SIZE), lambda b, h, scalars: (b, 0)),
                pl.BlockSpec((None, tokens, 1), lambda b, h, scalars: (h, 0, 0)),
            ],
            out_specs=[
                pl.BlockSpec((tokens, columns), lambda b, h, scalars: (0, 0)),
                pl.BlockSpec((None, tokens, 2 * HEAD_SIZE), lambda b, h, scalars: (b, 0, 0)),
            ],
            scratch_shapes=[
                pltpu.VMEM((heads, tokens, HEAD_SIZE), F32),
                pltpu.VMEM((tokens, HEAD_SIZE), F32),
                pltpu.VMEM((tokens, HEAD_SIZE), F32),
            ],
        ),
        out_shape=[
            jax.ShapeDtypeStruct((tokens, columns), BF),
            jax.ShapeDtypeStruct((blocks, tokens, 2 * HEAD_SIZE), BF),
        ],
        compiler_params=kernel_params(),
        cost_estimate=pl.CostEstimate(
            flops=10 * tokens * tokens * blocks * columns,
            bytes_accessed=8 * tokens * columns * blocks,
            transcendentals=2 * tokens * tokens * blocks * heads,
        ),
    )(scalars, query, dattended, attended, kv, logsum)


def residual_rows(attn, hidden, scale_two, scale_three):
    attn, hidden = attn.astype(F32), hidden.astype(F32)
    after = hidden + normalize(attn)[0] * scale_two
    return after, normalize(after)[0] * scale_three


def output_rows(ffn_out, after, cot, scale_four):
    normed, factor = normalize(ffn_out.astype(F32))
    cot = cot.astype(F32)
    return (
        after + normed * scale_four,
        norm_back(cot * scale_four, normed, factor),
        cot * normed,
    )


def residual_back_rows(dffn_in, after, attn, cot, scale_three, scale_two):
    dffn_in = dffn_in.astype(F32)
    normed, factor = normalize(after)
    dafter = cot.astype(F32) + norm_back(dffn_in * scale_three, normed, factor)
    normed_two, factor_two = normalize(attn.astype(F32))
    dattn = norm_back(dafter * scale_two, normed_two, factor_two)
    return dafter, dattn, dffn_in * normed, dafter * normed_two


def input_back_rows(dattn_in, hidden, dafter, scale_one):
    normed, factor = normalize(hidden.astype(F32))
    return (dafter + norm_back(dattn_in.astype(F32) * scale_one, normed, factor),)


def plane_body(
    hidden_in,
    lengths,
    query_weight,
    key_weight,
    value_weight,
    w_out,
    w_gate,
    w_up,
    w_down,
    gain_attn_in,
    gain_attn_out,
    gain_ffn_in,
    gain_ffn_out,
    cotangent,
):
    seqs_here, tok_here, width = hidden_in.shape
    row_count = seqs_here * tok_here
    head_groups = QUERY_HEADS // KEY_VALUE_HEADS
    half_width = width // 2
    q_cols, kv_cols = query_weight.shape[1], key_weight.shape[1]
    size = lax.axis_size("tp")
    kv_local = kv_cols // HEAD_SIZE
    planes, me = lax.axis_size("ctx"), lax.axis_index("ctx")

    core = lax.axis_index("fsdp")

    def gather(shard):
        return lax.all_gather(shard, ("fsdp", "ctx"), axis=0, tiled=True)

    def far_half(rows):
        return send("core", lax.dynamic_slice_in_dim(rows, (1 - core) * half_width, half_width, 1))

    attention_shards = jnp.concatenate([query_weight, key_weight, value_weight, w_out.T], 1)
    attention_w = gather(attention_shards)
    late = w_down.shape[0] - cut_of(w_down.shape[0])
    ffn_shards = jnp.concatenate([w_gate, w_up, w_down[:late].T], 1)
    rest_t = w_down[late:].T
    rest_x, rest_y = send("x", rest_t), send("y", rest_t)
    gains = jnp.stack([gain_attn_in, gain_attn_out, gain_ffn_in, gain_ffn_out])[None]
    gains = jnp.broadcast_to(gains, (2 * planes,) + gains.shape[1:])
    gains = lax.all_to_all(gains, ("fsdp", "ctx"), 0, 0, tiled=True)
    gains = gains.transpose(1, 0, 2).reshape(4, width).astype(F32)
    scale_one, scale_two, scale_three, scale_four = (1.0 + gains[i][None] for i in range(4))
    flat_in = hidden_in.astype(F32).reshape(row_count, width)
    normed_one, factor_one = normalize(flat_in)
    attention_input = (normed_one * scale_one).astype(BF)

    attention_w, attention_input, ffn_shards, rest_x, rest_y = tied(
        attention_w, attention_input, ffn_shards, rest_x, rest_y
    )
    ffn_w = gather(ffn_shards)
    qkv_cols = q_cols + 2 * kv_cols
    qkv_w, out_w = attention_w[:, :qkv_cols], attention_w[:, qkv_cols:]
    run = jnp.arange(tok_here, dtype=jnp.int32)
    query_pos = me * tok_here + run
    key_pos = jnp.concatenate([(me ^ k) * tok_here + run for k in range(planes)])
    valid = query_pos[None, :] < lengths[:, None]
    allowed = (
        (key_pos[None, None, :] <= query_pos[None, :, None])
        & (key_pos[None, None, :] < lengths[:, None, None])
    )[:, None, None]
    qkv = plain_dot(attention_input, qkv_w).astype(BF)
    query_b = qkv[:, :q_cols]
    kv = qkv[:, q_cols:].reshape(seqs_here, tok_here, 2 * kv_cols)
    kv_all = jnp.concatenate([kv, send("x", kv), send("y", kv), send("diagonal", kv)], 1)
    kv_all, rest_x, rest_y = tied(kv_all, rest_x, rest_y)
    rest_last = [send("y", halves(rest_x)[0]), send("x", halves(rest_y)[1])]
    query_five = query_b.reshape(seqs_here, tok_here, kv_local, head_groups, HEAD_SIZE)
    key_four = kv_all[:, :, :kv_cols].reshape(seqs_here, SEQUENCE_SLOTS, kv_local, HEAD_SIZE)
    value_four = kv_all[:, :, kv_cols:].reshape(seqs_here, SEQUENCE_SLOTS, kv_local, HEAD_SIZE)
    raw = jnp.einsum("stkgd,sukd->skgtu", query_five, key_four, preferred_element_type=F32) * QSCALE
    bent = jnp.tanh(raw / CAP)
    masked = jnp.where(allowed, CAP * bent, NEG)
    largest = jnp.max(masked, -1, keepdims=True)
    logsum = largest + jnp.log(jnp.sum(jnp.exp(masked - largest), -1, keepdims=True))
    probs = jnp.exp(masked - logsum)
    probs_b = probs.astype(BF)
    attended = (
        jnp.einsum("skgtu,sukd->stkgd", probs_b, value_four, preferred_element_type=F32)
        .astype(BF)
        .reshape(row_count, -1)
    )
    attended, rest_last = tied(attended, rest_last)
    attn = right_dot(attended, out_w).astype(BF)
    ring = Ring(attn, 2)
    ring.go()
    rows, start = rest_t.shape[0], [(me ^ k) * rest_t.shape[0] for k in range(4)]
    rest_near = place([rest_t, rest_x, rest_y, *rest_last], [*start, start[3] + rows // 2])
    ring.go()
    ring.going, rest_near = tied(ring.going, rest_near)
    rest_far = send("core", rest_near)
    ring.go()
    ring.go()
    ring.going[1], rest_far = tied(ring.going[1], rest_far)
    ring.go()
    down_rest = place([rest_near, rest_far], [core * half_width, (1 - core) * half_width])
    attn = ring.finish()
    hidden_rows = hidden_in.reshape(row_count, width)
    after_attn, ffn_in = rowwise(
        residual_rows, [attn, hidden_rows], [scale_two, scale_three], [F32, BF]
    )
    gate, upward, hidden_b, ffn_out = ffn_forward(ffn_in, ffn_w, down_rest)
    ffn_out, hidden_b, attended, ffn_in, attention_input, cotangent = tied(
        ffn_out, hidden_b, attended, ffn_in, attention_input, cotangent
    )
    ring = Ring(ffn_out, 2)

    hidden_far, attended_far = send("core", hidden_b), send("core", attended)
    ffn_in_far, attention_input_far = far_half(ffn_in), far_half(attention_input)
    cot = jnp.where(
        valid.reshape(row_count, 1), cotangent.reshape(row_count, width), jnp.zeros((), BF)
    )
    ring.go()
    ring.going[0], hidden_far, attended_far, ffn_in_far, attention_input_far, cot = tied(
        ring.going[0], hidden_far, attended_far, ffn_in_far, attention_input_far, cot
    )
    ffn_out = ring.finish()
    output, dffn_b, gain_four_rows = rowwise(
        output_rows, [ffn_out, after_attn, cot], [scale_four], [BF, BF], 1
    )
    dgate_b, dup_b, dffn_in = ffn_backward(
        dffn_b, ffn_w, down_rest, gate, upward
    )
    dffn_far = far_half(dffn_b)

    dffn_in, dffn_far, dgate_b, dup_b = tied(dffn_in, dffn_far, dgate_b, dup_b)
    ring = Ring(dffn_in, 2)
    dgate_far = send("core", dgate_b)
    down_s = Scatter(weight_grad(dffn_b, dffn_far, hidden_b, hidden_far))
    ring.going[1], down_s.blocks, dgate_far = tied(ring.going[1], down_s.blocks, dgate_far)
    ring.go()
    down_s.diagonal()
    dup_far = send("core", dup_b)
    gate_s = Scatter(weight_grad(ffn_in, ffn_in_far, dgate_b, dgate_far))
    ring.going[1], gate_s.blocks, dup_far, down_s.first = tied(
        ring.going[1], gate_s.blocks, dup_far, down_s.first
    )
    ring.go()
    down_s.direct()
    up_s = Scatter(weight_grad(ffn_in, ffn_in_far, dup_b, dup_far))
    ring.going[1], up_s.blocks, down_s.middle = tied(ring.going[1], up_s.blocks, down_s.middle)
    ring.go()
    down_s.sums()
    ring.going[1], down_s.last, gate_s.blocks = tied(ring.going[1], down_s.last, gate_s.blocks)
    ring.go()
    gate_s.diagonal()
    grad_down = down_s.result().T
    ring.going[1], gate_s.first, grad_down = tied(ring.going[1], gate_s.first, grad_down)
    ring.go()
    gate_s.direct()
    dffn_in, up_s.blocks, gate_s.first, gate_s.middle = tied(
        ring.finish(), up_s.blocks, gate_s.first, gate_s.middle
    )
    gate_s.sums()
    up_s.diagonal()
    dafter, dattn_b, gain_three_rows, gain_two_rows = rowwise(
        residual_back_rows,
        [dffn_in, after_attn, attn, cot],
        [scale_three, scale_two],
        [F32, BF],
        2,
    )
    dattended = plain_dot(dattn_b, out_w).astype(BF)
    dattn_far = far_half(dattn_b)
    dattended, gate_s.last, up_s.first, up_s.blocks = tied(
        dattended, gate_s.last, up_s.first, up_s.blocks
    )
    up_s.direct()
    dquery_b, dkv = attention_back(
        query_b, dattended, attended, kv_all[0], logsum.reshape(head_groups, row_count, 1), lengths[0]
    )
    dkv, dattn_far, up_s.middle = tied(dkv, dattn_far, up_s.middle)
    dkv = [dkv[0], send("x", dkv[1]), send("y", dkv[2]), send("diagonal", dkv[3])]
    out_s = Scatter(weight_grad(dattn_b, dattn_far, attended, attended_far, True))
    grad_gate = gate_s.result()
    dkv, dquery_b, out_s.blocks, grad_gate, up_s.blocks = tied(
        dkv, dquery_b, out_s.blocks, grad_gate, up_s.blocks
    )
    dkv_b = sum(part.astype(F32) for part in dkv).astype(BF)
    dqkv_b = jnp.concatenate([dquery_b, dkv_b], 1)
    dattn_in = right_dot(dqkv_b, qkv_w)
    dattn_in, dqkv_b, dafter, up_s.blocks = tied(
        dattn_in.astype(BF), dqkv_b, dafter, up_s.blocks
    )

    ring = Ring(dattn_in)
    dqkv_far = send("core", dqkv_b)
    qkv_s = Scatter(
        weight_grad(attention_input, attention_input_far, dqkv_b, dqkv_far, True)
    )
    up_s.sums()
    gain_rows = gain_two_rows, gain_three_rows, gain_four_rows
    ring.going, qkv_s.blocks, up_s.last, gain_rows = tied(
        ring.going, qkv_s.blocks, up_s.last, gain_rows
    )
    ring.go()
    qkv_s.both()
    grad_gain_one = jnp.sum(dattn_in.astype(F32) * normed_one, 0)
    grad_gains = jnp.stack([grad_gain_one] + [jnp.sum(rows, 0) / size for rows in gain_rows])
    grad_gains = grad_gains.reshape(4, 2 * planes, 1, -1).transpose(1, 2, 0, 3)
    grad_gains = jnp.broadcast_to(grad_gains, (2 * planes, size) + grad_gains.shape[2:])
    grad_gains = grad_gains.reshape((-1,) + grad_gains.shape[2:])
    ring.going, qkv_s.first, qkv_s.middle, out_s.blocks = tied(
        ring.going, qkv_s.first, qkv_s.middle, out_s.blocks
    )
    ring.go()
    qkv_s.sums()
    out_s.both()
    grad_up = up_s.result()
    ring.going, qkv_s.last, out_s.first, out_s.middle, grad_up, grad_gains = tied(
        ring.going, qkv_s.last, out_s.first, out_s.middle, grad_up, grad_gains
    )
    ring.go()
    out_s.sums()
    grad_gains = lax.all_to_all(grad_gains, ("fsdp", "ctx", "tp"), 0, 0, tiled=True)
    grad_qkv = qkv_s.result()
    ring.going, out_s.last, grad_qkv = tied(ring.going, out_s.last, grad_qkv)
    ring.go()
    grad_out = out_s.result().T
    ring.going, grad_out = tied(ring.going, grad_out)
    ring.go()
    dattn_in, grad_gains = tied(ring.finish(), grad_gains)
    grad_gains = jnp.sum(grad_gains, 0)
    (grad_input,) = rowwise(input_back_rows, [dattn_in, hidden_rows, dafter], [scale_one], [BF])
    return (
        output.reshape(hidden_in.shape),
        grad_input.reshape(hidden_in.shape),
        grad_qkv[:, :q_cols],
        grad_qkv[:, q_cols : q_cols + kv_cols],
        grad_qkv[:, q_cols + kv_cols :],
        grad_out,
        grad_gate,
        grad_up,
        grad_down,
        grad_gains[0],
        grad_gains[1],
        grad_gains[2],
        grad_gains[3],
    )


def general_body(
    hidden_in,
    lengths,
    query_weight,
    key_weight,
    value_weight,
    w_out,
    w_gate,
    w_up,
    w_down,
    gain_attn_in,
    gain_attn_out,
    gain_ffn_in,
    gain_ffn_out,
    cotangent,
):
    seqs_here, tok_here, width = hidden_in.shape
    row_count = seqs_here * tok_here
    head_groups = QUERY_HEADS // KEY_VALUE_HEADS
    gathered = (
        lax.all_gather(query_weight, ("fsdp", "ctx"), axis=0, tiled=True),
        lax.all_gather(key_weight, ("fsdp", "ctx"), axis=0, tiled=True),
        lax.all_gather(value_weight, ("fsdp", "ctx"), axis=0, tiled=True),
        lax.all_gather(w_out, ("fsdp", "ctx"), axis=1, tiled=True),
        lax.all_gather(w_gate, ("fsdp", "ctx"), axis=0, tiled=True),
        lax.all_gather(w_up, ("fsdp", "ctx"), axis=0, tiled=True),
        lax.all_gather(w_down, ("fsdp", "ctx"), axis=1, tiled=True),
        lax.all_gather(gain_attn_in, ("fsdp", "ctx"), axis=0, tiled=True),
        lax.all_gather(gain_attn_out, ("fsdp", "ctx"), axis=0, tiled=True),
        lax.all_gather(gain_ffn_in, ("fsdp", "ctx"), axis=0, tiled=True),
        lax.all_gather(gain_ffn_out, ("fsdp", "ctx"), axis=0, tiled=True),
    )
    query_full, key_full, value_full, out_full, gate_full, up_full, down_full = gathered[:7]
    scale_one = 1.0 + gathered[7].astype(jnp.float32)
    scale_two = 1.0 + gathered[8].astype(jnp.float32)
    scale_three = 1.0 + gathered[9].astype(jnp.float32)
    scale_four = 1.0 + gathered[10].astype(jnp.float32)
    kv_local = key_full.shape[1] // HEAD_SIZE
    own_start = lax.axis_index("ctx") * tok_here
    query_pos = own_start + jnp.arange(tok_here, dtype=jnp.int32)
    key_pos = jnp.arange(SEQUENCE_SLOTS, dtype=jnp.int32)
    valid = query_pos[None, :] < lengths[:, None]
    allowed = (
        (key_pos[None, None, :] <= query_pos[None, :, None])
        & (key_pos[None, None, :] < lengths[:, None, None])
    )[:, None, None]
    flat_in = hidden_in.astype(jnp.float32).reshape(row_count, width)
    normed_one, factor_one = normalize(flat_in)
    attention_input = (normed_one * scale_one).astype(jnp.bfloat16)
    query_b = plain_dot(attention_input, query_full).astype(jnp.bfloat16)
    key_b = (
        plain_dot(attention_input, key_full)
        .astype(jnp.bfloat16)
        .reshape(seqs_here, tok_here, kv_local * HEAD_SIZE)
    )
    value_b = (
        plain_dot(attention_input, value_full)
        .astype(jnp.bfloat16)
        .reshape(seqs_here, tok_here, kv_local * HEAD_SIZE)
    )
    key_all, value_all = (
        lax.all_gather(key_b, "ctx", axis=1, tiled=True),
        lax.all_gather(value_b, "ctx", axis=1, tiled=True),
    )
    query_five = query_b.reshape(seqs_here, tok_here, kv_local, head_groups, HEAD_SIZE)
    key_four = key_all.reshape(seqs_here, SEQUENCE_SLOTS, kv_local, HEAD_SIZE)
    value_four = value_all.reshape(seqs_here, SEQUENCE_SLOTS, kv_local, HEAD_SIZE)
    raw = (
        jnp.einsum("stkgd,sukd->skgtu", query_five, key_four, preferred_element_type=jnp.float32)
        * QSCALE
    )
    bent = jnp.tanh(raw / CAP)
    masked = jnp.where(allowed, CAP * bent, NEG)
    largest = jnp.max(masked, -1, keepdims=True)
    logsum = largest + jnp.log(jnp.sum(jnp.exp(masked - largest), -1, keepdims=True))
    probs = jnp.exp(masked - logsum)
    probs_b = probs.astype(jnp.bfloat16)
    attended = (
        jnp.einsum("skgtu,sukd->stkgd", probs_b, value_four, preferred_element_type=jnp.float32)
        .astype(jnp.bfloat16)
        .reshape(row_count, -1)
    )
    attn = lax.psum(plain_dot(attended, out_full).astype(jnp.bfloat16), "tp").astype(jnp.float32)
    normed_two, factor_two = normalize(attn)
    after_attn = flat_in + normed_two * scale_two
    normed_three, factor_three = normalize(after_attn)
    ffn_in = (normed_three * scale_three).astype(jnp.bfloat16)
    gate = plain_dot(ffn_in, gate_full)
    upward = plain_dot(ffn_in, up_full)
    activated, gelu_pull = jax.vjp(gelu_tanh, gate)
    hidden_b = (activated * upward).astype(jnp.bfloat16)
    ffn_out = lax.psum(plain_dot(hidden_b, down_full).astype(jnp.bfloat16), "tp").astype(
        jnp.float32
    )
    normed_four, factor_four = normalize(ffn_out)
    result = after_attn + normed_four * scale_four
    cot = cotangent.astype(jnp.float32).reshape(row_count, width) * valid.reshape(
        row_count, 1
    ).astype(jnp.float32)
    query_back, key_back, value_back, out_back, gate_back, up_back, down_back = (
        lax.all_gather(query_weight, ("fsdp", "ctx"), axis=0, tiled=True),
        lax.all_gather(key_weight, ("fsdp", "ctx"), axis=0, tiled=True),
        lax.all_gather(value_weight, ("fsdp", "ctx"), axis=0, tiled=True),
        lax.all_gather(w_out, ("fsdp", "ctx"), axis=1, tiled=True),
        lax.all_gather(w_gate, ("fsdp", "ctx"), axis=0, tiled=True),
        lax.all_gather(w_up, ("fsdp", "ctx"), axis=0, tiled=True),
        lax.all_gather(w_down, ("fsdp", "ctx"), axis=1, tiled=True),
    )
    grad_gain_four = jnp.sum(cot * normed_four, 0)
    dffn_b = norm_back(cot * scale_four, normed_four, factor_four).astype(jnp.bfloat16)
    grad_down = left_dot(hidden_b, dffn_b)
    dhidden = right_dot(dffn_b, down_back)
    dgate_b = gelu_pull(dhidden * upward)[0].astype(jnp.bfloat16)
    dup_b = (dhidden * activated).astype(jnp.bfloat16)
    grad_gate = left_dot(ffn_in, dgate_b)
    grad_up = left_dot(ffn_in, dup_b)
    dffn_in = lax.psum(
        (right_dot(dgate_b, gate_back) + right_dot(dup_b, up_back)).astype(jnp.bfloat16), "tp"
    ).astype(jnp.float32)
    grad_gain_three = jnp.sum(dffn_in * normed_three, 0)
    dafter = cot + norm_back(dffn_in * scale_three, normed_three, factor_three)
    grad_gain_two = jnp.sum(dafter * normed_two, 0)
    dattn_b = norm_back(dafter * scale_two, normed_two, factor_two).astype(jnp.bfloat16)
    grad_out = left_dot(attended, dattn_b)
    dattended = right_dot(dattn_b, out_back).astype(jnp.bfloat16).reshape(query_five.shape)
    dprobs = jnp.einsum(
        "stkgd,sukd->skgtu", dattended, value_four, preferred_element_type=jnp.float32
    )
    weighted = jnp.sum(probs * dprobs, -1, keepdims=True)
    draw_b = (probs * (dprobs - weighted) * (1.0 - bent * bent)).astype(jnp.bfloat16)
    dquery_b = (
        (
            jnp.einsum("skgtu,sukd->stkgd", draw_b, key_four, preferred_element_type=jnp.float32)
            * QSCALE
        )
        .astype(jnp.bfloat16)
        .reshape(row_count, -1)
    )
    dvalue_part = jnp.einsum(
        "skgtu,stkgd->sukd", probs_b, dattended, preferred_element_type=jnp.float32
    )
    dkey_part = (
        jnp.einsum("skgtu,stkgd->sukd", draw_b, query_five, preferred_element_type=jnp.float32)
        * QSCALE
    )
    dkey, dvalue = (
        lax.psum_scatter(
            dkey_part.astype(jnp.bfloat16), "ctx", scatter_dimension=1, tiled=True
        ).astype(jnp.float32),
        lax.psum_scatter(
            dvalue_part.astype(jnp.bfloat16), "ctx", scatter_dimension=1, tiled=True
        ).astype(jnp.float32),
    )
    dkey_b = dkey.astype(jnp.bfloat16).reshape(row_count, -1)
    dvalue_b = dvalue.astype(jnp.bfloat16).reshape(row_count, -1)
    grad_query = left_dot(attention_input, dquery_b)
    grad_key = left_dot(attention_input, dkey_b)
    grad_value = left_dot(attention_input, dvalue_b)
    dattn_in = lax.psum(
        (
            right_dot(dquery_b, query_back)
            + right_dot(dkey_b, key_back)
            + right_dot(dvalue_b, value_back)
        ).astype(jnp.bfloat16),
        "tp",
    ).astype(jnp.float32)
    grad_gain_one = jnp.sum(dattn_in * normed_one, 0)
    grad_input = dafter + norm_back(dattn_in * scale_one, normed_one, factor_one)
    summed = (
        lax.psum_scatter(
            grad_query.astype(jnp.bfloat16), ("fsdp", "ctx"), scatter_dimension=0, tiled=True
        ).astype(jnp.float32),
        lax.psum_scatter(
            grad_key.astype(jnp.bfloat16), ("fsdp", "ctx"), scatter_dimension=0, tiled=True
        ).astype(jnp.float32),
        lax.psum_scatter(
            grad_value.astype(jnp.bfloat16), ("fsdp", "ctx"), scatter_dimension=0, tiled=True
        ).astype(jnp.float32),
        lax.psum_scatter(
            grad_out.astype(jnp.bfloat16), ("fsdp", "ctx"), scatter_dimension=1, tiled=True
        ).astype(jnp.float32),
        lax.psum_scatter(
            grad_gate.astype(jnp.bfloat16), ("fsdp", "ctx"), scatter_dimension=0, tiled=True
        ).astype(jnp.float32),
        lax.psum_scatter(
            grad_up.astype(jnp.bfloat16), ("fsdp", "ctx"), scatter_dimension=0, tiled=True
        ).astype(jnp.float32),
        lax.psum_scatter(
            grad_down.astype(jnp.bfloat16), ("fsdp", "ctx"), scatter_dimension=1, tiled=True
        ).astype(jnp.float32),
        lax.psum_scatter(
            grad_gain_one.astype(jnp.bfloat16), ("fsdp", "ctx"), scatter_dimension=0, tiled=True
        ).astype(jnp.float32),
        lax.psum_scatter(
            grad_gain_two.astype(jnp.bfloat16), ("fsdp", "ctx"), scatter_dimension=0, tiled=True
        ).astype(jnp.float32),
        lax.psum_scatter(
            grad_gain_three.astype(jnp.bfloat16), ("fsdp", "ctx"), scatter_dimension=0, tiled=True
        ).astype(jnp.float32),
        lax.psum_scatter(
            grad_gain_four.astype(jnp.bfloat16), ("fsdp", "ctx"), scatter_dimension=0, tiled=True
        ).astype(jnp.float32),
    )
    return (
        result.astype(jnp.bfloat16).reshape(hidden_in.shape),
        grad_input.astype(jnp.bfloat16).reshape(hidden_in.shape),
        summed[0],
        summed[1],
        summed[2],
        summed[3],
        summed[4],
        summed[5],
        summed[6],
        summed[7],
        summed[8],
        summed[9],
        summed[10],
    )


def solution(mesh):
    square = mesh.shape["ctx"] == 4 and mesh.shape["fsdp"] == 2
    return jax.shard_map(
        plane_body if square else general_body,
        mesh=mesh,
        in_specs=(
            P("fsdp", "ctx", None),
            P("fsdp"),
            P(("fsdp", "ctx"), "tp"),
            P(("fsdp", "ctx"), "tp"),
            P(("fsdp", "ctx"), "tp"),
            P("tp", ("fsdp", "ctx")),
            P(("fsdp", "ctx"), "tp"),
            P(("fsdp", "ctx"), "tp"),
            P("tp", ("fsdp", "ctx")),
            P(("fsdp", "ctx")),
            P(("fsdp", "ctx")),
            P(("fsdp", "ctx")),
            P(("fsdp", "ctx")),
            P("fsdp", "ctx", None),
        ),
        out_specs=(
            P("fsdp", "ctx", None),
            P("fsdp", "ctx", None),
            P(("fsdp", "ctx"), "tp"),
            P(("fsdp", "ctx"), "tp"),
            P(("fsdp", "ctx"), "tp"),
            P("tp", ("fsdp", "ctx")),
            P(("fsdp", "ctx"), "tp"),
            P(("fsdp", "ctx"), "tp"),
            P("tp", ("fsdp", "ctx")),
            P(("fsdp", "ctx")),
            P(("fsdp", "ctx")),
            P(("fsdp", "ctx")),
            P(("fsdp", "ctx")),
        ),
        check_vma=False,
    )
```
